512 devices in a mesh: prow: 32 (over x, z), pcol: 16 (over y, core).
Axes of the slice: x: 4, y: 8, z: 8, core: 2. Of those that a mesh axis runs over, the one named last changes fastest.
Arguments:
- inverse_block: float32 [4, 32, 128, 8, 16, 128], P(None, 'prow', None, None, 'pcol'), may hold values from -6 to 6
- panel_first: float32 [4, 32, 256, 128], P(None, 'prow', 'pcol'), may hold values from -0.046875 to 0.046875
- panel_second: float32 [4, 32, 256, 128], P(None, 'prow', 'pcol'), may hold values from -0.046875 to 0.046875
- coupling: float32 [256, 256], P('prow'), may hold values from -0.375 to 0.375
- dinv_first: float32 [256, 256], replicated, may hold values from -6 to 6
- dinv_second: float32 [256, 256], replicated, may hold values from -6 to 6
- struct_first: int32 [128], replicated, may hold values 0 or 1
- struct_second: int32 [128], replicated, may hold values 0 or 1
Outputs:
- row_first: float32 [8, 16, 256, 128], P(None, 'pcol', 'prow')
- own_first: float32 [256, 256], replicated
- row_second: float32 [8, 16, 256, 128], P(None, 'pcol', 'prow')
- cross: float32 [256, 256], replicated
- own_second: float32 [256, 256], replicated
The draws below stay inside these ranges and needn't reach their ends.
Inputs may be any that keep to these rules, and one draw needn't show every extreme that they name: `struct_first`: 1 marks a block that lies in the supernode's structure, 0 one that does not. `struct_second`: 1 marks a block that lies in the supernode's structure, 0 one that does not.
All inputs are finite; a program needn't handle non-finite values.
Results may differ from the reference program's by a relative error of at most 0.000084.
Values sent between devices are 32-bit elements; how exact they have to be, the bound alone decides.
A program may use at most 64 MiB of HBM per device.

```python
import jax
import jax.numpy as jnp
from jax import lax

B = 128
W = 256
RB = 4
NC = 128
CB = 8
N_PROW = 32
N_PCOL = 16


def set_ends(result, stream_key, low, top_value):
    dims = result.shape
    index_at = [jax.random.randint(jax.random.fold_in(stream_key, axis), (), 0, dims[axis]) for axis in range(len(dims))]
    result = result.at[tuple(index_at)].set(low)
    longest = dims.index(max(dims))
    index_at[longest] = (index_at[longest] + 1) % dims[longest]
    return result.at[tuple(index_at)].set(top_value)


def shard_levels(rng, shape, pieces, low, high):
    factor_of, own = 1.0, jax.random.fold_in(rng, 6)
    for position, shards_of in pieces:
        steps = jnp.exp(jax.random.uniform(jax.random.fold_in(own, position), (shards_of,), jnp.float32, low / len(pieces), high / len(pieces)))
        factor_of = factor_of * jnp.repeat(steps, shape[position] // shards_of).reshape([-1 if axis == position else 1 for axis in range(len(shape))])
    return factor_of


def normal_values(rng, dims, scale, reach, shards=(), kind=jnp.bfloat16):
    result = jax.random.normal(rng, dims, jnp.float32) * scale
    if len(shards) > 0:
        result = shard_levels(rng, dims, shards, -0.22, 0.18) * result
    return jnp.clip(result, min=-reach, max=reach).astype(kind)


def setup_inputs(seed: int = 0) -> dict:
    key_of = jax.random.split(jax.random.key(seed), 9)
    return {
        "inverse_block": normal_values(key_of[0], (RB, N_PROW, B, CB, N_PCOL, B), 1.0, 6.0, ((1, 32), (4, 16)), jnp.float32),
        "panel_first": normal_values(key_of[1], (RB, N_PROW, W, B), (NC * B) ** -0.5, 0.046875, ((1, 32), (2, 16)), jnp.float32),
        "panel_second": normal_values(key_of[2], (RB, N_PROW, W, B), (NC * B) ** -0.5, 0.046875, ((1, 32), (2, 16)), jnp.float32),
        "coupling": normal_values(key_of[3], (W, W), W ** -0.5, 0.375, ((0, 32),), jnp.float32),
        "dinv_first": normal_values(key_of[4], (W, W), 1.0, 6.0, (), jnp.float32),
        "dinv_second": normal_values(key_of[5], (W, W), 1.0, 6.0, (), jnp.float32),
        "struct_first": set_ends((jax.random.randint(key_of[6], (NC,), 0, 2) < 1).astype(jnp.int32), jax.random.fold_in(key_of[6], 1), 0, 1),
        "struct_second": set_ends((jax.random.randint(key_of[7], (NC,), 0, 2) < 1).astype(jnp.int32), jax.random.fold_in(key_of[7], 1), 0, 1),
    }


def reference(inverse_block, panel_first, panel_second, coupling, dinv_first, dinv_second, struct_first, struct_second):
    highest = lax.Precision.HIGHEST
    blocks = RB * N_PROW
    grid = inverse_block.reshape(blocks, B, blocks, B)
    upper_a = panel_first.reshape(blocks, W, B)
    upper_b = panel_second.reshape(blocks, W, B)
    mask_a = struct_first.astype(jnp.float32)[:, None, None]
    mask_b = struct_second.astype(jnp.float32)[:, None, None]
    row_a = -jnp.einsum("jwx,jxiy->iwy", upper_a * mask_a, grid, precision=highest) * mask_a
    own_a = dinv_first - jnp.einsum("iwy,ivy->wv", row_a, upper_a, precision=highest)
    carried = jnp.einsum("av,iay->ivy", coupling, row_a, precision=highest)
    row_b = -(jnp.einsum("jwx,jxiy->iwy", upper_b * mask_b, grid, precision=highest) + carried) * mask_b
    cross = -(jnp.einsum("jvy,jay->va", upper_b * mask_b, row_a, precision=highest)
              + jnp.einsum("av,aw->vw", coupling, own_a, precision=highest))
    own_b = (dinv_second - jnp.einsum("ivy,iuy->vu", row_b, upper_b, precision=highest)
             - jnp.dot(cross, coupling, precision=highest))
    columns = RB * N_PROW // N_PCOL
    return (row_a.reshape(columns, N_PCOL, W, B), own_a,
            row_b.reshape(columns, N_PCOL, W, B), cross, own_b)
```

```python
import jax
import jax.numpy as jnp
from jax import lax
from jax.experimental import pallas as pl
from jax.experimental.pallas import tpu as pltpu
from jax.sharding import PartitionSpec as P

NX, NZ, NY = 4, 8, 8
F32, BF16 = jnp.float32, jnp.bfloat16
MESH = pl.DeviceIdType.MESH

NN = (((1,), (0,)), ((), ()))
NT = (((1,), (1,)), ((), ()))


def split(v):
    hi = v.astype(BF16)
    return hi, (v - hi.astype(F32)).astype(BF16)


def dot3(a, b, dims=NN):
    def one(u, v):
        return lax.dot_general(u, v, dims, preferred_element_type=F32)

    return one(a[0], b[0]) + (one(a[0], b[1]) + one(a[1], b[0]))


def steps_of(way, half):
    return 4 if (way == 0) == (half == 0) else 3


def kernel(
    g_hbm, a_hbm, b_hbm, c_hbm, d1_hbm, d2_hbm, s1, s2,
    out_a, own_1, out_b, cross_out, own_2,
    g_raw, g_hi, g_lo, full, p_hi, p_lo, c_full, d1, d2,
    pa, pb, za, sb,
    xa_mid, xa_fin, xb_mid, xb_fin, za_in, zb_in,
    se, ex, pt, rr, tile, fin,
    load_sem, own_sem,
    ag_send, ag_recv, sib_send, sib_recv, c_send, c_recv,
    xa_send, xa_recv, xb_send, xb_recv, za_send, za_recv, zb_send, zb_recv,
    ex_send, ex_recv, rr_send, rr_recv, yz_send, yz_recv,
    fx_send, fx_recv, fs_send, fs_recv,
):
    p = lax.axis_index("prow")
    q = lax.axis_index("pcol")
    x, z = p // NZ, lax.rem(p, NZ)
    y, core = q // 2, lax.rem(q, 2)

    def at_x(k):
        return lax.rem(x + k, NX)

    def at_z(k):
        return lax.rem(z + k, NZ)

    def at_y(k):
        return lax.rem(y + k, NY)

    sibling = (p, y * 2 + 1 - core)

    def remote(src, dst, send, recv, where):
        return pltpu.make_async_remote_copy(
            src_ref=src, dst_ref=dst, send_sem=send, recv_sem=recv,
            device_id=where, device_id_type=MESH,
        )

    loads = [
        pltpu.make_async_copy(g_hbm, g_raw, load_sem.at[0]),
        pltpu.make_async_copy(d1_hbm, d1, load_sem.at[1]),
        pltpu.make_async_copy(d2_hbm, d2, load_sem.at[2]),
    ]
    rows16 = pl.ds(pl.multiple_of(q * 16, 16), 16)
    rows8 = pl.ds(pl.multiple_of(p * 8, 8), 8)
    own = [
        pltpu.make_async_copy(a_hbm, full.at[0, :, rows16], own_sem.at[0]),
        pltpu.make_async_copy(b_hbm, full.at[1, :, rows16], own_sem.at[1]),
        pltpu.make_async_copy(c_hbm, c_full.at[rows8], own_sem.at[2]),
    ]
    for copy in own + loads:
        copy.start()

    barrier = pltpu.get_barrier_semaphore()
    for where in ((p, at_y(1) * 2 + core), (p, at_y(NY - 1) * 2 + core), sibling):
        pl.semaphore_signal(barrier, inc=1, device_id=where, device_id_type=MESH)

    def greet(k, carry):
        pl.semaphore_signal(
            barrier, inc=1, device_id=(lax.rem(p + k, NX * NZ), q), device_id_type=MESH
        )
        return carry

    lax.fori_loop(1, NX * NZ, greet, 0)
    pl.semaphore_wait(barrier, NX * NZ - 1 + 3)

    for copy in own:
        copy.wait()

    ends = []

    def shard(k, rows):
        return full.at[k, :, pl.ds(pl.multiple_of(rows * 16, 16), 16)]

    def hops(k, way):
        return 4 if k == way else 3

    def ring_send(k, way, step):
        back = step - 1
        from_y = at_y(NY - back) if way == 0 else at_y(back)
        to_y = at_y(1) if way == 0 else at_y(NY - 1)
        ref = shard(k, from_y * 2 + core)
        copy = remote(
            ref, ref, ag_send.at[k, way, step - 1], ag_recv.at[k, way, step - 1],
            (p, to_y * 2 + core),
        )
        copy.start()
        ends.append(copy)
        return copy

    def across(k, index, row_y):
        ref = shard(k, row_y * 2 + core)
        copy = remote(ref, ref, sib_send.at[k, index], sib_recv.at[k, index], sibling)
        copy.start()
        ends.append(copy)
        return copy

    pending = {}
    crossing = {0: [], 1: []}
    for k in (0, 1):
        for way in (0, 1):
            pending[k, way] = ring_send(k, way, 1)
    for k in (0, 1):
        crossing[k].append(across(k, 0, y))

    def c_start(k, carry):
        remote(
            c_full.at[rows8], c_full.at[rows8], c_send.at[k], c_recv.at[k],
            (lax.rem(p + k, NX * NZ), q),
        ).start()
        return carry

    lax.fori_loop(1, NX * NZ, c_start, 0)

    loads[0].wait()

    def split_g(c, carry):
        hi, lo = split(g_raw[pl.ds(c, 512, stride=8), :])
        columns = pl.ds(pl.multiple_of(c * 128, 128), 128)
        g_hi[:, columns] = hi
        g_lo[:, columns] = lo
        return carry

    lax.fori_loop(0, 8, split_g, 0)

    for step in range(1, 5):
        for k in (0, 1):
            for way in (0, 1):
                if step > hops(k, way):
                    continue
                pending[k, way].wait_recv()
                if step < hops(k, way):
                    pending[k, way] = ring_send(k, way, step + 1)
                row_y = at_y(NY - step) if way == 0 else at_y(step)
                crossing[k].append(across(k, len(crossing[k]), row_y))

    def prepare(k, struct):
        for copy in crossing[k]:
            copy.wait_recv()
        for r in range(4):
            mask = struct[r * (NX * NZ) + p].astype(F32)
            hi, lo = split(full[k, r] * mask)
            p_hi[k, :, r * 128:(r + 1) * 128] = hi
            p_lo[k, :, r * 128:(r + 1) * 128] = lo

    def col_mask(struct, c):
        return struct[c * (NY * 2) + q].astype(F32)

    prepare(0, s1)

    def mul_a(t, carry):
        columns = pl.ds(pl.multiple_of(t * 256, 256), 256)
        r = dot3((p_hi[0], p_lo[0]), (g_hi[:, columns], g_lo[:, columns]))
        pa[:, :, :, columns] = r.reshape(NX, NZ, 8, 256)
        return carry

    lax.fori_loop(0, 4, mul_a, 0)

    def x_start(piece, mid, last, send, recv):
        right, left = (at_x(1) * NZ + z, q), (at_x(NX - 1) * NZ + z, q)
        copies = {
            "far0": remote(piece(at_x(2), 0), mid.at[0], send.at[0], recv.at[0], right),
            "far1": remote(piece(at_x(2), 1), mid.at[1], send.at[1], recv.at[1], left),
            "near1": remote(piece(at_x(1), 1), last.at[0, 1], send.at[2], recv.at[2], right),
            "near0": remote(piece(at_x(3), 0), last.at[1, 0], send.at[3], recv.at[3], left),
            "sum0": remote(piece(at_x(1), 0), last.at[0, 0], send.at[4], recv.at[4], right),
            "sum1": remote(piece(at_x(3), 1), last.at[1, 1], send.at[5], recv.at[5], left),
        }
        for name in ("far0", "far1", "near1", "near0"):
            copies[name].start()
        ends.extend(copies.values())
        return copies

    def x_middle(copies, add, mid):
        copies["far0"].wait_recv()
        add(at_x(1), 0, mid)
        copies["sum0"].start()
        copies["far1"].wait_recv()
        add(at_x(3), 1, mid)
        copies["sum1"].start()

    def x_wait(copies):
        for name in ("near1", "near0", "sum0", "sum1"):
            copies[name].wait_recv()

    def xa_piece(d, half):
        return pa.at[d, half * 4:(half + 1) * 4]

    def xa_add(d, half, mid):
        pa[d, half * 4:(half + 1) * 4] += mid[half]

    xa = x_start(xa_piece, xa_mid, xa_fin, xa_send, xa_recv)

    def c_wait(k, carry):
        remote(
            c_full.at[rows8], c_full.at[rows8], c_send.at[k], c_recv.at[k],
            (lax.rem(p + k, NX * NZ), q),
        ).wait()
        return carry

    lax.fori_loop(1, NX * NZ, c_wait, 0)
    coupling = c_full[...]
    c_parts = split(coupling)
    ct_parts = split(coupling.T)

    prepare(1, s2)

    def mul_b(t, carry):
        columns = pl.ds(pl.multiple_of(t * 256, 256), 256)
        r = dot3((p_hi[1], p_lo[1]), (g_hi[:, columns], g_lo[:, columns]))
        first = pa[:, :, :, columns].reshape(256, 256)
        lane = lax.broadcasted_iota(jnp.int32, (256, 256), 1)
        masks = jnp.where(lane < 128, col_mask(s1, 2 * t), col_mask(s1, 2 * t + 1))
        r = r - dot3(ct_parts, split(first * masks))
        pb[:, :, :, columns] = r.reshape(NX, NZ, 8, 256)
        return carry

    lax.fori_loop(0, 4, mul_b, 0)

    def z_copy(piece, into, send, recv, way, half, step):
        n = steps_of(way, half)
        away = n - step + 1
        d = at_z(away) if way == 0 else at_z(NZ - away)
        to_z = at_z(1) if way == 0 else at_z(NZ - 1)
        return remote(
            piece(d, half), into.at[way, half, step - 1],
            send.at[way, half, step - 1], recv.at[way, half, step - 1],
            (x * NZ + to_z, q),
        )

    def z_step(piece, add, into, send, recv, step):
        for half in (0, 1):
            for way in (0, 1):
                n = steps_of(way, half)
                if step > n:
                    continue
                copy = z_copy(piece, into, send, recv, way, half, step)
                if step > 1:
                    z_copy(piece, into, send, recv, way, half, step - 1).wait_recv()
                    away = n - step + 1
                    d = at_z(away) if way == 0 else at_z(NZ - away)
                    add(d, half, into.at[way, half, step - 2])
                copy.start()
                ends.append(copy)

    def z_wait(piece, into, send, recv):
        for half in (0, 1):
            for way in (0, 1):
                z_copy(piece, into, send, recv, way, half, steps_of(way, half)).wait_recv()

    def zb_piece(d, half):
        return pb.at[half * 2:(half + 1) * 2, d]

    def zb_add(d, half, ref):
        pb[half * 2:(half + 1) * 2, d] += ref[...]

    def za_piece(d, half):
        return za.at[d, :, half * 512:(half + 1) * 512]

    def za_add(d, half, ref):
        za[d, :, half * 512:(half + 1) * 512] += ref[...]

    zb = (zb_piece, zb_add, zb_in, zb_send, zb_recv)
    zz = (za_piece, za_add, za_in, za_send, za_recv)

    z_step(*zb, 1)
    x_middle(xa, xa_add, xa_mid)
    z_step(*zb, 2)
    z_step(*zb, 3)
    x_wait(xa)
    for half in (0, 1):
        rows = slice(half * 4, half * 4 + 4)
        za[rows] = pa[x, rows] + xa_fin[0, half] + xa_fin[1, half]
    z_step(*zz, 1)
    z_step(*zb, 4)
    z_step(*zz, 2)

    z_wait(zb_piece, zb_in, zb_send, zb_recv)
    for half in (0, 1):
        rows = slice(half * 2, half * 2 + 2)
        sb[rows] = (
            pb[rows, z]
            + zb_in[0, half, steps_of(0, half) - 1]
            + zb_in[1, half, steps_of(1, half) - 1]
        )

    def xb_piece(d, half):
        return sb.at[d, :, half * 512:(half + 1) * 512]

    def xb_add(d, half, mid):
        sb[d, :, half * 512:(half + 1) * 512] += mid[half]

    xb = x_start(xb_piece, xb_mid, xb_fin, xb_send, xb_recv)
    z_step(*zz, 3)
    x_middle(xb, xb_add, xb_mid)
    z_step(*zz, 4)

    def deliver(which, half, value, struct, out):
        for k in range(4):
            c = half * 4 + k
            block = value[:, k * 128:(k + 1) * 128] * (-col_mask(struct, c))
            out[c] = block
            r = c // 2
            se[c % 2, which, :, r * 128:(r + 1) * 128] = block

    to_col = 2 * z + 1 - lax.rem(x, 2)
    slot = x // 2

    def hand_over(which):
        for parity in (0, 1):
            copy = remote(
                se.at[parity, which], ex.at[slot, which],
                ex_send.at[parity, which], ex_recv.at[slot, which],
                (q + 16 * parity, to_col),
            )
            copy.start()
            ends.append(copy)

    def taken(which):
        for s in (0, 1):
            remote(
                se.at[0, which], ex.at[s, which], ex_send.at[0, which], ex_recv.at[s, which],
                sibling,
            ).wait_recv()

    z_wait(za_piece, za_in, za_send, za_recv)
    for half in (0, 1):
        value = (
            za[z, :, half * 512:(half + 1) * 512]
            + za_in[0, half, steps_of(0, half) - 1]
            + za_in[1, half, steps_of(1, half) - 1]
        )
        deliver(0, half, value, s1, out_a)
    hand_over(0)
    x_wait(xb)
    for half in (0, 1):
        value = sb[x, :, half * 512:(half + 1) * 512] + xb_fin[0, half] + xb_fin[1, half]
        deliver(1, half, value, s2, out_b)
    hand_over(1)

    taken(0)
    ra = split(ex[:, 0].reshape(16, 512))
    parts = [
        dot3(ra, (p_hi[0], p_lo[0]), NT),
        dot3(ra, (p_hi[1], p_lo[1]), NT),
    ]
    taken(1)
    rb = split(ex[:, 1].reshape(16, 512))
    parts.append(dot3(rb, (p_hi[1], p_lo[1]), NT))
    for m in range(3):
        for s in range(2):
            for h in range(2):
                pt[m, s * 2 + h] = parts[m][s * 8:(s + 1) * 8, h * 128:(h + 1) * 128]

    def at_sum(m, j):
        return j * NZ + lax.rem(y + 3 * m, NZ)

    def tile_copy(m, j):
        return remote(
            pt.at[m, j], rr.at[p], rr_send.at[m, j], rr_recv.at[p], (at_sum(m, j), q)
        )

    for m in range(3):
        for j in range(4):
            @pl.when(at_sum(m, j) != p)
            def _():
                tile_copy(m, j).start()

    turn = lax.rem(z - y + NZ, NZ)
    mine = turn // 3
    sums = lax.rem(turn, 3) == 0
    block = fin.at[core, x]

    @pl.when(sums)
    def _():
        rr[p] = pt[mine, x]

        def arrived(k, carry):
            src = lax.rem(p + k, NX * NZ)
            remote(
                pt.at[0, 0], rr.at[src], rr_send.at[0, 0], rr_recv.at[src], sibling
            ).wait_recv()
            return carry

        lax.fori_loop(1, NX * NZ, arrived, 0)
        tile[...] = jnp.sum(rr[...], axis=0)
        place = fin.at[core, x, mine, y]
        local = pltpu.make_async_copy(tile, place, yz_recv.at[0])
        local.start()

        def spread(k, carry):
            remote(
                tile, place, yz_send.at[k], yz_recv.at[0],
                (x * NZ + lax.rem(z + k // NY, NZ), lax.rem(y + lax.rem(k, NY), NY) * 2 + core),
            ).start()
            return carry

        lax.fori_loop(1, NY * NZ, spread, 0)

    pltpu.make_async_copy(block, block, yz_recv.at[0]).wait()

    right, left = (at_x(1) * NZ + z, q), (at_x(NX - 1) * NZ + z, q)

    def block_to(origin, where, index):
        ref = fin.at[core, origin]
        return remote(ref, ref, fx_send.at[index], fx_recv.at[index], where)

    def half_to(origin, half, where, index):
        ref = fin.at[core, origin, :, half * 4:(half + 1) * 4]
        return remote(ref, ref, fx_send.at[index], fx_recv.at[index], where)

    def block_across(origin, index):
        ref = fin.at[core, origin]
        copy = remote(ref, ref, fs_send.at[index], fs_recv.at[index], sibling)
        copy.start()
        ends.append(copy)
        return copy

    to_right, to_left = block_to(x, right, 0), block_to(x, left, 1)
    to_right.start()
    to_left.start()
    over = [block_across(x, 0)]
    to_right.wait_recv()
    on_right = half_to(at_x(3), 0, right, 2)
    on_right.start()
    over.append(block_across(at_x(3), 1))
    to_left.wait_recv()
    on_left = half_to(at_x(1), 1, left, 3)
    on_left.start()
    over.append(block_across(at_x(1), 2))
    on_right.wait_recv()
    on_left.wait_recv()
    over.append(block_across(at_x(2), 3))
    ends.extend((to_right, to_left, on_right, on_left))
    for copy in over:
        copy.wait_recv()

    loads[1].wait()
    loads[2].wait()
    cross_t = []
    for co in range(2):
        for xo in range(4):
            xs, h = (1 - co) + 2 * (xo // 2), xo % 2
            rows, columns = slice(xs * 64, xs * 64 + 64), slice(h * 128, h * 128 + 128)
            own_1[rows, columns] = d1[rows, columns] - fin[co, xo, 0].reshape(64, 128)
            cross_out[rows, columns] = fin[co, xo, 1].reshape(64, 128)
            d2[rows, columns] = d2[rows, columns] - fin[co, xo, 2].reshape(64, 128)
    cross = -(cross_out[...].T + dot3(ct_parts, split(own_1[...])))
    cross_out[...] = cross
    own_2[...] = d2[...] - dot3(split(cross), c_parts)

    for copy in ends:
        copy.wait_send()
    for m in range(3):
        for j in range(4):
            @pl.when(at_sum(m, j) != p)
            def _():
                tile_copy(m, j).wait_send()

    @pl.when(sums)
    def _():
        def spread_end(k, carry):
            remote(tile, tile, yz_send.at[k], yz_recv.at[0], sibling).wait_send()
            return carry

        lax.fori_loop(1, NY * NZ, spread_end, 0)


def body(
    inverse_block,
    panel_first,
    panel_second,
    coupling,
    dinv_first,
    dinv_second,
    struct_first,
    struct_second,
):
    dma = pltpu.SemaphoreType.DMA
    any_space = pl.BlockSpec(memory_space=pl.ANY)
    smem = pl.BlockSpec(memory_space=pltpu.SMEM)
    vmem = pl.BlockSpec(memory_space=pltpu.VMEM)
    square = jax.ShapeDtypeStruct((256, 256), F32)
    rows = jax.ShapeDtypeStruct((8, 8, 128), F32)
    row_a, own_a, row_b, cross, own_b = pl.pallas_call(
        kernel,
        out_shape=(rows, square, rows, square, square),
        in_specs=[any_space] * 6 + [smem] * 2,
        out_specs=(vmem,) * 5,
        scratch_shapes=[
            pltpu.VMEM((4096, 128), F32),
            pltpu.VMEM((512, 1024), BF16),
            pltpu.VMEM((512, 1024), BF16),
            pltpu.VMEM((2, 4, 256, 128), F32),
            pltpu.VMEM((2, 256, 512), BF16),
            pltpu.VMEM((2, 256, 512), BF16),
            pltpu.VMEM((256, 256), F32),
            pltpu.VMEM((256, 256), F32),
            pltpu.VMEM((256, 256), F32),
            pltpu.VMEM((4, 8, 8, 1024), F32),
            pltpu.VMEM((4, 8, 8, 1024), F32),
            pltpu.VMEM((8, 8, 1024), F32),
            pltpu.VMEM((4, 8, 1024), F32),
            pltpu.VMEM((2, 4, 8, 1024), F32),
            pltpu.VMEM((2, 2, 4, 8, 1024), F32),
            pltpu.VMEM((2, 8, 512), F32),
            pltpu.VMEM((2, 2, 8, 512), F32),
            pltpu.VMEM((2, 2, 4, 8, 512), F32),
            pltpu.VMEM((2, 2, 4, 2, 8, 1024), F32),
            pltpu.VMEM((2, 2, 8, 512), F32),
            pltpu.VMEM((2, 2, 8, 512), F32),
            pltpu.VMEM((3, 4, 8, 128), F32),
            pltpu.VMEM((32, 8, 128), F32),
            pltpu.VMEM((8, 128), F32),
            pltpu.VMEM((2, 4, 3, 8, 8, 128), F32),
            dma((3,)), dma((3,)),
            dma((2, 2, 4)), dma((2, 2, 4)), dma((2, 8)), dma((2, 8)), dma((32,)), dma((32,)),
            dma((6,)), dma((6,)), dma((6,)), dma((6,)),
            dma((2, 2, 4)), dma((2, 2, 4)), dma((2, 2, 4)), dma((2, 2, 4)),
            dma((2, 2)), dma((2, 2)), dma((3, 4)), dma((32,)), dma((64,)), dma((1,)),
            dma((4,)), dma((4,)), dma((4,)), dma((4,)),
        ],
        compiler_params=pltpu.CompilerParams(
            collective_id=0, has_side_effects=True, vmem_limit_bytes=40 * 1024 * 1024
        ),
        name="selected_inversion",
    )(
        inverse_block.reshape(4096, 128),
        panel_first.reshape(4, 16, 128),
        panel_second.reshape(4, 16, 128),
        coupling, dinv_first, dinv_second, struct_first, struct_second,
    )
    return (
        row_a.reshape(8, 1, 8, 128), own_a, row_b.reshape(8, 1, 8, 128), cross, own_b,
    )


def solution(mesh):
    return jax.shard_map(
        body,
        mesh=mesh,
        in_specs=(
            P(None, "prow", None, None, "pcol", None),
            P(None, "prow", "pcol", None),
            P(None, "prow", "pcol", None),
            P("prow", None),
            P(),
            P(),
            P(),
            P(),
        ),
        out_specs=(P(None, "pcol", "prow", None), P(), P(None, "pcol", "prow", None), P(), P()),
        check_vma=False,
    )
```

```python
import jax
import jax.numpy as jnp
from jax import lax
from jax.experimental import pallas as pl
from jax.experimental.pallas import tpu as pltpu
from jax.sharding import PartitionSpec as P

NX, NZ, NY = 4, 8, 8
F32, BF16 = jnp.float32, jnp.bfloat16
MESH = pl.DeviceIdType.MESH

NN = (((1,), (0,)), ((), ()))
NT = (((1,), (1,)), ((), ()))


def split(v):
    hi = v.astype(BF16)
    return hi, (v - hi.astype(F32)).astype(BF16)


def dot3(a, b, dims=NN):
    def one(u, v):
        return lax.dot_general(u, v, dims, preferred_element_type=F32)

    return one(a[0], b[0]) + (one(a[0], b[1]) + one(a[1], b[0]))


def steps_of(way, half):
    return 4 if (way == 0) == (half == 0) else 3


def kernel(
    g_hbm, a_hbm, b_hbm, c_hbm, d1_hbm, d2_hbm, s1_hbm, s2_hbm,
    out_a, own_1, out_b, cross_out, own_2,
    s1, s2, g_raw, g_hi, g_lo, full, p_hi, p_lo, c_full, d1, d2,
    pa, pb, za, sb,
    xa_mid, xa_fin, xb_in, za_in, zb_in,
    rows_1, rows_2, ex_a, ex_b, pt, rr, tile, fin, all_sent,
    load_sem, own_sem,
    ag_send, ag_recv, sib_send, sib_recv, cz_send, cz_recv, cx_send, cx_recv,
    xa_send, xa_recv, xb_send, xb_recv, za_send, za_recv, zb_send, zb_recv,
    exa_send, exa_recv, exb_send, exb_recv, rr_send, rr_recv, yz_send, yz_recv,
    fx_send, fx_recv, fs_send, fs_recv,
):
    p = lax.axis_index("prow")
    q = lax.axis_index("pcol")
    x, z = p // NZ, lax.rem(p, NZ)
    y, core = q // 2, lax.rem(q, 2)

    def at_x(k):
        return lax.rem(x + k + NX, NX)

    def at_z(k):
        return lax.rem(z + k + NZ, NZ)

    def at_y(k):
        return lax.rem(y + k + NY, NY)

    sibling = (p, y * 2 + 1 - core)

    def remote(src, dst, send, recv, where):
        return pltpu.make_async_remote_copy(
            src_ref=src, dst_ref=dst, send_sem=send, recv_sem=recv,
            device_id=where, device_id_type=MESH,
        )

    rows16 = pl.ds(pl.multiple_of(q * 16, 16), 16)
    rows8 = pl.ds(pl.multiple_of(p * 8, 8), 8)
    own = [
        pltpu.make_async_copy(a_hbm, full.at[0, :, rows16], own_sem.at[0]),
        pltpu.make_async_copy(b_hbm, full.at[1, :, rows16], own_sem.at[1]),
        pltpu.make_async_copy(c_hbm, c_full.at[rows8], own_sem.at[2]),
    ]
    loads = [
        pltpu.make_async_copy(g_hbm, g_raw, load_sem.at[0]),
        pltpu.make_async_copy(d1_hbm, d1, load_sem.at[1]),
        pltpu.make_async_copy(d2_hbm, d2, load_sem.at[2]),
        pltpu.make_async_copy(s1_hbm, s1, load_sem.at[3]),
        pltpu.make_async_copy(s2_hbm, s2, load_sem.at[4]),
    ]
    for copy in own + loads:
        copy.start()

    barrier = pltpu.get_barrier_semaphore()
    near = [(p, at_y(k) * 2 + core) for k in (1, -1, 2, -2)] + [sibling]
    near += [(x * NZ + at_z(k), q) for k in range(1, NZ)]
    near += [(at_x(k) * NZ + z, q) for k in range(1, NX)]
    for where in near:
        pl.semaphore_signal(barrier, inc=1, device_id=where, device_id_type=MESH)
    pl.semaphore_wait(barrier, len(near))

    for copy in own:
        copy.wait()

    ends = []

    def shard(k, row_y):
        rows = row_y * 2 + core
        return full.at[k, :, pl.ds(pl.multiple_of(rows * 16, 16), 16)]

    def ring(k, of, to):
        ref = shard(k, at_y(of))
        return remote(
            ref, ref, ag_send.at[k, of - to + 4], ag_recv.at[k, of - to + 4],
            (p, at_y(to) * 2 + core),
        )

    def push(k, of, to):
        copy = ring(k, of, to)
        copy.start()
        ends.append(copy)

    crossing = {0: [], 1: []}

    def across(k, of):
        ref = shard(k, at_y(of))
        copy = remote(ref, ref, sib_send.at[k, of + 4], sib_recv.at[k, of + 4], sibling)
        copy.start()
        ends.append(copy)
        crossing[k].append(copy)

    def got(k, of):
        ring(k, of, 0).wait_recv()
        across(k, of)

    for k in (0, 1):
        for to in (2, -2, 1, -1):
            push(k, 0, to)
        across(k, 0)

    def cz_copy(k):
        return remote(
            c_full.at[rows8], c_full.at[rows8], cz_send.at[k], cz_recv.at[k],
            (x * NZ + at_z(k), q),
        )

    for k in range(1, NZ):
        cz_copy(k).start()

    for index in (0, 3, 4):
        loads[index].wait()

    def split_g(c, carry):
        hi, lo = split(g_raw[pl.ds(c, 512, stride=8), :])
        columns = pl.ds(pl.multiple_of(c * 128, 128), 128)
        g_hi[:, columns] = hi
        g_lo[:, columns] = lo
        return carry

    lax.fori_loop(0, 8, split_g, 0)

    for k in (0, 1):
        for of in (-2, 2):
            got(k, of)
            way = 1 if of < 0 else -1
            push(k, of, way)
            if (of < 0) == (k == 0):
                push(k, of, 2 * way)
        got(k, -1)
        got(k, 1)

    for k in range(1, NZ):
        cz_copy(k).wait_recv()
    rows64 = pl.ds(pl.multiple_of(x * 64, 64), 64)

    def cx_copy(k):
        return remote(
            c_full.at[rows64], c_full.at[rows64], cx_send.at[k], cx_recv.at[k],
            (at_x(k) * NZ + z, q),
        )

    for k in range(1, NX):
        cx_copy(k).start()

    def prepare(k, struct):
        for of in (-3, 3, -4 if k == 0 else 4):
            got(k, of)
        for copy in crossing[k]:
            copy.wait_recv()
        for r in range(4):
            mask = struct[r * (NX * NZ) + p].astype(F32)
            hi, lo = split(full[k, r] * mask)
            p_hi[k, :, r * 128:(r + 1) * 128] = hi
            p_lo[k, :, r * 128:(r + 1) * 128] = lo

    def col_mask(struct, c):
        return struct[c * (NY * 2) + q].astype(F32)

    prepare(0, s1)

    def mul_a(t, carry):
        columns = pl.ds(pl.multiple_of(t * 256, 256), 256)
        r = dot3((p_hi[0], p_lo[0]), (g_hi[:, columns], g_lo[:, columns]))
        pa[:, :, t, 0] = r[:, :128].reshape(NX, NZ, 8, 128)
        pa[:, :, t, 1] = r[:, 128:].reshape(NX, NZ, 8, 128)
        return carry

    lax.fori_loop(0, 4, mul_a, 0)

    x_right, x_left = (at_x(1) * NZ + z, q), (at_x(-1) * NZ + z, q)

    def xa_piece(d, half):
        return pa.at[d, half * 4:(half + 1) * 4]

    def xa_copy(index, d, half, into, where):
        return remote(xa_piece(d, half), into, xa_send.at[index], xa_recv.at[index], where)

    xa = {
        "far0": xa_copy(0, at_x(2), 0, xa_mid.at[0], x_right),
        "far1": xa_copy(1, at_x(2), 1, xa_mid.at[1], x_left),
        "near1": xa_copy(2, at_x(1), 1, xa_fin.at[0, 1], x_right),
        "near0": xa_copy(3, at_x(3), 0, xa_fin.at[1, 0], x_left),
        "sum0": xa_copy(4, at_x(1), 0, xa_fin.at[0, 0], x_right),
        "sum1": xa_copy(5, at_x(3), 1, xa_fin.at[1, 1], x_left),
    }
    for name in ("far0", "far1", "near1", "near0"):
        xa[name].start()
    ends.extend(xa.values())

    for k in range(1, NX):
        cx_copy(k).wait_recv()
    coupling = c_full[...]
    c_parts = split(coupling)
    ct_parts = split(coupling.T)

    prepare(1, s2)

    def mul_b(t, carry):
        columns = pl.ds(pl.multiple_of(t * 256, 256), 256)
        r = dot3((p_hi[1], p_lo[1]), (g_hi[:, columns], g_lo[:, columns]))
        first = jnp.concatenate(
            [pa[:, :, t, h].reshape(256, 128) * col_mask(s1, 2 * t + h) for h in (0, 1)], axis=1
        )
        r = r - dot3(ct_parts, split(first))
        pb[:, :, t, 0] = r[:, :128].reshape(NX, NZ, 8, 128)
        pb[:, :, t, 1] = r[:, 128:].reshape(NX, NZ, 8, 128)
        return carry

    lax.fori_loop(0, 4, mul_b, 0)

    def zb_copy(way, half, step):
        away = steps_of(way, half) - step + 1
        d = at_z(away) if way == 0 else at_z(-away)
        to_z = at_z(1) if way == 0 else at_z(-1)
        return d, remote(
            pb.at[half * 2:(half + 1) * 2, d], zb_in.at[way, half, step - 1],
            zb_send.at[way, half, step - 1], zb_recv.at[way, half, step - 1],
            (x * NZ + to_z, q),
        )

    def zb_step(step):
        for half in (0, 1):
            for way in (0, 1):
                if step > steps_of(way, half):
                    continue
                d, copy = zb_copy(way, half, step)
                if step > 1:
                    zb_copy(way, half, step - 1)[1].wait_recv()
                    pb[half * 2:(half + 1) * 2, d] += zb_in[way, half, step - 2]
                copy.start()
                ends.append(copy)

    zb_step(1)
    xa["far0"].wait_recv()
    pa[at_x(1), 0:4] += xa_mid[0]
    xa["sum0"].start()
    xa["far1"].wait_recv()
    pa[at_x(3), 4:8] += xa_mid[1]
    xa["sum1"].start()
    zb_step(2)
    zb_step(3)
    for name in ("near1", "near0", "sum0", "sum1"):
        xa[name].wait_recv()
    for half in (0, 1):
        rows = slice(half * 4, half * 4 + 4)
        za[rows] = pa[x, rows] + xa_fin[0, half] + xa_fin[1, half]

    def xb_copy(k):
        return remote(
            sb.at[at_x(k)], xb_in.at[k], xb_send.at[k], xb_recv.at[k], (at_x(k) * NZ + z, q)
        )

    def za_copy(k):
        return remote(
            za.at[at_z(k)], za_in.at[k], za_send.at[k], za_recv.at[k], (x * NZ + at_z(k), q)
        )

    to_col = 2 * z + 1 - lax.rem(x, 2)

    def hand_over(rows, into, parity, send, recv):
        return remote(
            rows.at[parity], into.at[x // 2], send.at[parity], recv.at[0],
            (q + 16 * parity, to_col),
        )

    for k in (4, 3, 5, 2, 6, 1, 7):
        za_copy(k).start()
    zb_step(4)
    for half in (0, 1):
        last = [steps_of(way, half) for way in (0, 1)]
        for way in (0, 1):
            zb_copy(way, half, last[way])[1].wait_recv()
        rows = slice(half * 2, half * 2 + 2)
        sb[rows] = pb[rows, z] + zb_in[0, half, last[0] - 1] + zb_in[1, half, last[1] - 1]
    for k in (2, 1, 3):
        xb_copy(k).start()

    for k in range(1, NZ):
        za_copy(k).wait_recv()
    value = za[z]
    for k in range(1, NZ):
        value = value + za_in[k]
    for c in range(8):
        block = value[c // 2, c % 2] * (-col_mask(s1, c))
        out_a[c] = block
        rows_1[c % 2, c // 2] = block
    for parity in (0, 1):
        hand_over(rows_1, ex_a, parity, exa_send, exa_recv).start()
    for k in range(1, NX):
        xb_copy(k).wait_recv()
    value = sb[x] + xb_in[1] + xb_in[2] + xb_in[3]
    for c in range(8):
        block = value[c // 2, c % 2] * (-col_mask(s2, c))
        out_b[c] = block
        rows_2[c % 2, c // 2] = block
    for parity in (0, 1):
        hand_over(rows_2, ex_b, parity, exb_send, exb_recv).start()

    def at_sum(m, j):
        return j * NZ + lax.rem(y + 3 * m, NZ)

    def tile_copy(m, j):
        return remote(
            pt.at[m, j], rr.at[p], rr_send.at[m, j], rr_recv.at[0], (at_sum(m, j), q)
        )

    def panel_rows(ref):
        return split(jnp.concatenate([ref[:, r].reshape(16, 128) for r in range(4)], axis=1))

    def send_tiles(m, value):
        for s in range(2):
            for h in range(2):
                pt[m, s * 2 + h] = value[s * 8:(s + 1) * 8, h * 128:(h + 1) * 128]
        for j in range(4):
            @pl.when(at_sum(m, j) != p)
            def _():
                tile_copy(m, j).start()

            @pl.when(at_sum(m, j) == p)
            def _():
                pltpu.make_async_copy(pt.at[m, j], rr.at[p], rr_recv.at[0]).start()

    pltpu.make_async_copy(ex_a, ex_a, exa_recv.at[0]).wait()
    rows_a = panel_rows(ex_a)
    send_tiles(0, dot3(rows_a, (p_hi[0], p_lo[0]), NT))
    send_tiles(1, dot3(rows_a, (p_hi[1], p_lo[1]), NT))
    pltpu.make_async_copy(ex_b, ex_b, exb_recv.at[0]).wait()
    rows_b = panel_rows(ex_b)
    send_tiles(2, dot3(rows_b, (p_hi[1], p_lo[1]), NT))

    turn = lax.rem(z - y + NZ, NZ)
    mine = turn // 3

    def make_sums(which):
        @pl.when(which)
        def _():
            pltpu.make_async_copy(rr, rr, rr_recv.at[0]).wait()
            tile[...] = jnp.sum(rr[...], axis=0)
            place = fin.at[core, x, mine, y]
            spot = yz_recv.at[mine // 2]
            pltpu.make_async_copy(tile, place, spot).start()

            def spread(k, carry):
                remote(
                    tile, place, yz_send.at[0], spot,
                    (x * NZ + at_z(k // NY), at_y(lax.rem(k, NY)) * 2 + core),
                ).start()
                return carry

            lax.fori_loop(1, NY * NZ, spread, 0)

    make_sums(jnp.logical_or(turn == 0, turn == 3))
    make_sums(turn == 6)

    def part(origin, which):
        return fin.at[core, origin, 0:2] if which == 0 else fin.at[core, origin, 2:3]

    def fx_copy(which, k):
        return remote(
            part(x, which), part(x, which), fx_send.at[which, k], fx_recv.at[which, k],
            (at_x(k) * NZ + z, q),
        )

    def fs_copy(which, k):
        ref = part(at_x(-k), which)
        return remote(ref, ref, fs_send.at[which, k], fs_recv.at[which, k], sibling)

    for which in (0, 1):
        block = part(x, which)
        pltpu.make_async_copy(block, block, yz_recv.at[which]).wait()
        for k in (2, 1, 3):
            fx_copy(which, k).start()
        fs_copy(which, 0).start()
    for which in (0, 1):
        for k in (1, 3, 2):
            fx_copy(which, k).wait_recv()
            fs_copy(which, k).start()

    loads[1].wait()
    loads[2].wait()
    for k in range(4):
        fs_copy(0, k).wait_recv()

    def places():
        for co in range(2):
            for xo in range(4):
                xs, h = (1 - co) + 2 * (xo // 2), xo % 2
                yield (
                    slice(xs * 64, xs * 64 + 64), slice(h * 128, h * 128 + 128),
                    fin.at[co, xo],
                )

    for rows, columns, ref in places():
        own_1[rows, columns] = d1[rows, columns] - ref[0].reshape(64, 128)
        cross_out[rows, columns] = ref[1].reshape(64, 128)
    cross = -(cross_out[...].T + dot3(ct_parts, split(own_1[...])))
    cross_out[...] = cross
    last = d2[...] - dot3(split(cross), c_parts)
    for k in range(4):
        fs_copy(1, k).wait_recv()
    for rows, columns, ref in places():
        own_2[rows, columns] = last[rows, columns] - ref[2].reshape(64, 128)

    for copy in ends:
        copy.wait_send()
    for k in range(1, NZ):
        cz_copy(k).wait_send()
        za_copy(k).wait_send()
    for k in range(1, NX):
        cx_copy(k).wait_send()
        xb_copy(k).wait_send()
        for which in (0, 1):
            fx_copy(which, k).wait_send()
    for k in range(4):
        for which in (0, 1):
            fs_copy(which, k).wait_send()
    for parity in (0, 1):
        hand_over(rows_1, ex_a, parity, exa_send, exa_recv).wait_send()
        hand_over(rows_2, ex_b, parity, exb_send, exb_recv).wait_send()
    for m in range(3):
        for j in range(4):
            @pl.when(at_sum(m, j) != p)
            def _():
                tile_copy(m, j).wait_send()

    @pl.when(lax.rem(turn, 3) == 0)
    def _():
        pltpu.make_async_copy(all_sent, all_sent, yz_send.at[0]).wait()


def body(
    inverse_block,
    panel_first,
    panel_second,
    coupling,
    dinv_first,
    dinv_second,
    struct_first,
    struct_second,
):
    dma = pltpu.SemaphoreType.DMA
    any_space = pl.BlockSpec(memory_space=pl.ANY)
    vmem = pl.BlockSpec(memory_space=pltpu.VMEM)
    square = jax.ShapeDtypeStruct((256, 256), F32)
    rows = jax.ShapeDtypeStruct((8, 8, 128), F32)
    row_a, own_a, row_b, cross, own_b = pl.pallas_call(
        kernel,
        out_shape=(rows, square, rows, square, square),
        in_specs=[any_space] * 8,
        out_specs=(vmem,) * 5,
        scratch_shapes=[
            pltpu.SMEM((128,), jnp.int32),
            pltpu.SMEM((128,), jnp.int32),
            pltpu.VMEM((4096, 128), F32),
            pltpu.VMEM((512, 1024), BF16),
            pltpu.VMEM((512, 1024), BF16),
            pltpu.VMEM((2, 4, 256, 128), F32),
            pltpu.VMEM((2, 256, 512), BF16),
            pltpu.VMEM((2, 256, 512), BF16),
            pltpu.VMEM((256, 256), F32),
            pltpu.VMEM((256, 256), F32),
            pltpu.VMEM((256, 256), F32),
            pltpu.VMEM((4, 8, 4, 2, 8, 128), F32),
            pltpu.VMEM((4, 8, 4, 2, 8, 128), F32),
            pltpu.VMEM((8, 4, 2, 8, 128), F32),
            pltpu.VMEM((4, 4, 2, 8, 128), F32),
            pltpu.VMEM((2, 4, 4, 2, 8, 128), F32),
            pltpu.VMEM((2, 2, 4, 4, 2, 8, 128), F32),
            pltpu.VMEM((4, 4, 2, 8, 128), F32),
            pltpu.VMEM((8, 4, 2, 8, 128), F32),
            pltpu.VMEM((2, 2, 4, 2, 4, 2, 8, 128), F32),
            pltpu.VMEM((2, 4, 8, 128), F32),
            pltpu.VMEM((2, 4, 8, 128), F32),
            pltpu.VMEM((2, 4, 8, 128), F32),
            pltpu.VMEM((2, 4, 8, 128), F32),
            pltpu.VMEM((3, 4, 8, 128), F32),
            pltpu.VMEM((32, 8, 128), F32),
            pltpu.VMEM((8, 128), F32),
            pltpu.VMEM((2, 4, 3, 8, 8, 128), F32),
            pltpu.VMEM((63, 8, 128), F32),
            dma((5,)), dma((3,)),
            dma((2, 9)), dma((2, 9)), dma((2, 9)), dma((2, 9)),
            dma((8,)), dma((8,)), dma((4,)), dma((4,)),
            dma((6,)), dma((6,)), dma((4,)), dma((4,)),
            dma((8,)), dma((8,)), dma((2, 2, 4)), dma((2, 2, 4)),
            dma((2,)), dma((1,)), dma((2,)), dma((1,)),
            dma((3, 4)), dma((1,)), dma((1,)), dma((2,)),
            dma((2, 4)), dma((2, 4)), dma((2, 4)), dma((2, 4)),
        ],
        compiler_params=pltpu.CompilerParams(
            collective_id=0, has_side_effects=True, vmem_limit_bytes=60 * 1024 * 1024
        ),
        name="selected_inversion",
    )(
        inverse_block.reshape(4096, 128),
        panel_first.reshape(4, 16, 128),
        panel_second.reshape(4, 16, 128),
        coupling, dinv_first, dinv_second, struct_first, struct_second,
    )
    return (
        row_a.reshape(8, 1, 8, 128), own_a, row_b.reshape(8, 1, 8, 128), cross, own_b,
    )


def solution(mesh):
    return jax.shard_map(
        body,
        mesh=mesh,
        in_specs=(
            P(None, "prow", None, None, "pcol", None),
            P(None, "prow", "pcol", None),
            P(None, "prow", "pcol", None),
            P("prow", None),
            P(),
            P(),
            P(),
            P(),
        ),
        out_specs=(P(None, "pcol", "prow", None), P(), P(None, "pcol", "prow", None), P(), P()),
        check_vma=False,
    )
```

```python
import jax
import jax.numpy as jnp
from jax import lax
from jax.experimental import pallas as pl
from jax.experimental.pallas import tpu as pltpu
from jax.sharding import PartitionSpec as P

NX, NZ, NY = 4, 8, 8
F32, BF16 = jnp.float32, jnp.bfloat16
MESH = pl.DeviceIdType.MESH

NN = (((1,), (0,)), ((), ()))
NT = (((1,), (1,)), ((), ()))


def split(v):
    hi = v.astype(BF16)
    return hi, (v - hi.astype(F32)).astype(BF16)


def dot3(a, b, dims=NN):
    def one(u, v):
        return lax.dot_general(u, v, dims, preferred_element_type=F32)

    return one(a[0], b[0]) + (one(a[0], b[1]) + one(a[1], b[0]))


def steps_of(way, half):
    return 4 if (way == 0) == (half == 0) else 3


def kernel(
    g_hbm, a_hbm, b_hbm, c_hbm, d1_hbm, d2_hbm, s1_hbm, s2_hbm,
    out_a, own_1, out_b, cross_out, own_2,
    s1, s2, g_raw, g_hi, g_lo, full, p_hi, p_lo, c_full, d1, d2,
    pa, pb, za, sb,
    xa_mid, xa_fin, xb_in, za_in, zb_in,
    rows_1, rows_2, ex_a, ex_b, pt, rr, tile, fin, all_sent,
    load_sem, own_sem,
    ag_send, ag_recv, sib_send, sib_recv, cz_send, cz_recv, cx_send, cx_recv,
    xa_send, xa_recv, xb_send, xb_recv, za_send, za_recv, zb_send, zb_recv,
    exa_send, exa_recv, exb_send, exb_recv, rr_send, rr_recv, yz_send, yz_recv,
    fx_send, fx_recv, fs_send, fs_recv,
):
    p = lax.axis_index("prow")
    q = lax.axis_index("pcol")
    x, z = p // NZ, lax.rem(p, NZ)
    y, core = q // 2, lax.rem(q, 2)

    def at_x(k):
        return lax.rem(x + k + NX, NX)

    def at_z(k):
        return lax.rem(z + k + NZ, NZ)

    def at_y(k):
        return lax.rem(y + k + NY, NY)

    sibling = (p, y * 2 + 1 - core)

    def remote(src, dst, send, recv, where):
        return pltpu.make_async_remote_copy(
            src_ref=src, dst_ref=dst, send_sem=send, recv_sem=recv,
            device_id=where, device_id_type=MESH,
        )

    barrier = pltpu.get_barrier_semaphore()
    near = [(p, at_y(k) * 2 + core) for k in (1, -1, 2, -2)] + [sibling]
    near += [(x * NZ + at_z(k), q) for k in range(1, NZ)]
    near += [(at_x(k) * NZ + z, q) for k in range(1, NX)]
    for where in near:
        pl.semaphore_signal(barrier, inc=1, device_id=where, device_id_type=MESH)

    rows16 = pl.ds(pl.multiple_of(q * 16, 16), 16)
    rows8 = pl.ds(pl.multiple_of(p * 8, 8), 8)
    own = [
        pltpu.make_async_copy(a_hbm, full.at[0, :, rows16], own_sem.at[0]),
        pltpu.make_async_copy(b_hbm, full.at[1, :, rows16], own_sem.at[1]),
        pltpu.make_async_copy(c_hbm, c_full.at[rows8], own_sem.at[2]),
    ]
    loads = [
        pltpu.make_async_copy(g_hbm, g_raw, load_sem.at[0]),
        pltpu.make_async_copy(d1_hbm, d1, load_sem.at[1]),
        pltpu.make_async_copy(d2_hbm, d2, load_sem.at[2]),
        pltpu.make_async_copy(s1_hbm, s1, load_sem.at[3]),
        pltpu.make_async_copy(s2_hbm, s2, load_sem.at[4]),
    ]
    for copy in own + loads:
        copy.start()

    pl.semaphore_wait(barrier, len(near))

    ends = []

    def shard(k, row_y):
        rows = row_y * 2 + core
        return full.at[k, :, pl.ds(pl.multiple_of(rows * 16, 16), 16)]

    def ring(k, of, to):
        ref = shard(k, at_y(of))
        return remote(
            ref, ref, ag_send.at[k, of - to + 4], ag_recv.at[k, of - to + 4],
            (p, at_y(to) * 2 + core),
        )

    def push(k, of, to):
        copy = ring(k, of, to)
        copy.start()
        ends.append(copy)

    crossing = {0: [], 1: []}

    def across(k, of):
        ref = shard(k, at_y(of))
        copy = remote(ref, ref, sib_send.at[k, of + 4], sib_recv.at[k, of + 4], sibling)
        copy.start()
        ends.append(copy)
        crossing[k].append(copy)

    def got(k, of):
        ring(k, of, 0).wait_recv()
        across(k, of)

    own[0].wait()
    for to in (2, -2, 1, -1):
        push(0, 0, to)
    across(0, 0)
    own[1].wait()
    for to in (2, -2):
        push(1, 0, to)
    own[2].wait()

    def cz_copy(k):
        return remote(
            c_full.at[rows8], c_full.at[rows8], cz_send.at[k], cz_recv.at[k],
            (x * NZ + at_z(k), q),
        )

    for k in range(1, NZ):
        cz_copy(k).start()

    for index in (0, 3, 4):
        loads[index].wait()

    def split_g(c, carry):
        hi, lo = split(g_raw[pl.ds(c, 512, stride=8), :])
        columns = pl.ds(pl.multiple_of(c * 128, 128), 128)
        g_hi[:, columns] = hi
        g_lo[:, columns] = lo
        return carry

    lax.fori_loop(0, 8, split_g, 0)

    def forward(k, of):
        ring(k, of, 0).wait_recv()
        way = 1 if of < 0 else -1
        push(k, of, way)
        if (of < 0) == (k == 0):
            push(k, of, 2 * way)
        across(k, of)

    forward(0, -2)
    forward(0, 2)
    for to in (1, -1):
        push(1, 0, to)
    across(1, 0)
    got(0, -1)
    got(0, 1)
    for k in range(1, NZ):
        cz_copy(k).wait_recv()
    rows64 = pl.ds(pl.multiple_of(x * 64, 64), 64)

    def cx_copy(k):
        return remote(
            c_full.at[rows64], c_full.at[rows64], cx_send.at[k], cx_recv.at[k],
            (at_x(k) * NZ + z, q),
        )

    for k in range(1, NX):
        cx_copy(k).start()
    got(0, -3)
    got(0, 3)
    forward(1, -2)
    forward(1, 2)
    got(0, -4)

    def prepare(k, struct):
        for copy in crossing[k]:
            copy.wait_recv()
        for r in range(4):
            mask = struct[r * (NX * NZ) + p].astype(F32)
            hi, lo = split(full[k, r] * mask)
            p_hi[k, :, r * 128:(r + 1) * 128] = hi
            p_lo[k, :, r * 128:(r + 1) * 128] = lo

    def col_mask(struct, c):
        return struct[c * (NY * 2) + q].astype(F32)

    prepare(0, s1)

    def mul_a(t, carry):
        columns = pl.ds(pl.multiple_of(t * 256, 256), 256)
        r = dot3((p_hi[0], p_lo[0]), (g_hi[:, columns], g_lo[:, columns]))
        pa[:, :, t, 0] = r[:, :128].reshape(NX, NZ, 8, 128)
        pa[:, :, t, 1] = r[:, 128:].reshape(NX, NZ, 8, 128)
        return carry

    lax.fori_loop(0, 4, mul_a, 0)

    x_right, x_left = (at_x(1) * NZ + z, q), (at_x(-1) * NZ + z, q)

    def xa_piece(d, half):
        return pa.at[d, half * 4:(half + 1) * 4]

    def xa_copy(index, d, half, into, where):
        return remote(xa_piece(d, half), into, xa_send.at[index], xa_recv.at[index], where)

    xa = {
        "far0": xa_copy(0, at_x(2), 0, xa_mid.at[0], x_right),
        "far1": xa_copy(1, at_x(2), 1, xa_mid.at[1], x_left),
        "near1": xa_copy(2, at_x(1), 1, xa_fin.at[0, 1], x_right),
        "near0": xa_copy(3, at_x(3), 0, xa_fin.at[1, 0], x_left),
        "sum0": xa_copy(4, at_x(1), 0, xa_fin.at[0, 0], x_right),
        "sum1": xa_copy(5, at_x(3), 1, xa_fin.at[1, 1], x_left),
    }
    for name in ("far0", "far1", "near1", "near0"):
        xa[name].start()
    ends.extend(xa.values())

    for of in (-1, 1, -3, 3, 4):
        got(1, of)
    for k in range(1, NX):
        cx_copy(k).wait_recv()
    coupling = c_full[...]
    c_parts = split(coupling)
    ct_parts = split(coupling.T)

    prepare(1, s2)

    def mul_b(t, carry):
        columns = pl.ds(pl.multiple_of(t * 256, 256), 256)
        r = dot3((p_hi[1], p_lo[1]), (g_hi[:, columns], g_lo[:, columns]))
        first = jnp.concatenate(
            [pa[:, :, t, h].reshape(256, 128) * col_mask(s1, 2 * t + h) for h in (0, 1)], axis=1
        )
        r = r - dot3(ct_parts, split(first))
        pb[:, :, t, 0] = r[:, :128].reshape(NX, NZ, 8, 128)
        pb[:, :, t, 1] = r[:, 128:].reshape(NX, NZ, 8, 128)
        return carry

    lax.fori_loop(0, 4, mul_b, 0)

    def zb_copy(way, j, step):
        away = steps_of(way, j // 2) - step + 1
        d = at_z(away) if way == 0 else at_z(-away)
        to_z = at_z(1) if way == 0 else at_z(-1)
        return d, remote(
            pb.at[j, d], zb_in.at[way, j, step - 1],
            zb_send.at[way, j, step - 1], zb_recv.at[way, j, step - 1],
            (x * NZ + to_z, q),
        )

    def zb_step(step):
        for j in range(4):
            for way in (0, 1):
                if step > steps_of(way, j // 2):
                    continue
                d, copy = zb_copy(way, j, step)
                if step > 1:
                    zb_copy(way, j, step - 1)[1].wait_recv()
                    pb[j, d] += zb_in[way, j, step - 2]
                copy.start()
                ends.append(copy)

    zb_step(1)
    xa["far0"].wait_recv()
    pa[at_x(1), 0:4] += xa_mid[0]
    xa["sum0"].start()
    xa["far1"].wait_recv()
    pa[at_x(3), 4:8] += xa_mid[1]
    xa["sum1"].start()
    zb_step(2)
    zb_step(3)
    for name in ("near1", "near0", "sum0", "sum1"):
        xa[name].wait_recv()
    for half in (0, 1):
        rows = slice(half * 4, half * 4 + 4)
        za[rows] = pa[x, rows] + xa_fin[0, half] + xa_fin[1, half]

    def xb_copy(k):
        return remote(
            sb.at[at_x(k)], xb_in.at[k], xb_send.at[k], xb_recv.at[k], (at_x(k) * NZ + z, q)
        )

    def za_copy(k):
        return remote(
            za.at[at_z(k)], za_in.at[k], za_send.at[k], za_recv.at[k], (x * NZ + at_z(k), q)
        )

    to_col = 2 * z + 1 - lax.rem(x, 2)

    def hand_over(rows, into, parity, send, recv):
        return remote(
            rows.at[parity], into.at[x // 2], send.at[parity], recv.at[0],
            (q + 16 * parity, to_col),
        )

    for k in (4, 3, 5, 2, 6, 1, 7):
        za_copy(k).start()
    zb_step(4)
    for j in range(4):
        last = [steps_of(way, j // 2) for way in (0, 1)]
        for way in (0, 1):
            zb_copy(way, j, last[way])[1].wait_recv()
        sb[j] = pb[j, z] + zb_in[0, j, last[0] - 1] + zb_in[1, j, last[1] - 1]
    for k in (2, 1, 3):
        xb_copy(k).start()

    for k in range(1, NZ):
        za_copy(k).wait_recv()
    value = za[z]
    for k in range(1, NZ):
        value = value + za_in[k]
    for c in range(8):
        block = value[c // 2, c % 2] * (-col_mask(s1, c))
        out_a[c] = block
        rows_1[c % 2, c // 2] = block
    for parity in (0, 1):
        hand_over(rows_1, ex_a, parity, exa_send, exa_recv).start()
    for k in range(1, NX):
        xb_copy(k).wait_recv()
    value = sb[x] + xb_in[1] + xb_in[2] + xb_in[3]
    for c in range(8):
        block = value[c // 2, c % 2] * (-col_mask(s2, c))
        out_b[c] = block
        rows_2[c % 2, c // 2] = block
    for parity in (0, 1):
        hand_over(rows_2, ex_b, parity, exb_send, exb_recv).start()

    def at_sum(m, j):
        return j * NZ + lax.rem(y + 3 * m, NZ)

    def tile_copy(m, j):
        return remote(
            pt.at[m, j], rr.at[p], rr_send.at[m, j], rr_recv.at[0], (at_sum(m, j), q)
        )

    def panel_rows(ref):
        return split(jnp.concatenate([ref[:, r].reshape(16, 128) for r in range(4)], axis=1))

    def send_tiles(m, value):
        for s in range(2):
            for h in range(2):
                pt[m, s * 2 + h] = value[s * 8:(s + 1) * 8, h * 128:(h + 1) * 128]
        for j in range(4):
            @pl.when(at_sum(m, j) != p)
            def _():
                tile_copy(m, j).start()

            @pl.when(at_sum(m, j) == p)
            def _():
                pltpu.make_async_copy(pt.at[m, j], rr.at[p], rr_recv.at[0]).start()

    pltpu.make_async_copy(ex_a, ex_a, exa_recv.at[0]).wait()
    rows_a = panel_rows(ex_a)
    send_tiles(0, dot3(rows_a, (p_hi[0], p_lo[0]), NT))
    send_tiles(1, dot3(rows_a, (p_hi[1], p_lo[1]), NT))
    pltpu.make_async_copy(ex_b, ex_b, exb_recv.at[0]).wait()
    rows_b = panel_rows(ex_b)
    send_tiles(2, dot3(rows_b, (p_hi[1], p_lo[1]), NT))

    turn = lax.rem(z - y + NZ, NZ)
    mine = turn // 3

    def make_sums(which):
        @pl.when(which)
        def _():
            pltpu.make_async_copy(rr, rr, rr_recv.at[0]).wait()
            tile[...] = jnp.sum(rr[...], axis=0)
            place = fin.at[core, x, mine, y]
            spot = yz_recv.at[mine]
            pltpu.make_async_copy(tile, place, spot).start()

            def spread(k, carry):
                remote(
                    tile, place, yz_send.at[0], spot,
                    (x * NZ + at_z(k // NY), at_y(lax.rem(k, NY)) * 2 + core),
                ).start()
                return carry

            lax.fori_loop(1, NY * NZ, spread, 0)

    make_sums(jnp.logical_or(turn == 0, turn == 3))
    make_sums(turn == 6)

    def part(origin, which):
        return fin.at[core, origin, which]

    def fx_copy(which, k):
        return remote(
            part(x, which), part(x, which), fx_send.at[which, k], fx_recv.at[which, k],
            (at_x(k) * NZ + z, q),
        )

    def fs_copy(which, k):
        ref = part(at_x(-k), which)
        return remote(ref, ref, fs_send.at[which, k], fs_recv.at[which, k], sibling)

    for which in range(3):
        block = part(x, which)
        pltpu.make_async_copy(block, block, yz_recv.at[which]).wait()
        for k in (2, 1, 3):
            fx_copy(which, k).start()
        fs_copy(which, 0).start()
    for which in range(3):
        for k in (1, 3, 2):
            fx_copy(which, k).wait_recv()
            fs_copy(which, k).start()

    loads[1].wait()
    loads[2].wait()
    for k in range(4):
        fs_copy(0, k).wait_recv()
        fs_copy(1, k).wait_recv()

    def places():
        for co in range(2):
            for xo in range(4):
                xs, h = (1 - co) + 2 * (xo // 2), xo % 2
                yield (
                    slice(xs * 64, xs * 64 + 64), slice(h * 128, h * 128 + 128),
                    fin.at[co, xo],
                )

    for rows, columns, ref in places():
        own_1[rows, columns] = d1[rows, columns] - ref[0].reshape(64, 128)
        cross_out[rows, columns] = ref[1].reshape(64, 128)
    cross = -(cross_out[...].T + dot3(ct_parts, split(own_1[...])))
    cross_out[...] = cross
    last = d2[...] - dot3(split(cross), c_parts)
    for k in range(4):
        fs_copy(2, k).wait_recv()
    for rows, columns, ref in places():
        own_2[rows, columns] = last[rows, columns] - ref[2].reshape(64, 128)

    for copy in ends:
        copy.wait_send()
    for k in range(1, NZ):
        cz_copy(k).wait_send()
        za_copy(k).wait_send()
    for k in range(1, NX):
        cx_copy(k).wait_send()
        xb_copy(k).wait_send()
        for which in range(3):
            fx_copy(which, k).wait_send()
    for k in range(4):
        for which in range(3):
            fs_copy(which, k).wait_send()
    for parity in (0, 1):
        hand_over(rows_1, ex_a, parity, exa_send, exa_recv).wait_send()
        hand_over(rows_2, ex_b, parity, exb_send, exb_recv).wait_send()
    for m in range(3):
        for j in range(4):
            @pl.when(at_sum(m, j) != p)
            def _():
                tile_copy(m, j).wait_send()

    @pl.when(lax.rem(turn, 3) == 0)
    def _():
        pltpu.make_async_copy(all_sent, all_sent, yz_send.at[0]).wait()


def body(
    inverse_block,
    panel_first,
    panel_second,
    coupling,
    dinv_first,
    dinv_second,
    struct_first,
    struct_second,
):
    dma = pltpu.SemaphoreType.DMA
    any_space = pl.BlockSpec(memory_space=pl.ANY)
    vmem = pl.BlockSpec(memory_space=pltpu.VMEM)
    square = jax.ShapeDtypeStruct((256, 256), F32)
    rows = jax.ShapeDtypeStruct((8, 8, 128), F32)
    row_a, own_a, row_b, cross, own_b = pl.pallas_call(
        kernel,
        out_shape=(rows, square, rows, square, square),
        in_specs=[any_space] * 8,
        out_specs=(vmem,) * 5,
        scratch_shapes=[
            pltpu.SMEM((128,), jnp.int32),
            pltpu.SMEM((128,), jnp.int32),
            pltpu.VMEM((4096, 128), F32),
            pltpu.VMEM((512, 1024), BF16),
            pltpu.VMEM((512, 1024), BF16),
            pltpu.VMEM((2, 4, 256, 128), F32),
            pltpu.VMEM((2, 256, 512), BF16),
            pltpu.VMEM((2, 256, 512), BF16),
            pltpu.VMEM((256, 256), F32),
            pltpu.VMEM((256, 256), F32),
            pltpu.VMEM((256, 256), F32),
            pltpu.VMEM((4, 8, 4, 2, 8, 128), F32),
            pltpu.VMEM((4, 8, 4, 2, 8, 128), F32),
            pltpu.VMEM((8, 4, 2, 8, 128), F32),
            pltpu.VMEM((4, 4, 2, 8, 128), F32),
            pltpu.VMEM((2, 4, 4, 2, 8, 128), F32),
            pltpu.VMEM((2, 2, 4, 4, 2, 8, 128), F32),
            pltpu.VMEM((4, 4, 2, 8, 128), F32),
            pltpu.VMEM((8, 4, 2, 8, 128), F32),
            pltpu.VMEM((2, 4, 4, 4, 2, 8, 128), F32),
            pltpu.VMEM((2, 4, 8, 128), F32),
            pltpu.VMEM((2, 4, 8, 128), F32),
            pltpu.VMEM((2, 4, 8, 128), F32),
            pltpu.VMEM((2, 4, 8, 128), F32),
            pltpu.VMEM((3, 4, 8, 128), F32),
            pltpu.VMEM((32, 8, 128), F32),
            pltpu.VMEM((8, 128), F32),
            pltpu.VMEM((2, 4, 3, 8, 8, 128), F32),
            pltpu.VMEM((63, 8, 128), F32),
            dma((5,)), dma((3,)),
            dma((2, 9)), dma((2, 9)), dma((2, 9)), dma((2, 9)),
            dma((8,)), dma((8,)), dma((4,)), dma((4,)),
            dma((6,)), dma((6,)), dma((4,)), dma((4,)),
            dma((8,)), dma((8,)), dma((2, 4, 4)), dma((2, 4, 4)),
            dma((2,)), dma((1,)), dma((2,)), dma((1,)),
            dma((3, 4)), dma((1,)), dma((1,)), dma((3,)),
            dma((3, 4)), dma((3, 4)), dma((3, 4)), dma((3, 4)),
        ],
        compiler_params=pltpu.CompilerParams(
            collective_id=0, has_side_effects=True, vmem_limit_bytes=60 * 1024 * 1024
        ),
        name="selected_inversion",
    )(
        inverse_block.reshape(4096, 128),
        panel_first.reshape(4, 16, 128),
        panel_second.reshape(4, 16, 128),
        coupling, dinv_first, dinv_second, struct_first, struct_second,
    )
    return (
        row_a.reshape(8, 1, 8, 128), own_a, row_b.reshape(8, 1, 8, 128), cross, own_b,
    )


def solution(mesh):
    return jax.shard_map(
        body,
        mesh=mesh,
        in_specs=(
            P(None, "prow", None, None, "pcol", None),
            P(None, "prow", "pcol", None),
            P(None, "prow", "pcol", None),
            P("prow", None),
            P(),
            P(),
            P(),
            P(),
        ),
        out_specs=(P(None, "pcol", "prow", None), P(), P(None, "pcol", "prow", None), P(), P()),
        check_vma=False,
    )
```

```python
import jax
import jax.numpy as jnp
from jax import lax
from jax.experimental import pallas as pl
from jax.experimental.pallas import tpu as pltpu
from jax.sharding import PartitionSpec as P

NX, NZ, NY = 4, 8, 8
F32, BF16 = jnp.float32, jnp.bfloat16
MESH = pl.DeviceIdType.MESH

NN = (((1,), (0,)), ((), ()))
NT = (((1,), (1,)), ((), ()))


def split(v):
    hi = v.astype(BF16)
    return hi, (v - hi.astype(F32)).astype(BF16)


def dot3(a, b, dims=NN):
    def one(u, v):
        return lax.dot_general(u, v, dims, preferred_element_type=F32)

    return one(a[0], b[0]) + (one(a[0], b[1]) + one(a[1], b[0]))


def steps_of(way, half):
    return 4 if (way == 0) == (half == 0) else 3


def kernel(
    g_hbm, a_hbm, b_hbm, c_hbm, d1_hbm, d2_hbm, s1_hbm, s2_hbm,
    out_a, own_1, out_b, cross_out, own_2,
    s1, s2, g_raw, g_hi, g_lo, full, p_hi, p_lo, c_full, d1, d2,
    pa, pb, za, sb,
    xa_mid, xa_fin, xb_in, za_in, zb_in,
    rows_1, rows_2, ex_a, ex_b, pt, rr, tile, fin, all_sent,
    load_sem, own_sem,
    ag_send, ag_recv, sib_send, sib_recv, cz_send, cz_recv, cx_send, cx_recv,
    xa_send, xa_recv, xb_send, xb_recv, za_send, za_recv, zb_send, zb_recv,
    exa_send, exa_recv, exb_send, exb_recv, rr_send, rr_recv, yz_send, yz_recv,
    fx_send, fx_recv, fs_send, fs_recv,
):
    p = lax.axis_index("prow")
    q = lax.axis_index("pcol")
    x, z = p // NZ, lax.rem(p, NZ)
    y, core = q // 2, lax.rem(q, 2)

    def at_x(k):
        return lax.rem(x + k + NX, NX)

    def at_z(k):
        return lax.rem(z + k + NZ, NZ)

    def at_y(k):
        return lax.rem(y + k + NY, NY)

    sibling = (p, y * 2 + 1 - core)

    def remote(src, dst, send, recv, where):
        return pltpu.make_async_remote_copy(
            src_ref=src, dst_ref=dst, send_sem=send, recv_sem=recv,
            device_id=where, device_id_type=MESH,
        )

    barrier = pltpu.get_barrier_semaphore()
    near = [(p, at_y(k) * 2 + core) for k in (1, -1, 2, -2)] + [sibling]
    near += [(x * NZ + at_z(k), q) for k in range(1, NZ)]
    near += [(at_x(k) * NZ + z, q) for k in range(1, NX)]
    for where in near:
        pl.semaphore_signal(barrier, inc=1, device_id=where, device_id_type=MESH)

    rows16 = pl.ds(pl.multiple_of(q * 16, 16), 16)
    rows8 = pl.ds(pl.multiple_of(p * 8, 8), 8)
    own = [
        pltpu.make_async_copy(a_hbm, full.at[0, :, rows16], own_sem.at[0]),
        pltpu.make_async_copy(b_hbm, full.at[1, :, rows16], own_sem.at[1]),
        pltpu.make_async_copy(c_hbm, c_full.at[rows8], own_sem.at[2]),
    ]
    loads = [
        pltpu.make_async_copy(g_hbm, g_raw, load_sem.at[0]),
        pltpu.make_async_copy(d1_hbm, d1, load_sem.at[1]),
        pltpu.make_async_copy(d2_hbm, d2, load_sem.at[2]),
        pltpu.make_async_copy(s1_hbm, s1, load_sem.at[3]),
        pltpu.make_async_copy(s2_hbm, s2, load_sem.at[4]),
    ]
    for copy in own + loads:
        copy.start()

    pl.semaphore_wait(barrier, len(near))

    ends = []

    def shard(k, row_y):
        rows = row_y * 2 + core
        return full.at[k, :, pl.ds(pl.multiple_of(rows * 16, 16), 16)]

    def ring(k, of, to):
        ref = shard(k, at_y(of))
        return remote(
            ref, ref, ag_send.at[k, of - to + 4], ag_recv.at[k, of - to + 4],
            (p, at_y(to) * 2 + core),
        )

    def push(k, of, to):
        copy = ring(k, of, to)
        copy.start()
        ends.append(copy)

    crossing = {0: [], 1: []}

    def across(k, of):
        ref = shard(k, at_y(of))
        copy = remote(ref, ref, sib_send.at[k, of + 4], sib_recv.at[k, of + 4], sibling)
        copy.start()
        ends.append(copy)
        crossing[k].append(copy)

    def got(k, of):
        ring(k, of, 0).wait_recv()
        across(k, of)

    own[0].wait()
    for to in (2, -2, 1, -1):
        push(0, 0, to)
    across(0, 0)
    own[1].wait()
    for to in (2, -2):
        push(1, 0, to)
    own[2].wait()

    def cz_copy(k):
        return remote(
            c_full.at[rows8], c_full.at[rows8], cz_send.at[k], cz_recv.at[k],
            (x * NZ + at_z(k), q),
        )

    for k in range(1, NZ):
        cz_copy(k).start()

    for index in (0, 3, 4):
        loads[index].wait()

    def split_g(c, carry):
        hi, lo = split(g_raw[pl.ds(c, 512, stride=8), :])
        columns = pl.ds(pl.multiple_of(c * 128, 128), 128)
        g_hi[:, columns] = hi
        g_lo[:, columns] = lo
        return carry

    lax.fori_loop(0, 8, split_g, 0)

    def forward(k, of):
        ring(k, of, 0).wait_recv()
        way = 1 if of < 0 else -1
        push(k, of, way)
        if (of < 0) == (k == 0):
            push(k, of, 2 * way)
        across(k, of)

    forward(0, -2)
    forward(0, 2)
    for to in (1, -1):
        push(1, 0, to)
    across(1, 0)
    got(0, -1)
    got(0, 1)
    forward(1, -2)
    forward(1, 2)
    for k in range(1, NZ):
        cz_copy(k).wait_recv()
    rows64 = pl.ds(pl.multiple_of(x * 64, 64), 64)

    def cx_copy(k):
        return remote(
            c_full.at[rows64], c_full.at[rows64], cx_send.at[k], cx_recv.at[k],
            (at_x(k) * NZ + z, q),
        )

    for k in range(1, NX):
        cx_copy(k).start()
    got(0, -3)
    got(0, 3)
    got(0, -4)

    def prepare(k, struct):
        for copy in crossing[k]:
            copy.wait_recv()
        for r in range(4):
            mask = struct[r * (NX * NZ) + p].astype(F32)
            hi, lo = split(full[k, r] * mask)
            p_hi[k, :, r * 128:(r + 1) * 128] = hi
            p_lo[k, :, r * 128:(r + 1) * 128] = lo

    def col_mask(struct, c):
        return struct[c * (NY * 2) + q].astype(F32)

    prepare(0, s1)

    def mul_a(t, carry):
        columns = pl.ds(pl.multiple_of(t * 256, 256), 256)
        r = dot3((p_hi[0], p_lo[0]), (g_hi[:, columns], g_lo[:, columns]))
        pa[:, :, t, 0] = r[:, :128].reshape(NX, NZ, 8, 128)
        pa[:, :, t, 1] = r[:, 128:].reshape(NX, NZ, 8, 128)
        return carry

    lax.fori_loop(0, 4, mul_a, 0)

    def zb_copy(way, j, step):
        away = steps_of(way, j // 2) - step + 1
        d = at_z(away) if way == 0 else at_z(-away)
        to_z = at_z(1) if way == 0 else at_z(-1)
        mine = pa.at[j, d] if step == 1 else zb_in.at[way, j, step - 2]
        return d, remote(
            mine, zb_in.at[way, j, step - 1],
            zb_send.at[way, j, step - 1], zb_recv.at[way, j, step - 1],
            (x * NZ + to_z, q),
        )

    def zb_step(step):
        for j in range(4):
            for way in (0, 1):
                if step > steps_of(way, j // 2):
                    continue
                d, copy = zb_copy(way, j, step)
                if step > 1:
                    zb_copy(way, j, step - 1)[1].wait_recv()
                    zb_in[way, j, step - 2] += pa[j, d]
                copy.start()
                ends.append(copy)

    zb_step(1)

    for of in (-1, 1, -3, 3, 4):
        got(1, of)
    zb_step(2)
    for k in range(1, NX):
        cx_copy(k).wait_recv()
    coupling = c_full[...]
    c_parts = split(coupling)
    ct_parts = split(coupling.T)

    prepare(1, s2)

    def mul_b(t, carry):
        columns = pl.ds(pl.multiple_of(t * 256, 256), 256)
        r = dot3((p_hi[1], p_lo[1]), (g_hi[:, columns], g_lo[:, columns]))
        first = jnp.concatenate(
            [pa[:, :, t, h].reshape(256, 128) * col_mask(s1, 2 * t + h) for h in (0, 1)], axis=1
        )
        r = r - dot3(ct_parts, split(first))
        pb[:, :, t, 0] = r[:, :128].reshape(NX, NZ, 8, 128)
        pb[:, :, t, 1] = r[:, 128:].reshape(NX, NZ, 8, 128)
        return carry

    lax.fori_loop(0, 4, mul_b, 0)

    x_right, x_left = (at_x(1) * NZ + z, q), (at_x(-1) * NZ + z, q)

    def xa_piece(d, half):
        return pb.at[d, half * 4:(half + 1) * 4]

    def xa_copy(index, d, half, into, where):
        return remote(xa_piece(d, half), into, xa_send.at[index], xa_recv.at[index], where)

    xa = {
        "far0": xa_copy(0, at_x(2), 0, xa_mid.at[0], x_right),
        "far1": xa_copy(1, at_x(2), 1, xa_mid.at[1], x_left),
        "near1": xa_copy(2, at_x(1), 1, xa_fin.at[0, 1], x_right),
        "near0": xa_copy(3, at_x(3), 0, xa_fin.at[1, 0], x_left),
        "sum0": xa_copy(4, at_x(1), 0, xa_fin.at[0, 0], x_right),
        "sum1": xa_copy(5, at_x(3), 1, xa_fin.at[1, 1], x_left),
    }
    for name in ("far0", "far1", "near1", "near0"):
        xa[name].start()
    ends.extend(xa.values())
    zb_step(3)
    xa["far0"].wait_recv()
    pb[at_x(1), 0:4] += xa_mid[0]
    xa["sum0"].start()
    xa["far1"].wait_recv()
    pb[at_x(3), 4:8] += xa_mid[1]
    xa["sum1"].start()
    zb_step(4)
    for j in range(4):
        last = [steps_of(way, j // 2) for way in (0, 1)]
        for way in (0, 1):
            zb_copy(way, j, last[way])[1].wait_recv()
        sb[j] = pa[j, z] + zb_in[0, j, last[0] - 1] + zb_in[1, j, last[1] - 1]

    def xb_copy(k):
        return remote(
            sb.at[at_x(k)], xb_in.at[k], xb_send.at[k], xb_recv.at[k], (at_x(k) * NZ + z, q)
        )

    def za_copy(k):
        return remote(
            za.at[at_z(k)], za_in.at[k], za_send.at[k], za_recv.at[k], (x * NZ + at_z(k), q)
        )

    to_col = 2 * z + 1 - lax.rem(x, 2)

    def hand_over(rows, into, parity, send, recv):
        return remote(
            rows.at[parity], into.at[x // 2], send.at[parity], recv.at[0],
            (q + 16 * parity, to_col),
        )

    for k in (2, 1, 3):
        xb_copy(k).start()
    for name in ("near1", "near0", "sum0", "sum1"):
        xa[name].wait_recv()
    for half in (0, 1):
        rows = slice(half * 4, half * 4 + 4)
        za[rows] = pb[x, rows] + xa_fin[0, half] + xa_fin[1, half]
    for k in (4, 3, 5, 2, 6, 1, 7):
        za_copy(k).start()

    def deliver(value, struct, out, rows, into, send, recv):
        for c in range(8):
            block = value[c // 2, c % 2] * (-col_mask(struct, c))
            out[c] = block
            rows[c % 2, c // 2] = block
        for parity in (0, 1):
            hand_over(rows, into, parity, send, recv).start()

    for k in range(1, NX):
        xb_copy(k).wait_recv()
    deliver(
        sb[x] + xb_in[1] + xb_in[2] + xb_in[3], s1, out_a, rows_1, ex_a, exa_send, exa_recv
    )
    for k in range(1, NZ):
        za_copy(k).wait_recv()
    value = za[z]
    for k in range(1, NZ):
        value = value + za_in[k]
    deliver(value, s2, out_b, rows_2, ex_b, exb_send, exb_recv)

    def at_sum(m, j):
        return j * NZ + lax.rem(y + 3 * m, NZ)

    def tile_copy(m, j):
        return remote(
            pt.at[m, j], rr.at[p], rr_send.at[m, j], rr_recv.at[0], (at_sum(m, j), q)
        )

    def panel_rows(ref):
        return split(jnp.concatenate([ref[:, r].reshape(16, 128) for r in range(4)], axis=1))

    def send_tiles(m, value):
        for s in range(2):
            for h in range(2):
                pt[m, s * 2 + h] = value[s * 8:(s + 1) * 8, h * 128:(h + 1) * 128]
        for j in range(4):
            @pl.when(at_sum(m, j) != p)
            def _():
                tile_copy(m, j).start()

            @pl.when(at_sum(m, j) == p)
            def _():
                pltpu.make_async_copy(pt.at[m, j], rr.at[p], rr_recv.at[0]).start()

    pltpu.make_async_copy(ex_a, ex_a, exa_recv.at[0]).wait()
    rows_a = panel_rows(ex_a)
    send_tiles(0, dot3(rows_a, (p_hi[0], p_lo[0]), NT))
    send_tiles(1, dot3(rows_a, (p_hi[1], p_lo[1]), NT))
    pltpu.make_async_copy(ex_b, ex_b, exb_recv.at[0]).wait()
    rows_b = panel_rows(ex_b)
    send_tiles(2, dot3(rows_b, (p_hi[1], p_lo[1]), NT))

    turn = lax.rem(z - y + NZ, NZ)
    mine = turn // 3

    def make_sums(which):
        @pl.when(which)
        def _():
            pltpu.make_async_copy(rr, rr, rr_recv.at[0]).wait()
            tile[...] = jnp.sum(rr[...], axis=0)
            place = fin.at[core, x, mine, y]
            spot = yz_recv.at[mine]
            pltpu.make_async_copy(tile, place, spot).start()

            def far_first(k):
                return 4 + (k + 1) // 2 * (1 - 2 * lax.rem(k, 2))

            def spread(k, carry):
                to_z, to_y = at_z(far_first(k // NY)), at_y(far_first(lax.rem(k, NY)))
                remote(
                    tile, place, yz_send.at[0], spot, (x * NZ + to_z, to_y * 2 + core)
                ).start()
                return carry

            lax.fori_loop(0, NY * NZ - 1, spread, 0)

    make_sums(jnp.logical_or(turn == 0, turn == 3))
    make_sums(turn == 6)

    def part(origin, which):
        return fin.at[core, origin, which]

    def fx_copy(which, k):
        return remote(
            part(x, which), part(x, which), fx_send.at[which, k], fx_recv.at[which, k],
            (at_x(k) * NZ + z, q),
        )

    def fs_copy(which, k):
        ref = part(at_x(-k), which)
        return remote(ref, ref, fs_send.at[which, k], fs_recv.at[which, k], sibling)

    for which in range(3):
        block = part(x, which)
        pltpu.make_async_copy(block, block, yz_recv.at[which]).wait()
        for k in (2, 1, 3):
            fx_copy(which, k).start()
        fs_copy(which, 0).start()
    for which in range(3):
        for k in (1, 3, 2):
            fx_copy(which, k).wait_recv()
            fs_copy(which, k).start()

    loads[1].wait()
    loads[2].wait()
    for k in range(4):
        fs_copy(0, k).wait_recv()
        fs_copy(1, k).wait_recv()

    def places():
        for co in range(2):
            for xo in range(4):
                xs, h = (1 - co) + 2 * (xo // 2), xo % 2
                yield (
                    slice(xs * 64, xs * 64 + 64), slice(h * 128, h * 128 + 128),
                    fin.at[co, xo],
                )

    for rows, columns, ref in places():
        own_1[rows, columns] = d1[rows, columns] - ref[0].reshape(64, 128)
        cross_out[rows, columns] = ref[1].reshape(64, 128)
    cross = -(cross_out[...].T + dot3(ct_parts, split(own_1[...])))
    cross_out[...] = cross
    last = d2[...] - dot3(split(cross), c_parts)
    for k in range(4):
        fs_copy(2, k).wait_recv()
    for rows, columns, ref in places():
        own_2[rows, columns] = last[rows, columns] - ref[2].reshape(64, 128)

    for copy in ends:
        copy.wait_send()
    for k in range(1, NZ):
        cz_copy(k).wait_send()
        za_copy(k).wait_send()
    for k in range(1, NX):
        cx_copy(k).wait_send()
        xb_copy(k).wait_send()
        for which in range(3):
            fx_copy(which, k).wait_send()
    for k in range(4):
        for which in range(3):
            fs_copy(which, k).wait_send()
    for parity in (0, 1):
        hand_over(rows_1, ex_a, parity, exa_send, exa_recv).wait_send()
        hand_over(rows_2, ex_b, parity, exb_send, exb_recv).wait_send()
    for m in range(3):
        for j in range(4):
            @pl.when(at_sum(m, j) != p)
            def _():
                tile_copy(m, j).wait_send()

    @pl.when(lax.rem(turn, 3) == 0)
    def _():
        pltpu.make_async_copy(all_sent, all_sent, yz_send.at[0]).wait()


def body(
    inverse_block,
    panel_first,
    panel_second,
    coupling,
    dinv_first,
    dinv_second,
    struct_first,
    struct_second,
):
    dma = pltpu.SemaphoreType.DMA
    any_space = pl.BlockSpec(memory_space=pl.ANY)
    vmem = pl.BlockSpec(memory_space=pltpu.VMEM)
    square = jax.ShapeDtypeStruct((256, 256), F32)
    rows = jax.ShapeDtypeStruct((8, 8, 128), F32)
    row_a, own_a, row_b, cross, own_b = pl.pallas_call(
        kernel,
        out_shape=(rows, square, rows, square, square),
        in_specs=[any_space] * 8,
        out_specs=(vmem,) * 5,
        scratch_shapes=[
            pltpu.SMEM((128,), jnp.int32),
            pltpu.SMEM((128,), jnp.int32),
            pltpu.VMEM((4096, 128), F32),
            pltpu.VMEM((512, 1024), BF16),
            pltpu.VMEM((512, 1024), BF16),
            pltpu.VMEM((2, 4, 256, 128), F32),
            pltpu.VMEM((2, 256, 512), BF16),
            pltpu.VMEM((2, 256, 512), BF16),
            pltpu.VMEM((256, 256), F32),
            pltpu.VMEM((256, 256), F32),
            pltpu.VMEM((256, 256), F32),
            pltpu.VMEM((4, 8, 4, 2, 8, 128), F32),
            pltpu.VMEM((4, 8, 4, 2, 8, 128), F32),
            pltpu.VMEM((8, 4, 2, 8, 128), F32),
            pltpu.VMEM((4, 4, 2, 8, 128), F32),
            pltpu.VMEM((2, 4, 4, 2, 8, 128), F32),
            pltpu.VMEM((2, 2, 4, 4, 2, 8, 128), F32),
            pltpu.VMEM((4, 4, 2, 8, 128), F32),
            pltpu.VMEM((8, 4, 2, 8, 128), F32),
            pltpu.VMEM((2, 4, 4, 4, 2, 8, 128), F32),
            pltpu.VMEM((2, 4, 8, 128), F32),
            pltpu.VMEM((2, 4, 8, 128), F32),
            pltpu.VMEM((2, 4, 8, 128), F32),
            pltpu.VMEM((2, 4, 8, 128), F32),
            pltpu.VMEM((3, 4, 8, 128), F32),
            pltpu.VMEM((32, 8, 128), F32),
            pltpu.VMEM((8, 128), F32),
            pltpu.VMEM((2, 4, 3, 8, 8, 128), F32),
            pltpu.VMEM((63, 8, 128), F32),
            dma((5,)), dma((3,)),
            dma((2, 9)), dma((2, 9)), dma((2, 9)), dma((2, 9)),
            dma((8,)), dma((8,)), dma((4,)), dma((4,)),
            dma((6,)), dma((6,)), dma((4,)), dma((4,)),
            dma((8,)), dma((8,)), dma((2, 4, 4)), dma((2, 4, 4)),
            dma((2,)), dma((1,)), dma((2,)), dma((1,)),
            dma((3, 4)), dma((1,)), dma((1,)), dma((3,)),
            dma((3, 4)), dma((3, 4)), dma((3, 4)), dma((3, 4)),
        ],
        compiler_params=pltpu.CompilerParams(
            collective_id=0, has_side_effects=True, vmem_limit_bytes=60 * 1024 * 1024
        ),
        name="selected_inversion",
    )(
        inverse_block.reshape(4096, 128),
        panel_first.reshape(4, 16, 128),
        panel_second.reshape(4, 16, 128),
        coupling, dinv_first, dinv_second, struct_first, struct_second,
    )
    return (
        row_a.reshape(8, 1, 8, 128), own_a, row_b.reshape(8, 1, 8, 128), cross, own_b,
    )


def solution(mesh):
    return jax.shard_map(
        body,
        mesh=mesh,
        in_specs=(
            P(None, "prow", None, None, "pcol", None),
            P(None, "prow", "pcol", None),
            P(None, "prow", "pcol", None),
            P("prow", None),
            P(),
            P(),
            P(),
            P(),
        ),
        out_specs=(P(None, "pcol", "prow", None), P(), P(None, "pcol", "prow", None), P(), P()),
        check_vma=False,
    )
```

```python
import jax
import jax.numpy as jnp
from jax import lax
from jax.experimental import pallas as pl
from jax.experimental.pallas import tpu as pltpu
from jax.sharding import PartitionSpec as P

NX, NZ, NY = 4, 8, 8
F32, BF16 = jnp.float32, jnp.bfloat16
MESH = pl.DeviceIdType.MESH

NN = (((1,), (0,)), ((), ()))
NT = (((1,), (1,)), ((), ()))


def split(v):
    hi = v.astype(BF16)
    return hi, (v - hi.astype(F32)).astype(BF16)


def dot3(a, b, dims=NN):
    def one(u, v):
        return lax.dot_general(u, v, dims, preferred_element_type=F32)

    return one(a[0], b[0]) + (one(a[0], b[1]) + one(a[1], b[0]))


def steps_of(way, half):
    return 4 if (way == 0) == (half == 0) else 3


def kernel(
    g_hbm, a_hbm, b_hbm, c_hbm, d1_hbm, d2_hbm, s1_hbm, s2_hbm,
    out_a, own_1, out_b, cross_out, own_2,
    s1, s2, g_raw, g_hi, g_lo, full, p_hi, p_lo, c_full, d1, d2,
    pa, pb, za, sb,
    xa_mid, xa_fin, xb_in, za_in, zb_in,
    rows_1, rows_2, ex_a, ex_b, pt, rr, tile, fin, all_sent,
    load_sem, own_sem,
    ag_send, ag_recv, sib_send, sib_recv, cz_send, cz_recv, cx_send, cx_recv,
    xa_send, xa_recv, xb_send, xb_recv, za_send, za_recv, zb_send, zb_recv,
    exa_send, exa_recv, exb_send, exb_recv, rr_send, rr_recv, yz_send, yz_recv,
    fx_send, fx_recv, fs_send, fs_recv,
):
    p = lax.axis_index("prow")
    q = lax.axis_index("pcol")
    x, z = p // NZ, lax.rem(p, NZ)
    y, core = q // 2, lax.rem(q, 2)

    def at_x(k):
        return lax.rem(x + k + NX, NX)

    def at_z(k):
        return lax.rem(z + k + NZ, NZ)

    def at_y(k):
        return lax.rem(y + k + NY, NY)

    sibling = (p, y * 2 + 1 - core)

    def remote(src, dst, send, recv, where):
        return pltpu.make_async_remote_copy(
            src_ref=src, dst_ref=dst, send_sem=send, recv_sem=recv,
            device_id=where, device_id_type=MESH,
        )

    barrier = pltpu.get_barrier_semaphore()
    near = [(p, at_y(k) * 2 + core) for k in (1, -1, 2, -2)] + [sibling]
    near += [(x * NZ + at_z(k), q) for k in range(1, NZ)]
    near += [(at_x(k) * NZ + z, q) for k in range(1, NX)]
    for where in near:
        pl.semaphore_signal(barrier, inc=1, device_id=where, device_id_type=MESH)

    rows16 = pl.ds(pl.multiple_of(q * 16, 16), 16)
    rows8 = pl.ds(pl.multiple_of(p * 8, 8), 8)
    own = [
        pltpu.make_async_copy(a_hbm, full.at[0, :, rows16], own_sem.at[0]),
        pltpu.make_async_copy(b_hbm, full.at[1, :, rows16], own_sem.at[1]),
        pltpu.make_async_copy(c_hbm, c_full.at[rows8], own_sem.at[2]),
    ]
    loads = [
        pltpu.make_async_copy(g_hbm, g_raw, load_sem.at[0]),
        pltpu.make_async_copy(d1_hbm, d1, load_sem.at[1]),
        pltpu.make_async_copy(d2_hbm, d2, load_sem.at[2]),
        pltpu.make_async_copy(s1_hbm, s1, load_sem.at[3]),
        pltpu.make_async_copy(s2_hbm, s2, load_sem.at[4]),
    ]
    for copy in own + loads:
        copy.start()

    pl.semaphore_wait(barrier, len(near))

    ends = []

    def shard(k, row_y):
        rows = row_y * 2 + core
        return full.at[k, :, pl.ds(pl.multiple_of(rows * 16, 16), 16)]

    def ring(k, of, to):
        ref = shard(k, at_y(of))
        return remote(
            ref, ref, ag_send.at[k, of - to + 4], ag_recv.at[k, of - to + 4],
            (p, at_y(to) * 2 + core),
        )

    def push(k, of, to):
        copy = ring(k, of, to)
        copy.start()
        ends.append(copy)

    crossing = {0: [], 1: []}

    def across(k, of):
        ref = shard(k, at_y(of))
        copy = remote(ref, ref, sib_send.at[k, of + 4], sib_recv.at[k, of + 4], sibling)
        copy.start()
        ends.append(copy)
        crossing[k].append(copy)

    def got(k, of):
        ring(k, of, 0).wait_recv()
        across(k, of)

    own[0].wait()
    for to in (2, -2, 1, -1):
        push(0, 0, to)
    across(0, 0)
    own[1].wait()
    for to in (2, -2):
        push(1, 0, to)
    own[2].wait()

    def cz_copy(k):
        return remote(
            c_full.at[rows8], c_full.at[rows8], cz_send.at[k], cz_recv.at[k],
            (x * NZ + at_z(k), q),
        )

    for k in range(1, NZ):
        cz_copy(k).start()

    for index in (0, 3, 4):
        loads[index].wait()

    def split_g(c, carry):
        hi, lo = split(g_raw[pl.ds(c, 512, stride=8), :])
        columns = pl.ds(pl.multiple_of(c * 128, 128), 128)
        g_hi[:, columns] = hi
        g_lo[:, columns] = lo
        return carry

    lax.fori_loop(0, 8, split_g, 0)

    def forward(k, of):
        ring(k, of, 0).wait_recv()
        way = 1 if of < 0 else -1
        push(k, of, way)
        if (of < 0) == (k == 0):
            push(k, of, 2 * way)
        across(k, of)

    forward(0, -2)
    forward(0, 2)
    for to in (1, -1):
        push(1, 0, to)
    across(1, 0)
    got(0, -1)
    got(0, 1)
    forward(1, -2)
    forward(1, 2)
    for k in range(1, NZ):
        cz_copy(k).wait_recv()
    rows64 = pl.ds(pl.multiple_of(x * 64, 64), 64)

    def cx_copy(k):
        return remote(
            c_full.at[rows64], c_full.at[rows64], cx_send.at[k], cx_recv.at[k],
            (at_x(k) * NZ + z, q),
        )

    for k in range(1, NX):
        cx_copy(k).start()
    got(0, -3)
    got(0, 3)
    got(0, -4)

    def prepare(k, struct):
        for copy in crossing[k]:
            copy.wait_recv()
        for r in range(4):
            mask = struct[r * (NX * NZ) + p].astype(F32)
            hi, lo = split(full[k, r] * mask)
            p_hi[k, :, r * 128:(r + 1) * 128] = hi
            p_lo[k, :, r * 128:(r + 1) * 128] = lo

    def col_mask(struct, c):
        return struct[c * (NY * 2) + q].astype(F32)

    prepare(0, s1)

    def mul_a(t, carry):
        columns = pl.ds(pl.multiple_of(t * 256, 256), 256)
        r = dot3((p_hi[0], p_lo[0]), (g_hi[:, columns], g_lo[:, columns]))
        pa[:, :, t, 0] = r[:, :128].reshape(NX, NZ, 8, 128)
        pa[:, :, t, 1] = r[:, 128:].reshape(NX, NZ, 8, 128)
        return carry

    lax.fori_loop(0, 4, mul_a, 0)

    x_right, x_left = (at_x(1) * NZ + z, q), (at_x(-1) * NZ + z, q)

    def xa_piece(d, half):
        return pa.at[d, half * 4:(half + 1) * 4]

    def xa_copy(index, d, half, into, where):
        return remote(xa_piece(d, half), into, xa_send.at[index], xa_recv.at[index], where)

    xa = {
        "far0": xa_copy(0, at_x(2), 0, xa_mid.at[0], x_right),
        "far1": xa_copy(1, at_x(2), 1, xa_mid.at[1], x_left),
        "near1": xa_copy(2, at_x(1), 1, xa_fin.at[0, 1], x_right),
        "near0": xa_copy(3, at_x(3), 0, xa_fin.at[1, 0], x_left),
        "sum0": xa_copy(4, at_x(1), 0, xa_fin.at[0, 0], x_right),
        "sum1": xa_copy(5, at_x(3), 1, xa_fin.at[1, 1], x_left),
    }
    for name in ("far0", "far1", "near1", "near0"):
        xa[name].start()
    ends.extend(xa.values())

    for of in (-1, 1, -3, 3, 4):
        got(1, of)
    for k in range(1, NX):
        cx_copy(k).wait_recv()
    coupling = c_full[...]
    c_parts = split(coupling)
    ct_parts = split(coupling.T)

    def mul_c(t, carry):
        first = jnp.concatenate(
            [pa[:, :, t, h].reshape(256, 128) * col_mask(s1, 2 * t + h) for h in (0, 1)], axis=1
        )
        r = dot3(ct_parts, split(first))
        pb[:, :, t, 0] = r[:, :128].reshape(NX, NZ, 8, 128)
        pb[:, :, t, 1] = r[:, 128:].reshape(NX, NZ, 8, 128)
        return carry

    lax.fori_loop(0, 4, mul_c, 0)
    prepare(1, s2)

    def mul_b(t, carry):
        columns = pl.ds(pl.multiple_of(t * 256, 256), 256)
        r = dot3((p_hi[1], p_lo[1]), (g_hi[:, columns], g_lo[:, columns]))
        for h in (0, 1):
            block = r[:, h * 128:(h + 1) * 128].reshape(NX, NZ, 8, 128)
            pb[:, :, t, h] = block - pb[:, :, t, h]
        return carry

    lax.fori_loop(0, 4, mul_b, 0)

    def zb_copy(way, j, step):
        away = steps_of(way, j // 2) - step + 1
        d = at_z(away) if way == 0 else at_z(-away)
        to_z = at_z(1) if way == 0 else at_z(-1)
        return d, remote(
            pb.at[j, d], zb_in.at[way, j, step - 1],
            zb_send.at[way, j, step - 1], zb_recv.at[way, j, step - 1],
            (x * NZ + to_z, q),
        )

    def zb_step(step):
        for j in range(4):
            for way in (0, 1):
                if step > steps_of(way, j // 2):
                    continue
                d, copy = zb_copy(way, j, step)
                if step > 1:
                    zb_copy(way, j, step - 1)[1].wait_recv()
                    pb[j, d] += zb_in[way, j, step - 2]
                copy.start()
                ends.append(copy)

    zb_step(1)
    xa["far0"].wait_recv()
    pa[at_x(1), 0:4] += xa_mid[0]
    xa["sum0"].start()
    xa["far1"].wait_recv()
    pa[at_x(3), 4:8] += xa_mid[1]
    xa["sum1"].start()
    zb_step(2)
    zb_step(3)
    for name in ("near1", "near0", "sum0", "sum1"):
        xa[name].wait_recv()
    for half in (0, 1):
        rows = slice(half * 4, half * 4 + 4)
        za[rows] = pa[x, rows] + xa_fin[0, half] + xa_fin[1, half]

    def xb_copy(k):
        return remote(
            sb.at[at_x(k)], xb_in.at[k], xb_send.at[k], xb_recv.at[k], (at_x(k) * NZ + z, q)
        )

    def za_copy(way, half, step):
        away = steps_of(way, half) - step + 1
        d = at_z(away) if way == 0 else at_z(-away)
        to_z = at_z(1) if way == 0 else at_z(-1)
        return d, remote(
            za.at[d, half * 2:(half + 1) * 2], za_in.at[way, half, step - 1],
            za_send.at[way, half, step - 1], za_recv.at[way, half, step - 1],
            (x * NZ + to_z, q),
        )

    def za_step(step):
        for half in (0, 1):
            for way in (0, 1):
                if step > steps_of(way, half):
                    continue
                d, copy = za_copy(way, half, step)
                if step > 1:
                    za_copy(way, half, step - 1)[1].wait_recv()
                    za[d, half * 2:(half + 1) * 2] += za_in[way, half, step - 2]
                copy.start()
                ends.append(copy)

    to_col = 2 * z + 1 - lax.rem(x, 2)

    def hand_over(rows, into, parity, send, recv):
        return remote(
            rows.at[parity], into.at[x // 2], send.at[parity], recv.at[0],
            (q + 16 * parity, to_col),
        )

    za_step(1)
    zb_step(4)
    za_step(2)
    za_step(3)
    for j in range(4):
        last = [steps_of(way, j // 2) for way in (0, 1)]
        for way in (0, 1):
            zb_copy(way, j, last[way])[1].wait_recv()
        sb[j] = pb[j, z] + zb_in[0, j, last[0] - 1] + zb_in[1, j, last[1] - 1]
    for k in (2, 1, 3):
        xb_copy(k).start()

    za_step(4)

    def deliver(value, c, struct, out, rows):
        block = value * (-col_mask(struct, c))
        out[c] = block
        rows[c % 2, c // 2] = block

    for k in range(1, NX):
        xb_copy(k).wait_recv()
    value = sb[x] + xb_in[1] + xb_in[2] + xb_in[3]
    for c in range(8):
        deliver(value[c // 2, c % 2], c, s2, out_b, rows_2)
    for parity in (0, 1):
        hand_over(rows_2, ex_b, parity, exb_send, exb_recv).start()
    for half in (0, 1):
        last = [steps_of(way, half) for way in (0, 1)]
        for way in (0, 1):
            za_copy(way, half, last[way])[1].wait_recv()
        value = za[z, half * 2:(half + 1) * 2]
        value = value + za_in[0, half, last[0] - 1] + za_in[1, half, last[1] - 1]
        for c in range(4 * half, 4 * half + 4):
            deliver(value[c // 2 - 2 * half, c % 2], c, s1, out_a, rows_1)
    for parity in (0, 1):
        hand_over(rows_1, ex_a, parity, exa_send, exa_recv).start()

    def at_sum(m, j):
        return j * NZ + lax.rem(y + 3 * m, NZ)

    def tile_copy(m, j):
        return remote(
            pt.at[m, j], rr.at[p], rr_send.at[m, j], rr_recv.at[0], (at_sum(m, j), q)
        )

    def panel_rows(ref):
        return split(jnp.concatenate([ref[:, r].reshape(16, 128) for r in range(4)], axis=1))

    def send_tiles(m, value):
        for s in range(2):
            for h in range(2):
                pt[m, s * 2 + h] = value[s * 8:(s + 1) * 8, h * 128:(h + 1) * 128]
        for j in range(4):
            @pl.when(at_sum(m, j) != p)
            def _():
                tile_copy(m, j).start()

            @pl.when(at_sum(m, j) == p)
            def _():
                pltpu.make_async_copy(pt.at[m, j], rr.at[p], rr_recv.at[0]).start()

    pltpu.make_async_copy(ex_a, ex_a, exa_recv.at[0]).wait()
    rows_a = panel_rows(ex_a)
    send_tiles(0, dot3(rows_a, (p_hi[0], p_lo[0]), NT))
    send_tiles(1, dot3(rows_a, (p_hi[1], p_lo[1]), NT))
    pltpu.make_async_copy(ex_b, ex_b, exb_recv.at[0]).wait()
    rows_b = panel_rows(ex_b)
    send_tiles(2, dot3(rows_b, (p_hi[1], p_lo[1]), NT))

    turn = lax.rem(z - y + NZ, NZ)
    mine = turn // 3

    def make_sums(which):
        @pl.when(which)
        def _():
            pltpu.make_async_copy(rr, rr, rr_recv.at[0]).wait()
            tile[...] = jnp.sum(rr[...], axis=0)
            place = fin.at[core, x, mine, y]
            spot = yz_recv.at[mine]
            pltpu.make_async_copy(tile, place, spot).start()

            def far_first(k):
                return 4 + (k + 1) // 2 * (1 - 2 * lax.rem(k, 2))

            def spread(k, carry):
                to_z, to_y = at_z(far_first(k // NY)), at_y(far_first(lax.rem(k, NY)))
                remote(
                    tile, place, yz_send.at[0], spot, (x * NZ + to_z, to_y * 2 + core)
                ).start()
                return carry

            lax.fori_loop(0, NY * NZ - 1, spread, 0)

    make_sums(jnp.logical_or(turn == 0, turn == 3))
    make_sums(turn == 6)

    def part(origin, which):
        return fin.at[core, origin, which]

    def fx_copy(which, k):
        return remote(
            part(x, which), part(x, which), fx_send.at[which, k], fx_recv.at[which, k],
            (at_x(k) * NZ + z, q),
        )

    def fs_copy(which, k):
        ref = part(at_x(-k), which)
        return remote(ref, ref, fs_send.at[which, k], fs_recv.at[which, k], sibling)

    for which in range(3):
        block = part(x, which)
        pltpu.make_async_copy(block, block, yz_recv.at[which]).wait()
        for k in (2, 1, 3):
            fx_copy(which, k).start()
        fs_copy(which, 0).start()
    for which in range(3):
        for k in (1, 3, 2):
            fx_copy(which, k).wait_recv()
            fs_copy(which, k).start()

    loads[1].wait()
    loads[2].wait()
    for k in range(4):
        fs_copy(0, k).wait_recv()
        fs_copy(1, k).wait_recv()

    def places():
        for co in range(2):
            for xo in range(4):
                xs, h = (1 - co) + 2 * (xo // 2), xo % 2
                yield (
                    slice(xs * 64, xs * 64 + 64), slice(h * 128, h * 128 + 128),
                    fin.at[co, xo],
                )

    for rows, columns, ref in places():
        own_1[rows, columns] = d1[rows, columns] - ref[0].reshape(64, 128)
        cross_out[rows, columns] = ref[1].reshape(64, 128)
    cross = -(cross_out[...].T + dot3(ct_parts, split(own_1[...])))
    cross_out[...] = cross
    last = d2[...] - dot3(split(cross), c_parts)
    for k in range(4):
        fs_copy(2, k).wait_recv()
    for rows, columns, ref in places():
        own_2[rows, columns] = last[rows, columns] - ref[2].reshape(64, 128)

    for copy in ends:
        copy.wait_send()
    for k in range(1, NZ):
        cz_copy(k).wait_send()
    for k in range(1, NX):
        cx_copy(k).wait_send()
        xb_copy(k).wait_send()
        for which in range(3):
            fx_copy(which, k).wait_send()
    for k in range(4):
        for which in range(3):
            fs_copy(which, k).wait_send()
    for parity in (0, 1):
        hand_over(rows_1, ex_a, parity, exa_send, exa_recv).wait_send()
        hand_over(rows_2, ex_b, parity, exb_send, exb_recv).wait_send()
    for m in range(3):
        for j in range(4):
            @pl.when(at_sum(m, j) != p)
            def _():
                tile_copy(m, j).wait_send()

    @pl.when(lax.rem(turn, 3) == 0)
    def _():
        pltpu.make_async_copy(all_sent, all_sent, yz_send.at[0]).wait()


def body(
    inverse_block,
    panel_first,
    panel_second,
    coupling,
    dinv_first,
    dinv_second,
    struct_first,
    struct_second,
):
    dma = pltpu.SemaphoreType.DMA
    any_space = pl.BlockSpec(memory_space=pl.ANY)
    vmem = pl.BlockSpec(memory_space=pltpu.VMEM)
    square = jax.ShapeDtypeStruct((256, 256), F32)
    rows = jax.ShapeDtypeStruct((8, 8, 128), F32)
    row_a, own_a, row_b, cross, own_b = pl.pallas_call(
        kernel,
        out_shape=(rows, square, rows, square, square),
        in_specs=[any_space] * 8,
        out_specs=(vmem,) * 5,
        scratch_shapes=[
            pltpu.SMEM((128,), jnp.int32),
            pltpu.SMEM((128,), jnp.int32),
            pltpu.VMEM((4096, 128), F32),
            pltpu.VMEM((512, 1024), BF16),
            pltpu.VMEM((512, 1024), BF16),
            pltpu.VMEM((2, 4, 256, 128), F32),
            pltpu.VMEM((2, 256, 512), BF16),
            pltpu.VMEM((2, 256, 512), BF16),
            pltpu.VMEM((256, 256), F32),
            pltpu.VMEM((256, 256), F32),
            pltpu.VMEM((256, 256), F32),
            pltpu.VMEM((4, 8, 4, 2, 8, 128), F32),
            pltpu.VMEM((4, 8, 4, 2, 8, 128), F32),
            pltpu.VMEM((8, 4, 2, 8, 128), F32),
            pltpu.VMEM((4, 4, 2, 8, 128), F32),
            pltpu.VMEM((2, 4, 4, 2, 8, 128), F32),
            pltpu.VMEM((2, 2, 4, 4, 2, 8, 128), F32),
            pltpu.VMEM((4, 4, 2, 8, 128), F32),
            pltpu.VMEM((2, 2, 4, 2, 2, 8, 128), F32),
            pltpu.VMEM((2, 4, 4, 4, 2, 8, 128), F32),
            pltpu.VMEM((2, 4, 8, 128), F32),
            pltpu.VMEM((2, 4, 8, 128), F32),
            pltpu.VMEM((2, 4, 8, 128), F32),
            pltpu.VMEM((2, 4, 8, 128), F32),
            pltpu.VMEM((3, 4, 8, 128), F32),
            pltpu.VMEM((32, 8, 128), F32),
            pltpu.VMEM((8, 128), F32),
            pltpu.VMEM((2, 4, 3, 8, 8, 128), F32),
            pltpu.VMEM((63, 8, 128), F32),
            dma((5,)), dma((3,)),
            dma((2, 9)), dma((2, 9)), dma((2, 9)), dma((2, 9)),
            dma((8,)), dma((8,)), dma((4,)), dma((4,)),
            dma((6,)), dma((6,)), dma((4,)), dma((4,)),
            dma((2, 2, 4)), dma((2, 2, 4)), dma((2, 4, 4)), dma((2, 4, 4)),
            dma((2,)), dma((1,)), dma((2,)), dma((1,)),
            dma((3, 4)), dma((1,)), dma((1,)), dma((3,)),
            dma((3, 4)), dma((3, 4)), dma((3, 4)), dma((3, 4)),
        ],
        compiler_params=pltpu.CompilerParams(
            collective_id=0, has_side_effects=True, vmem_limit_bytes=60 * 1024 * 1024
        ),
        name="selected_inversion",
    )(
        inverse_block.reshape(4096, 128),
        panel_first.reshape(4, 16, 128),
        panel_second.reshape(4, 16, 128),
        coupling, dinv_first, dinv_second, struct_first, struct_second,
    )
    return (
        row_a.reshape(8, 1, 8, 128), own_a, row_b.reshape(8, 1, 8, 128), cross, own_b,
    )


def solution(mesh):
    return jax.shard_map(
        body,
        mesh=mesh,
        in_specs=(
            P(None, "prow", None, None, "pcol", None),
            P(None, "prow", "pcol", None),
            P(None, "prow", "pcol", None),
            P("prow", None),
            P(),
            P(),
            P(),
            P(),
        ),
        out_specs=(P(None, "pcol", "prow", None), P(), P(None, "pcol", "prow", None), P(), P()),
        check_vma=False,
    )
```

```python
import jax
import jax.numpy as jnp
from jax import lax
from jax.experimental import pallas as pl
from jax.experimental.pallas import tpu as pltpu
from jax.sharding import PartitionSpec as P

NX, NZ, NY = 4, 8, 8
F32, BF16 = jnp.float32, jnp.bfloat16
MESH = pl.DeviceIdType.MESH

NN = (((1,), (0,)), ((), ()))
NT = (((1,), (1,)), ((), ()))


def split(v):
    hi = v.astype(BF16)
    return hi, (v - hi.astype(F32)).astype(BF16)


def dot3(a, b, dims=NN):
    def one(u, v):
        return lax.dot_general(u, v, dims, preferred_element_type=F32)

    return one(a[0], b[0]) + (one(a[0], b[1]) + one(a[1], b[0]))


def steps_of(way, half):
    return 4 if (way == 0) == (half == 0) else 3


def kernel(
    g_hbm, a_hbm, b_hbm, c_hbm, d1_hbm, d2_hbm, s1_hbm, s2_hbm,
    out_a, own_1, out_b, cross_out, own_2,
    s1, s2, g_raw, g_hi, g_lo, full, p_hi, p_lo, c_full, d1, d2,
    pa, pb, za, sb,
    xa_mid, xa_fin, xb_in, za_in, zb_in,
    rows_1, rows_2, ex_a, ex_b, pt, rr, tile, fin, all_sent,
    load_sem, own_sem,
    sent, ag_recv, sib_recv, cz_recv, cx_recv,
    xa_recv, xb_recv, za_recv, zb_recv,
    exa_recv, exb_recv, rr_send, rr_recv, yz_send, yz_recv,
    fx_recv, fs_recv,
):
    p = lax.axis_index("prow")
    q = lax.axis_index("pcol")
    x, z = p // NZ, lax.rem(p, NZ)
    y, core = q // 2, lax.rem(q, 2)

    def at_x(k):
        return lax.rem(x + k + NX, NX)

    def at_z(k):
        return lax.rem(z + k + NZ, NZ)

    def at_y(k):
        return lax.rem(y + k + NY, NY)

    sibling = (p, y * 2 + 1 - core)

    def remote(src, dst, send, recv, where):
        return pltpu.make_async_remote_copy(
            src_ref=src, dst_ref=dst, send_sem=send, recv_sem=recv,
            device_id=where, device_id_type=MESH,
        )

    barrier = pltpu.get_barrier_semaphore()
    near = [(p, at_y(k) * 2 + core) for k in (1, -1, 2, -2)] + [sibling]
    near += [(x * NZ + at_z(k), q) for k in range(1, NZ)]
    near += [(at_x(k) * NZ + z, q) for k in range(1, NX)]
    for where in near:
        pl.semaphore_signal(barrier, inc=1, device_id=where, device_id_type=MESH)

    def all_of(ref, semaphore):
        pltpu.make_async_copy(ref, ref, semaphore).wait()

    rows16 = pl.ds(pl.multiple_of(q * 16, 16), 16)
    rows8 = pl.ds(pl.multiple_of(p * 8, 8), 8)
    own = [
        pltpu.make_async_copy(a_hbm, full.at[0, :, rows16], own_sem.at[0]),
        pltpu.make_async_copy(b_hbm, full.at[1, :, rows16], own_sem.at[1]),
        pltpu.make_async_copy(c_hbm, c_full.at[rows8], own_sem.at[2]),
    ]
    loads = [
        pltpu.make_async_copy(g_hbm, g_raw, load_sem.at[0]),
        pltpu.make_async_copy(d1_hbm, d1, load_sem.at[1]),
        pltpu.make_async_copy(d2_hbm, d2, load_sem.at[2]),
        pltpu.make_async_copy(s1_hbm, s1, load_sem.at[3]),
        pltpu.make_async_copy(s2_hbm, s2, load_sem.at[4]),
    ]
    for copy in own + loads:
        copy.start()

    pl.semaphore_wait(barrier, len(near))

    def shard(k, row_y):
        rows = row_y * 2 + core
        return full.at[k, :, pl.ds(pl.multiple_of(rows * 16, 16), 16)]

    def ring(k, of, to):
        ref = shard(k, at_y(of))
        return remote(
            ref, ref, sent.at[0], ag_recv.at[k, of - to + 4],
            (p, at_y(to) * 2 + core),
        )

    def push(k, of, to):
        copy = ring(k, of, to)
        copy.start()

    def across(k, of):
        ref = shard(k, at_y(of))
        copy = remote(ref, ref, sent.at[0], sib_recv.at[k], sibling)
        copy.start()

    def got(k, of):
        ring(k, of, 0).wait_recv()
        across(k, of)

    own[0].wait()
    for to in (2, -2, 1, -1):
        push(0, 0, to)
    across(0, 0)
    own[1].wait()
    for to in (2, -2):
        push(1, 0, to)
    own[2].wait()

    def cz_copy(k):
        return remote(
            c_full.at[rows8], c_full.at[rows8], sent.at[0], cz_recv.at[0],
            (x * NZ + at_z(k), q),
        )

    for k in range(1, NZ):
        cz_copy(k).start()

    for index in (0, 3, 4):
        loads[index].wait()

    def split_g(c, carry):
        hi, lo = split(g_raw[pl.ds(c, 512, stride=8), :])
        columns = pl.ds(pl.multiple_of(c * 128, 128), 128)
        g_hi[:, columns] = hi
        g_lo[:, columns] = lo
        return carry

    lax.fori_loop(0, 8, split_g, 0)

    def forward(k, of):
        ring(k, of, 0).wait_recv()
        way = 1 if of < 0 else -1
        push(k, of, way)
        if (of < 0) == (k == 0):
            push(k, of, 2 * way)
        across(k, of)

    forward(0, -2)
    forward(0, 2)
    for to in (1, -1):
        push(1, 0, to)
    across(1, 0)
    got(0, -1)
    got(0, 1)
    forward(1, -2)
    forward(1, 2)
    all_of(c_full.at[0:56], cz_recv.at[0])
    rows64 = pl.ds(pl.multiple_of(x * 64, 64), 64)

    def cx_copy(k):
        return remote(
            c_full.at[rows64], c_full.at[rows64], sent.at[0], cx_recv.at[0],
            (at_x(k) * NZ + z, q),
        )

    for k in range(1, NX):
        cx_copy(k).start()
    got(0, -3)
    got(0, 3)
    got(0, -4)

    def prepare(k, struct):
        all_of(full.at[k, :, 0:128], sib_recv.at[k])
        for r in range(4):
            mask = struct[r * (NX * NZ) + p].astype(F32)
            hi, lo = split(full[k, r] * mask)
            p_hi[k, :, r * 128:(r + 1) * 128] = hi
            p_lo[k, :, r * 128:(r + 1) * 128] = lo

    def col_mask(struct, c):
        return struct[c * (NY * 2) + q].astype(F32)

    prepare(0, s1)

    def mul_a(t, carry):
        columns = pl.ds(pl.multiple_of(t * 256, 256), 256)
        r = dot3((p_hi[0], p_lo[0]), (g_hi[:, columns], g_lo[:, columns]))
        pa[:, :, t, 0] = r[:, :128].reshape(NX, NZ, 8, 128)
        pa[:, :, t, 1] = r[:, 128:].reshape(NX, NZ, 8, 128)
        return carry

    lax.fori_loop(0, 4, mul_a, 0)

    x_right, x_left = (at_x(1) * NZ + z, q), (at_x(-1) * NZ + z, q)

    def xa_piece(d, half):
        return pa.at[d, half * 4:(half + 1) * 4]

    def xa_copy(index, d, half, into, where):
        return remote(xa_piece(d, half), into, sent.at[1], xa_recv.at[min(index, 2)], where)

    xa = {
        "far0": xa_copy(0, at_x(2), 0, xa_mid.at[0], x_right),
        "far1": xa_copy(1, at_x(2), 1, xa_mid.at[1], x_left),
        "near1": xa_copy(2, at_x(1), 1, xa_fin.at[0, 1], x_right),
        "near0": xa_copy(3, at_x(3), 0, xa_fin.at[1, 0], x_left),
        "sum0": xa_copy(4, at_x(1), 0, xa_fin.at[0, 0], x_right),
        "sum1": xa_copy(5, at_x(3), 1, xa_fin.at[1, 1], x_left),
    }
    for name in ("far0", "far1", "near1", "near0"):
        xa[name].start()

    for of in (-1, 1, -3, 3, 4):
        got(1, of)
    all_of(c_full.at[0:192], cx_recv.at[0])
    coupling = c_full[...]
    c_parts = split(coupling)
    ct_parts = split(coupling.T)

    def mul_c(t, carry):
        first = jnp.concatenate(
            [pa[:, :, t, h].reshape(256, 128) * col_mask(s1, 2 * t + h) for h in (0, 1)], axis=1
        )
        r = dot3(ct_parts, split(first))
        pb[:, :, t, 0] = r[:, :128].reshape(NX, NZ, 8, 128)
        pb[:, :, t, 1] = r[:, 128:].reshape(NX, NZ, 8, 128)
        return carry

    lax.fori_loop(0, 4, mul_c, 0)
    prepare(1, s2)

    def mul_b(t, carry):
        columns = pl.ds(pl.multiple_of(t * 256, 256), 256)
        r = dot3((p_hi[1], p_lo[1]), (g_hi[:, columns], g_lo[:, columns]))
        for h in (0, 1):
            block = r[:, h * 128:(h + 1) * 128].reshape(NX, NZ, 8, 128)
            pb[:, :, t, h] = block - pb[:, :, t, h]
        return carry

    lax.fori_loop(0, 4, mul_b, 0)

    def zb_copy(way, j, step):
        away = steps_of(way, j // 2) - step + 1
        d = at_z(away) if way == 0 else at_z(-away)
        to_z = at_z(1) if way == 0 else at_z(-1)
        return d, remote(
            pb.at[j, d], zb_in.at[way, j, step - 1],
            sent.at[1], zb_recv.at[way, j, step - 1],
            (x * NZ + to_z, q),
        )

    def zb_step(step):
        for j in range(4):
            for way in (0, 1):
                if step > steps_of(way, j // 2):
                    continue
                d, copy = zb_copy(way, j, step)
                if step > 1:
                    zb_copy(way, j, step - 1)[1].wait_recv()
                    pb[j, d] += zb_in[way, j, step - 2]
                copy.start()

    zb_step(1)
    xa["far0"].wait_recv()
    pa[at_x(1), 0:4] += xa_mid[0]
    xa["sum0"].start()
    xa["far1"].wait_recv()
    pa[at_x(3), 4:8] += xa_mid[1]
    xa["sum1"].start()
    zb_step(2)
    zb_step(3)
    all_of(xa_fin, xa_recv.at[2])
    for half in (0, 1):
        rows = slice(half * 4, half * 4 + 4)
        za[rows] = pa[x, rows] + xa_fin[0, half] + xa_fin[1, half]

    def xb_copy(k):
        return remote(
            sb.at[at_x(k)], xb_in.at[k], sent.at[1], xb_recv.at[0], (at_x(k) * NZ + z, q)
        )

    def za_copy(way, half, step):
        away = steps_of(way, half) - step + 1
        d = at_z(away) if way == 0 else at_z(-away)
        to_z = at_z(1) if way == 0 else at_z(-1)
        return d, remote(
            za.at[d, half * 2:(half + 1) * 2], za_in.at[way, half, step - 1],
            sent.at[1], za_recv.at[way, half, step - 1],
            (x * NZ + to_z, q),
        )

    def za_step(step):
        for half in (0, 1):
            for way in (0, 1):
                if step > steps_of(way, half):
                    continue
                d, copy = za_copy(way, half, step)
                if step > 1:
                    za_copy(way, half, step - 1)[1].wait_recv()
                    za[d, half * 2:(half + 1) * 2] += za_in[way, half, step - 2]
                copy.start()

    to_col = 2 * z + 1 - lax.rem(x, 2)

    def hand_over(rows, into, parity, recv):
        return remote(
            rows.at[parity], into.at[x // 2], sent.at[1], recv.at[0],
            (q + 16 * parity, to_col),
        )

    za_step(1)
    zb_step(4)
    za_step(2)
    za_step(3)
    for j in range(4):
        last = [steps_of(way, j // 2) for way in (0, 1)]
        for way in (0, 1):
            zb_copy(way, j, last[way])[1].wait_recv()
        sb[j] = pb[j, z] + zb_in[0, j, last[0] - 1] + zb_in[1, j, last[1] - 1]
    for k in (2, 1, 3):
        xb_copy(k).start()

    za_step(4)

    def deliver(value, c, struct, out, rows):
        block = value * (-col_mask(struct, c))
        out[c] = block
        rows[c % 2, c // 2] = block

    all_of(xb_in.at[1:4], xb_recv.at[0])
    value = sb[x] + xb_in[1] + xb_in[2] + xb_in[3]
    for c in range(8):
        deliver(value[c // 2, c % 2], c, s2, out_b, rows_2)
    for parity in (0, 1):
        hand_over(rows_2, ex_b, parity, exb_recv).start()
    for half in (0, 1):
        last = [steps_of(way, half) for way in (0, 1)]
        for way in (0, 1):
            za_copy(way, half, last[way])[1].wait_recv()
        value = za[z, half * 2:(half + 1) * 2]
        value = value + za_in[0, half, last[0] - 1] + za_in[1, half, last[1] - 1]
        for c in range(4 * half, 4 * half + 4):
            deliver(value[c // 2 - 2 * half, c % 2], c, s1, out_a, rows_1)
    for parity in (0, 1):
        hand_over(rows_1, ex_a, parity, exa_recv).start()

    def at_sum(m, j):
        return j * NZ + lax.rem(y + 3 * m, NZ)

    def tile_copy(m, j):
        return remote(
            pt.at[m, j], rr.at[p], rr_send.at[0], rr_recv.at[0], (at_sum(m, j), q)
        )

    def panel_rows(ref):
        return split(jnp.concatenate([ref[:, r].reshape(16, 128) for r in range(4)], axis=1))

    def send_tiles(m, value):
        for s in range(2):
            for h in range(2):
                pt[m, s * 2 + h] = value[s * 8:(s + 1) * 8, h * 128:(h + 1) * 128]
        for j in range(4):
            @pl.when(at_sum(m, j) != p)
            def _():
                tile_copy(m, j).start()

            @pl.when(at_sum(m, j) == p)
            def _():
                pltpu.make_async_copy(pt.at[m, j], rr.at[p], rr_recv.at[0]).start()

    pltpu.make_async_copy(ex_a, ex_a, exa_recv.at[0]).wait()
    rows_a = panel_rows(ex_a)
    send_tiles(0, dot3(rows_a, (p_hi[0], p_lo[0]), NT))
    send_tiles(1, dot3(rows_a, (p_hi[1], p_lo[1]), NT))
    pltpu.make_async_copy(ex_b, ex_b, exb_recv.at[0]).wait()
    rows_b = panel_rows(ex_b)
    send_tiles(2, dot3(rows_b, (p_hi[1], p_lo[1]), NT))

    turn = lax.rem(z - y + NZ, NZ)
    mine = turn // 3

    def make_sums(which):
        @pl.when(which)
        def _():
            pltpu.make_async_copy(rr, rr, rr_recv.at[0]).wait()
            tile[...] = jnp.sum(rr[...], axis=0)
            place = fin.at[core, x, mine, y]
            spot = yz_recv.at[mine]
            pltpu.make_async_copy(tile, place, spot).start()

            def far_first(k):
                return 4 + (k + 1) // 2 * (1 - 2 * lax.rem(k, 2))

            def spread(k, carry):
                to_z, to_y = at_z(far_first(k // NY)), at_y(far_first(lax.rem(k, NY)))
                remote(
                    tile, place, yz_send.at[0], spot, (x * NZ + to_z, to_y * 2 + core)
                ).start()
                return carry

            lax.fori_loop(0, NY * NZ - 1, spread, 0)

    make_sums(jnp.logical_or(turn == 0, turn == 3))
    make_sums(turn == 6)

    def part(origin, which):
        return fin.at[core, origin, which]

    def fx_copy(which, k):
        return remote(
            part(x, which), part(x, which), sent.at[2], fx_recv.at[which, k],
            (at_x(k) * NZ + z, q),
        )

    def fs_copy(which, k):
        ref = part(at_x(-k), which)
        return remote(ref, ref, sent.at[2], fs_recv.at[which], sibling)

    for which in range(3):
        block = part(x, which)
        pltpu.make_async_copy(block, block, yz_recv.at[which]).wait()
        for k in (2, 1, 3):
            fx_copy(which, k).start()
        fs_copy(which, 0).start()
    for which in range(3):
        for k in (1, 3, 2):
            fx_copy(which, k).wait_recv()
            fs_copy(which, k).start()

    loads[1].wait()
    loads[2].wait()
    for which in (0, 1):
        all_of(fin.at[1 - core, :, which], fs_recv.at[which])

    def places():
        for co in range(2):
            for xo in range(4):
                xs, h = (1 - co) + 2 * (xo // 2), xo % 2
                yield (
                    slice(xs * 64, xs * 64 + 64), slice(h * 128, h * 128 + 128),
                    fin.at[co, xo],
                )

    for rows, columns, ref in places():
        own_1[rows, columns] = d1[rows, columns] - ref[0].reshape(64, 128)
        cross_out[rows, columns] = ref[1].reshape(64, 128)
    cross = -(cross_out[...].T + dot3(ct_parts, split(own_1[...])))
    cross_out[...] = cross
    last = d2[...] - dot3(split(cross), c_parts)
    all_of(fin.at[1 - core, :, 2], fs_recv.at[2])
    for rows, columns, ref in places():
        own_2[rows, columns] = last[rows, columns] - ref[2].reshape(64, 128)

    all_of(all_sent.at[0:302], sent.at[0])
    all_of(all_sent, sent.at[1])
    all_of(all_sent.at[0:168], sent.at[2])

    @pl.when(lax.rem(turn, 3) == 0)
    def _():
        all_of(all_sent.at[0:11], rr_send.at[0])
        all_of(all_sent.at[0:63], yz_send.at[0])

    @pl.when(lax.rem(turn, 3) != 0)
    def _():
        all_of(all_sent.at[0:12], rr_send.at[0])


def body(
    inverse_block,
    panel_first,
    panel_second,
    coupling,
    dinv_first,
    dinv_second,
    struct_first,
    struct_second,
):
    dma = pltpu.SemaphoreType.DMA
    any_space = pl.BlockSpec(memory_space=pl.ANY)
    vmem = pl.BlockSpec(memory_space=pltpu.VMEM)
    square = jax.ShapeDtypeStruct((256, 256), F32)
    rows = jax.ShapeDtypeStruct((8, 8, 128), F32)
    row_a, own_a, row_b, cross, own_b = pl.pallas_call(
        kernel,
        out_shape=(rows, square, rows, square, square),
        in_specs=[any_space] * 8,
        out_specs=(vmem,) * 5,
        scratch_shapes=[
            pltpu.SMEM((128,), jnp.int32),
            pltpu.SMEM((128,), jnp.int32),
            pltpu.VMEM((4096, 128), F32),
            pltpu.VMEM((512, 1024), BF16),
            pltpu.VMEM((512, 1024), BF16),
            pltpu.VMEM((2, 4, 256, 128), F32),
            pltpu.VMEM((2, 256, 512), BF16),
            pltpu.VMEM((2, 256, 512), BF16),
            pltpu.VMEM((256, 256), F32),
            pltpu.VMEM((256, 256), F32),
            pltpu.VMEM((256, 256), F32),
            pltpu.VMEM((4, 8, 4, 2, 8, 128), F32),
            pltpu.VMEM((4, 8, 4, 2, 8, 128), F32),
            pltpu.VMEM((8, 4, 2, 8, 128), F32),
            pltpu.VMEM((4, 4, 2, 8, 128), F32),
            pltpu.VMEM((2, 4, 4, 2, 8, 128), F32),
            pltpu.VMEM((2, 2, 4, 4, 2, 8, 128), F32),
            pltpu.VMEM((4, 4, 2, 8, 128), F32),
            pltpu.VMEM((2, 2, 4, 2, 2, 8, 128), F32),
            pltpu.VMEM((2, 4, 4, 4, 2, 8, 128), F32),
            pltpu.VMEM((2, 4, 8, 128), F32),
            pltpu.VMEM((2, 4, 8, 128), F32),
            pltpu.VMEM((2, 4, 8, 128), F32),
            pltpu.VMEM((2, 4, 8, 128), F32),
            pltpu.VMEM((3, 4, 8, 128), F32),
            pltpu.VMEM((32, 8, 128), F32),
            pltpu.VMEM((8, 128), F32),
            pltpu.VMEM((2, 4, 3, 8, 8, 128), F32),
            pltpu.VMEM((512, 8, 128), F32),
            dma((5,)), dma((3,)),
            dma((3,)), dma((2, 9)), dma((2,)), dma((1,)), dma((1,)),
            dma((3,)), dma((1,)), dma((2, 2, 4)), dma((2, 4, 4)),
            dma((1,)), dma((1,)), dma((1,)), dma((1,)), dma((1,)), dma((3,)),
            dma((3, 4)), dma((3,)),
        ],
        compiler_params=pltpu.CompilerParams(
            collective_id=0, has_side_effects=True, vmem_limit_bytes=60 * 1024 * 1024
        ),
        name="selected_inversion",
    )(
        inverse_block.reshape(4096, 128),
        panel_first.reshape(4, 16, 128),
        panel_second.reshape(4, 16, 128),
        coupling, dinv_first, dinv_second, struct_first, struct_second,
    )
    return (
        row_a.reshape(8, 1, 8, 128), own_a, row_b.reshape(8, 1, 8, 128), cross, own_b,
    )


def solution(mesh):
    return jax.shard_map(
        body,
        mesh=mesh,
        in_specs=(
            P(None, "prow", None, None, "pcol", None),
            P(None, "prow", "pcol", None),
            P(None, "prow", "pcol", None),
            P("prow", None),
            P(),
            P(),
            P(),
            P(),
        ),
        out_specs=(P(None, "pcol", "prow", None), P(), P(None, "pcol", "prow", None), P(), P()),
        check_vma=False,
    )
```

```python
import jax
import jax.numpy as jnp
from jax import lax
from jax.experimental import pallas as pl
from jax.experimental.pallas import tpu as pltpu
from jax.sharding import PartitionSpec as P

NX, NZ, NY = 4, 8, 8
F32, BF16 = jnp.float32, jnp.bfloat16
MESH = pl.DeviceIdType.MESH

NN = (((1,), (0,)), ((), ()))
NT = (((1,), (1,)), ((), ()))


def split(v):
    hi = v.astype(BF16)
    return hi, (v - hi.astype(F32)).astype(BF16)


def dot3(a, b, dims=NN):
    def one(u, v):
        return lax.dot_general(u, v, dims, preferred_element_type=F32)

    return one(a[0], b[0]) + (one(a[0], b[1]) + one(a[1], b[0]))


def steps_of(way, half):
    return 4 if (way == 0) == (half == 0) else 3


def kernel(
    g_hbm, a_hbm, b_hbm, c_hbm, d1_hbm, d2_hbm, s1_hbm, s2_hbm,
    out_a, own_1, out_b, cross_out, own_2,
    s1, s2, g_raw, g_hi, g_lo, full, p_hi, p_lo, c_full, d1, d2,
    pa, pb, za, sb,
    xa_mid, xa_fin, xb_in, za_in, zb_in,
    rows_1, rows_2, ex_a, ex_b, pt, rr, tile, fin, all_sent,
    load_sem, own_sem,
    sent, ag_recv, sib_recv, cz_recv, cx_recv,
    xa_recv, xb_recv, za_recv, zb_recv,
    exa_recv, exb_recv, rr_send, rr_recv, yz_send, yz_recv,
    fx_recv, fs_recv,
):
    p = lax.axis_index("prow")
    q = lax.axis_index("pcol")
    x, z = p // NZ, lax.rem(p, NZ)
    y, core = q // 2, lax.rem(q, 2)

    def at_x(k):
        return lax.rem(x + k + NX, NX)

    def at_z(k):
        return lax.rem(z + k + NZ, NZ)

    def at_y(k):
        return lax.rem(y + k + NY, NY)

    sibling = (p, y * 2 + 1 - core)

    def remote(src, dst, send, recv, where):
        return pltpu.make_async_remote_copy(
            src_ref=src, dst_ref=dst, send_sem=send, recv_sem=recv,
            device_id=where, device_id_type=MESH,
        )

    barrier = pltpu.get_barrier_semaphore()
    near = [(p, at_y(k) * 2 + core) for k in (1, -1, 2, -2)] + [sibling]
    near += [(x * NZ + at_z(k), q) for k in range(1, NZ)]
    near += [(at_x(k) * NZ + z, q) for k in range(1, NX)]
    for where in near:
        pl.semaphore_signal(barrier, inc=1, device_id=where, device_id_type=MESH)

    def all_of(ref, semaphore):
        pltpu.make_async_copy(ref, ref, semaphore).wait()

    rows16 = pl.ds(pl.multiple_of(q * 16, 16), 16)
    rows8 = pl.ds(pl.multiple_of(p * 8, 8), 8)
    own = [
        pltpu.make_async_copy(a_hbm, full.at[0, :, rows16], own_sem.at[0]),
        pltpu.make_async_copy(b_hbm, full.at[1, :, rows16], own_sem.at[1]),
        pltpu.make_async_copy(c_hbm, c_full.at[rows8], own_sem.at[2]),
    ]
    loads = [
        pltpu.make_async_copy(g_hbm, g_raw, load_sem.at[0]),
        pltpu.make_async_copy(d1_hbm, d1, load_sem.at[1]),
        pltpu.make_async_copy(d2_hbm, d2, load_sem.at[2]),
        pltpu.make_async_copy(s1_hbm, s1, load_sem.at[3]),
        pltpu.make_async_copy(s2_hbm, s2, load_sem.at[4]),
    ]
    for copy in own + loads:
        copy.start()

    pl.semaphore_wait(barrier, len(near))

    def shard(k, row_y):
        rows = row_y * 2 + core
        return full.at[k, :, pl.ds(pl.multiple_of(rows * 16, 16), 16)]

    def ring(k, of, to):
        ref = shard(k, at_y(of))
        return remote(
            ref, ref, sent.at[0], ag_recv.at[k, of - to + 4],
            (p, at_y(to) * 2 + core),
        )

    def push(k, of, to):
        copy = ring(k, of, to)
        copy.start()

    def across(k, of):
        ref = shard(k, at_y(of))
        copy = remote(ref, ref, sent.at[0], sib_recv.at[k], sibling)
        copy.start()

    def got(k, of):
        ring(k, of, 0).wait_recv()
        across(k, of)

    own[0].wait()
    for to in (2, -2, 1, -1):
        push(0, 0, to)
    across(0, 0)
    own[1].wait()
    for to in (2, -2):
        push(1, 0, to)
    own[2].wait()

    def cz_copy(k):
        return remote(
            c_full.at[rows8], c_full.at[rows8], sent.at[0], cz_recv.at[0],
            (x * NZ + at_z(k), q),
        )

    for k in range(1, NZ):
        cz_copy(k).start()

    for index in (0, 3, 4):
        loads[index].wait()

    def split_g(c, carry):
        hi, lo = split(g_raw[pl.ds(c, 512, stride=8), :])
        columns = pl.ds(pl.multiple_of(c * 128, 128), 128)
        g_hi[:, columns] = hi
        g_lo[:, columns] = lo
        return carry

    lax.fori_loop(0, 8, split_g, 0)

    def forward(k, of):
        ring(k, of, 0).wait_recv()
        way = 1 if of < 0 else -1
        push(k, of, way)
        if (of < 0) == (k == 0):
            push(k, of, 2 * way)
        across(k, of)

    forward(0, -2)
    forward(0, 2)
    for to in (1, -1):
        push(1, 0, to)
    across(1, 0)
    got(0, -1)
    got(0, 1)
    forward(1, -2)
    forward(1, 2)
    all_of(c_full.at[0:56], cz_recv.at[0])
    rows64 = pl.ds(pl.multiple_of(x * 64, 64), 64)

    def cx_copy(k):
        return remote(
            c_full.at[rows64], c_full.at[rows64], sent.at[0], cx_recv.at[0],
            (at_x(k) * NZ + z, q),
        )

    for k in range(1, NX):
        cx_copy(k).start()
    got(0, -3)
    got(0, 3)
    got(0, -4)

    def prepare(k, struct):
        all_of(full.at[k, :, 0:128], sib_recv.at[k])
        for r in range(4):
            mask = struct[r * (NX * NZ) + p].astype(F32)
            hi, lo = split(full[k, r] * mask)
            p_hi[k, :, r * 128:(r + 1) * 128] = hi
            p_lo[k, :, r * 128:(r + 1) * 128] = lo

    def col_mask(struct, c):
        return struct[c * (NY * 2) + q].astype(F32)

    prepare(0, s1)

    def mul_a(t, carry):
        columns = pl.ds(pl.multiple_of(t * 256, 256), 256)
        r = dot3((p_hi[0], p_lo[0]), (g_hi[:, columns], g_lo[:, columns]))
        pa[:, :, t, 0] = r[:, :128].reshape(NX, NZ, 8, 128)
        pa[:, :, t, 1] = r[:, 128:].reshape(NX, NZ, 8, 128)
        return carry

    lax.fori_loop(0, 4, mul_a, 0)

    x_right, x_left = (at_x(1) * NZ + z, q), (at_x(-1) * NZ + z, q)

    def xa_piece(d, half):
        return pa.at[d, half * 4:(half + 1) * 4]

    def xa_copy(index, d, half, into, where):
        return remote(xa_piece(d, half), into, sent.at[1], xa_recv.at[min(index, 2)], where)

    xa = {
        "far0": xa_copy(0, at_x(2), 0, xa_mid.at[0], x_right),
        "far1": xa_copy(1, at_x(2), 1, xa_mid.at[1], x_left),
        "near1": xa_copy(2, at_x(1), 1, xa_fin.at[0, 1], x_right),
        "near0": xa_copy(3, at_x(3), 0, xa_fin.at[1, 0], x_left),
        "sum0": xa_copy(4, at_x(1), 0, xa_fin.at[0, 0], x_right),
        "sum1": xa_copy(5, at_x(3), 1, xa_fin.at[1, 1], x_left),
    }
    for name in ("far0", "far1", "near1", "near0"):
        xa[name].start()

    for of in (-1, 1, -3, 3, 4):
        got(1, of)
    all_of(c_full.at[0:192], cx_recv.at[0])
    coupling = c_full[...]
    c_parts = split(coupling)
    ct_parts = split(coupling.T)

    def mul_c(t, carry):
        first = jnp.concatenate(
            [pa[:, :, t, h].reshape(256, 128) * col_mask(s1, 2 * t + h) for h in (0, 1)], axis=1
        )
        r = dot3(ct_parts, split(first))
        pb[:, :, t, 0] = r[:, :128].reshape(NX, NZ, 8, 128)
        pb[:, :, t, 1] = r[:, 128:].reshape(NX, NZ, 8, 128)
        return carry

    lax.fori_loop(0, 4, mul_c, 0)
    prepare(1, s2)

    def mul_b(t, carry):
        columns = pl.ds(pl.multiple_of(t * 256, 256), 256)
        r = dot3((p_hi[1], p_lo[1]), (g_hi[:, columns], g_lo[:, columns]))
        for h in (0, 1):
            block = r[:, h * 128:(h + 1) * 128].reshape(NX, NZ, 8, 128)
            pb[:, :, t, h] = block - pb[:, :, t, h]
        return carry

    lax.fori_loop(0, 4, mul_b, 0)

    def zb_copy(way, j, step):
        away = steps_of(way, j // 2) - step + 1
        d = at_z(away) if way == 0 else at_z(-away)
        to_z = at_z(1) if way == 0 else at_z(-1)
        return d, remote(
            pb.at[j, d], zb_in.at[way, j, step - 1],
            sent.at[1], zb_recv.at[way, j, step - 1],
            (x * NZ + to_z, q),
        )

    def zb_step(step):
        for j in range(4):
            for way in (0, 1):
                if step > steps_of(way, j // 2):
                    continue
                d, copy = zb_copy(way, j, step)
                if step > 1:
                    zb_copy(way, j, step - 1)[1].wait_recv()
                    pb[j, d] += zb_in[way, j, step - 2]
                copy.start()

    zb_step(1)
    xa["far0"].wait_recv()
    pa[at_x(1), 0:4] += xa_mid[0]
    xa["sum0"].start()
    xa["far1"].wait_recv()
    pa[at_x(3), 4:8] += xa_mid[1]
    xa["sum1"].start()
    zb_step(2)
    zb_step(3)
    all_of(xa_fin, xa_recv.at[2])
    for half in (0, 1):
        rows = slice(half * 4, half * 4 + 4)
        za[rows] = pa[x, rows] + xa_fin[0, half] + xa_fin[1, half]

    def xb_copy(k):
        return remote(
            sb.at[at_x(k)], xb_in.at[k], sent.at[1], xb_recv.at[0], (at_x(k) * NZ + z, q)
        )

    def za_copy(way, half, index):
        away, over = ((4, 2), (3, 2), (2, 2), (1, 1))[index]
        sign = 1 - 2 * way
        return remote(
            za.at[at_z(sign * away), half * 2:(half + 1) * 2], za_in.at[way, half, index],
            sent.at[1], za_recv.at[way, half, index], (x * NZ + at_z(sign * over), q),
        )

    sides = [(way, half) for half in (0, 1) for way in (0, 1)]

    def za_start():
        for way, half in sides:
            if steps_of(way, half) == 4:
                za_copy(way, half, 0).start()
            za_copy(way, half, 1).start()
        for way, half in sides:
            if steps_of(way, half) == 3:
                za_copy(way, half, 2).start()

    def za_middle():
        for way, half in sides:
            for index in (0, 1):
                if index == 0 and steps_of(way, half) == 3:
                    continue
                za_copy(way, half, index).wait_recv()
                d = at_z((2 - index) * (1 - 2 * way))
                za[d, half * 2:(half + 1) * 2] += za_in[way, half, index]
                za_copy(way, half, index + 2).start()

    to_col = 2 * z + 1 - lax.rem(x, 2)

    def hand_over(rows, into, parity, recv):
        return remote(
            rows.at[parity], into.at[x // 2], sent.at[1], recv.at[0],
            (q + 16 * parity, to_col),
        )

    za_start()
    zb_step(4)
    za_middle()
    for j in range(4):
        last = [steps_of(way, j // 2) for way in (0, 1)]
        for way in (0, 1):
            zb_copy(way, j, last[way])[1].wait_recv()
        sb[j] = pb[j, z] + zb_in[0, j, last[0] - 1] + zb_in[1, j, last[1] - 1]
    for k in (2, 1, 3):
        xb_copy(k).start()


    def deliver(value, c, struct, out, rows):
        block = value * (-col_mask(struct, c))
        out[c] = block
        rows[c % 2, c // 2] = block

    for half in (0, 1):
        value = za[z, half * 2:(half + 1) * 2]
        for way in (0, 1):
            for index in (2, 3):
                za_copy(way, half, index).wait_recv()
                value = value + za_in[way, half, index]
        for c in range(4 * half, 4 * half + 4):
            deliver(value[c // 2 - 2 * half, c % 2], c, s1, out_a, rows_1)
    for parity in (0, 1):
        hand_over(rows_1, ex_a, parity, exa_recv).start()
    all_of(xb_in.at[1:4], xb_recv.at[0])
    value = sb[x] + xb_in[1] + xb_in[2] + xb_in[3]
    for c in range(8):
        deliver(value[c // 2, c % 2], c, s2, out_b, rows_2)
    for parity in (0, 1):
        hand_over(rows_2, ex_b, parity, exb_recv).start()

    def at_sum(m, j):
        return j * NZ + lax.rem(y + 3 * m, NZ)

    def tile_copy(m, j):
        return remote(
            pt.at[m, j], rr.at[p], rr_send.at[0], rr_recv.at[0], (at_sum(m, j), q)
        )

    def panel_rows(ref):
        return split(jnp.concatenate([ref[:, r].reshape(16, 128) for r in range(4)], axis=1))

    def send_tiles(m, value):
        for s in range(2):
            for h in range(2):
                pt[m, s * 2 + h] = value[s * 8:(s + 1) * 8, h * 128:(h + 1) * 128]
        for j in range(4):
            @pl.when(at_sum(m, j) != p)
            def _():
                tile_copy(m, j).start()

            @pl.when(at_sum(m, j) == p)
            def _():
                pltpu.make_async_copy(pt.at[m, j], rr.at[p], rr_recv.at[0]).start()

    pltpu.make_async_copy(ex_a, ex_a, exa_recv.at[0]).wait()
    rows_a = panel_rows(ex_a)
    send_tiles(0, dot3(rows_a, (p_hi[0], p_lo[0]), NT))
    send_tiles(1, dot3(rows_a, (p_hi[1], p_lo[1]), NT))
    pltpu.make_async_copy(ex_b, ex_b, exb_recv.at[0]).wait()
    rows_b = panel_rows(ex_b)
    send_tiles(2, dot3(rows_b, (p_hi[1], p_lo[1]), NT))

    turn = lax.rem(z - y + NZ, NZ)
    mine = turn // 3

    def make_sums(which):
        @pl.when(which)
        def _():
            pltpu.make_async_copy(rr, rr, rr_recv.at[0]).wait()
            tile[...] = jnp.sum(rr[...], axis=0)
            place = fin.at[core, x, mine, y]
            spot = yz_recv.at[mine]
            pltpu.make_async_copy(tile, place, spot).start()

            def far_first(k):
                return 4 + (k + 1) // 2 * (1 - 2 * lax.rem(k, 2))

            def spread(k, carry):
                to_z, to_y = at_z(far_first(k // NY)), at_y(far_first(lax.rem(k, NY)))
                remote(
                    tile, place, yz_send.at[0], spot, (x * NZ + to_z, to_y * 2 + core)
                ).start()
                return carry

            lax.fori_loop(0, NY * NZ - 1, spread, 0)

    make_sums(jnp.logical_or(turn == 0, turn == 3))
    make_sums(turn == 6)

    def part(origin, which):
        return fin.at[core, origin, which]

    def fx_copy(which, k):
        return remote(
            part(x, which), part(x, which), sent.at[2], fx_recv.at[which, k],
            (at_x(k) * NZ + z, q),
        )

    def fs_copy(which, k):
        ref = part(at_x(-k), which)
        return remote(ref, ref, sent.at[2], fs_recv.at[which], sibling)

    for which in range(3):
        block = part(x, which)
        pltpu.make_async_copy(block, block, yz_recv.at[which]).wait()
        for k in (2, 1, 3):
            fx_copy(which, k).start()
        fs_copy(which, 0).start()
    for which in range(3):
        for k in (1, 3, 2):
            fx_copy(which, k).wait_recv()
            fs_copy(which, k).start()

    loads[1].wait()
    loads[2].wait()
    for which in (0, 1):
        all_of(fin.at[1 - core, :, which], fs_recv.at[which])

    def places():
        for co in range(2):
            for xo in range(4):
                xs, h = (1 - co) + 2 * (xo // 2), xo % 2
                yield (
                    slice(xs * 64, xs * 64 + 64), slice(h * 128, h * 128 + 128),
                    fin.at[co, xo],
                )

    for rows, columns, ref in places():
        own_1[rows, columns] = d1[rows, columns] - ref[0].reshape(64, 128)
        cross_out[rows, columns] = ref[1].reshape(64, 128)
    cross = -(cross_out[...].T + dot3(ct_parts, split(own_1[...])))
    cross_out[...] = cross
    last = d2[...] - dot3(split(cross), c_parts)
    all_of(fin.at[1 - core, :, 2], fs_recv.at[2])
    for rows, columns, ref in places():
        own_2[rows, columns] = last[rows, columns] - ref[2].reshape(64, 128)

    all_of(all_sent.at[0:302], sent.at[0])
    all_of(all_sent, sent.at[1])
    all_of(all_sent.at[0:168], sent.at[2])

    @pl.when(lax.rem(turn, 3) == 0)
    def _():
        all_of(all_sent.at[0:11], rr_send.at[0])
        all_of(all_sent.at[0:63], yz_send.at[0])

    @pl.when(lax.rem(turn, 3) != 0)
    def _():
        all_of(all_sent.at[0:12], rr_send.at[0])


def body(
    inverse_block,
    panel_first,
    panel_second,
    coupling,
    dinv_first,
    dinv_second,
    struct_first,
    struct_second,
):
    dma = pltpu.SemaphoreType.DMA
    any_space = pl.BlockSpec(memory_space=pl.ANY)
    vmem = pl.BlockSpec(memory_space=pltpu.VMEM)
    square = jax.ShapeDtypeStruct((256, 256), F32)
    rows = jax.ShapeDtypeStruct((8, 8, 128), F32)
    row_a, own_a, row_b, cross, own_b = pl.pallas_call(
        kernel,
        out_shape=(rows, square, rows, square, square),
        in_specs=[any_space] * 8,
        out_specs=(vmem,) * 5,
        scratch_shapes=[
            pltpu.SMEM((128,), jnp.int32),
            pltpu.SMEM((128,), jnp.int32),
            pltpu.VMEM((4096, 128), F32),
            pltpu.VMEM((512, 1024), BF16),
            pltpu.VMEM((512, 1024), BF16),
            pltpu.VMEM((2, 4, 256, 128), F32),
            pltpu.VMEM((2, 256, 512), BF16),
            pltpu.VMEM((2, 256, 512), BF16),
            pltpu.VMEM((256, 256), F32),
            pltpu.VMEM((256, 256), F32),
            pltpu.VMEM((256, 256), F32),
            pltpu.VMEM((4, 8, 4, 2, 8, 128), F32),
            pltpu.VMEM((4, 8, 4, 2, 8, 128), F32),
            pltpu.VMEM((8, 4, 2, 8, 128), F32),
            pltpu.VMEM((4, 4, 2, 8, 128), F32),
            pltpu.VMEM((2, 4, 4, 2, 8, 128), F32),
            pltpu.VMEM((2, 2, 4, 4, 2, 8, 128), F32),
            pltpu.VMEM((4, 4, 2, 8, 128), F32),
            pltpu.VMEM((2, 2, 4, 2, 2, 8, 128), F32),
            pltpu.VMEM((2, 4, 4, 4, 2, 8, 128), F32),
            pltpu.VMEM((2, 4, 8, 128), F32),
            pltpu.VMEM((2, 4, 8, 128), F32),
            pltpu.VMEM((2, 4, 8, 128), F32),
            pltpu.VMEM((2, 4, 8, 128), F32),
            pltpu.VMEM((3, 4, 8, 128), F32),
            pltpu.VMEM((32, 8, 128), F32),
            pltpu.VMEM((8, 128), F32),
            pltpu.VMEM((2, 4, 3, 8, 8, 128), F32),
            pltpu.VMEM((512, 8, 128), F32),
            dma((5,)), dma((3,)),
            dma((3,)), dma((2, 9)), dma((2,)), dma((1,)), dma((1,)),
            dma((3,)), dma((1,)), dma((2, 2, 4)), dma((2, 4, 4)),
            dma((1,)), dma((1,)), dma((1,)), dma((1,)), dma((1,)), dma((3,)),
            dma((3, 4)), dma((3,)),
        ],
        compiler_params=pltpu.CompilerParams(
            collective_id=0, has_side_effects=True, vmem_limit_bytes=60 * 1024 * 1024
        ),
        name="selected_inversion",
    )(
        inverse_block.reshape(4096, 128),
        panel_first.reshape(4, 16, 128),
        panel_second.reshape(4, 16, 128),
        coupling, dinv_first, dinv_second, struct_first, struct_second,
    )
    return (
        row_a.reshape(8, 1, 8, 128), own_a, row_b.reshape(8, 1, 8, 128), cross, own_b,
    )


def solution(mesh):
    return jax.shard_map(
        body,
        mesh=mesh,
        in_specs=(
            P(None, "prow", None, None, "pcol", None),
            P(None, "prow", "pcol", None),
            P(None, "prow", "pcol", None),
            P("prow", None),
            P(),
            P(),
            P(),
            P(),
        ),
        out_specs=(P(None, "pcol", "prow", None), P(), P(None, "pcol", "prow", None), P(), P()),
        check_vma=False,
    )
```

```python
import jax
import jax.numpy as jnp
from jax import lax
from jax.experimental import pallas as pl
from jax.experimental.pallas import tpu as pltpu
from jax.sharding import PartitionSpec as P

NX, NZ, NY = 4, 8, 8
F32, BF16 = jnp.float32, jnp.bfloat16
MESH = pl.DeviceIdType.MESH

NN = (((1,), (0,)), ((), ()))
NT = (((1,), (1,)), ((), ()))


def split(v):
    hi = v.astype(BF16)
    return hi, (v - hi.astype(F32)).astype(BF16)


def dot3(a, b, dims=NN):
    def one(u, v):
        return lax.dot_general(u, v, dims, preferred_element_type=F32)

    return one(a[0], b[0]) + (one(a[0], b[1]) + one(a[1], b[0]))


def steps_of(way, half):
    return 4 if (way == 0) == (half == 0) else 3


def kernel(
    g_hbm, a_hbm, b_hbm, c_hbm, d1_hbm, d2_hbm, s1_hbm, s2_hbm,
    out_a, own_1, out_b, cross_out, own_2,
    s1, s2, g_raw, g_hi, g_lo, full, p_hi, p_lo, c_full, d1, d2,
    pa, pb, za, sb,
    xa_mid, xa_fin, xb_in, za_in, zb_in,
    rows_1, rows_2, ex_a, ex_b, pt, rr, tile, fin, all_sent,
    load_sem, own_sem,
    sent, ag_recv, sib_recv, cz_recv, cx_recv,
    xa_recv, xb_recv, za_recv, zb_recv,
    exa_recv, exb_recv, rr_send, rr_recv, yz_send, yz_recv,
    fx_recv, fs_recv,
):
    p = lax.axis_index("prow")
    q = lax.axis_index("pcol")
    x, z = p // NZ, lax.rem(p, NZ)
    y, core = q // 2, lax.rem(q, 2)

    def at_x(k):
        return lax.rem(x + k + NX, NX)

    def at_z(k):
        return lax.rem(z + k + NZ, NZ)

    def at_y(k):
        return lax.rem(y + k + NY, NY)

    sibling = (p, y * 2 + 1 - core)

    def remote(src, dst, send, recv, where):
        return pltpu.make_async_remote_copy(
            src_ref=src, dst_ref=dst, send_sem=send, recv_sem=recv,
            device_id=where, device_id_type=MESH,
        )

    barrier = pltpu.get_barrier_semaphore()
    near = [(p, at_y(k) * 2 + core) for k in (1, -1, 2, -2)] + [sibling]
    near += [(x * NZ + at_z(k), q) for k in range(1, NZ)]
    near += [(at_x(k) * NZ + z, q) for k in range(1, NX)]
    for where in near:
        pl.semaphore_signal(barrier, inc=1, device_id=where, device_id_type=MESH)

    def all_of(ref, semaphore):
        pltpu.make_async_copy(ref, ref, semaphore).wait()

    rows16 = pl.ds(pl.multiple_of(q * 16, 16), 16)
    rows8 = pl.ds(pl.multiple_of(p * 8, 8), 8)
    own = [
        pltpu.make_async_copy(a_hbm, full.at[0, :, rows16], own_sem.at[0]),
        pltpu.make_async_copy(b_hbm, full.at[1, :, rows16], own_sem.at[1]),
        pltpu.make_async_copy(c_hbm, c_full.at[rows8], own_sem.at[2]),
    ]
    loads = [
        pltpu.make_async_copy(g_hbm, g_raw, load_sem.at[0]),
        pltpu.make_async_copy(d1_hbm, d1, load_sem.at[1]),
        pltpu.make_async_copy(d2_hbm, d2, load_sem.at[2]),
        pltpu.make_async_copy(s1_hbm, s1, load_sem.at[3]),
        pltpu.make_async_copy(s2_hbm, s2, load_sem.at[4]),
    ]
    for copy in own + loads:
        copy.start()

    pl.semaphore_wait(barrier, len(near))

    def shard(k, row_y):
        rows = row_y * 2 + core
        return full.at[k, :, pl.ds(pl.multiple_of(rows * 16, 16), 16)]

    def ring(k, of, to):
        ref = shard(k, at_y(of))
        return remote(
            ref, ref, sent.at[0], ag_recv.at[k, of - to + 4],
            (p, at_y(to) * 2 + core),
        )

    def push(k, of, to):
        copy = ring(k, of, to)
        copy.start()

    def across(k, of):
        ref = shard(k, at_y(of))
        copy = remote(ref, ref, sent.at[0], sib_recv.at[k], sibling)
        copy.start()

    def got(k, of):
        ring(k, of, 0).wait_recv()
        across(k, of)

    own[0].wait()
    for to in (2, -2, 1, -1):
        push(0, 0, to)
    across(0, 0)
    own[1].wait()
    for to in (2, -2):
        push(1, 0, to)
    own[2].wait()

    def cz_copy(k):
        return remote(
            c_full.at[rows8], c_full.at[rows8], sent.at[0], cz_recv.at[0],
            (x * NZ + at_z(k), q),
        )

    for k in range(1, NZ):
        cz_copy(k).start()

    for index in (0, 3, 4):
        loads[index].wait()

    def split_g(c, carry):
        hi, lo = split(g_raw[pl.ds(c, 512, stride=8), :])
        columns = pl.ds(pl.multiple_of(c * 128, 128), 128)
        g_hi[:, columns] = hi
        g_lo[:, columns] = lo
        return carry

    lax.fori_loop(0, 8, split_g, 0)

    def forward(k, of):
        ring(k, of, 0).wait_recv()
        way = 1 if of < 0 else -1
        push(k, of, way)
        if (of < 0) == (k == 0):
            push(k, of, 2 * way)
        across(k, of)

    forward(0, -2)
    forward(0, 2)
    for to in (1, -1):
        push(1, 0, to)
    across(1, 0)
    got(0, -1)
    got(0, 1)
    forward(1, -2)
    forward(1, 2)
    all_of(c_full.at[0:56], cz_recv.at[0])
    rows64 = pl.ds(pl.multiple_of(x * 64, 64), 64)

    def cx_copy(k):
        return remote(
            c_full.at[rows64], c_full.at[rows64], sent.at[0], cx_recv.at[0],
            (at_x(k) * NZ + z, q),
        )

    for k in range(1, NX):
        cx_copy(k).start()
    got(0, -3)
    got(0, 3)
    got(0, -4)

    def prepare(k, struct):
        all_of(full.at[k, :, 0:128], sib_recv.at[k])
        for r in range(4):
            mask = struct[r * (NX * NZ) + p].astype(F32)
            hi, lo = split(full[k, r] * mask)
            p_hi[k, :, r * 128:(r + 1) * 128] = hi
            p_lo[k, :, r * 128:(r + 1) * 128] = lo

    def col_mask(struct, c):
        return struct[c * (NY * 2) + q].astype(F32)

    prepare(0, s1)

    def mul_a(t, carry):
        columns = pl.ds(pl.multiple_of(t * 256, 256), 256)
        r = dot3((p_hi[0], p_lo[0]), (g_hi[:, columns], g_lo[:, columns]))
        pa[:, :, t, 0] = r[:, :128].reshape(NX, NZ, 8, 128)
        pa[:, :, t, 1] = r[:, 128:].reshape(NX, NZ, 8, 128)
        return carry

    lax.fori_loop(0, 4, mul_a, 0)

    x_right, x_left = (at_x(1) * NZ + z, q), (at_x(-1) * NZ + z, q)

    def xa_piece(d, half):
        return pa.at[d, half * 4:(half + 1) * 4]

    def xa_copy(index, d, half, into, where):
        return remote(xa_piece(d, half), into, sent.at[1], xa_recv.at[min(index, 2)], where)

    xa = {
        "far0": xa_copy(0, at_x(2), 0, xa_mid.at[0], x_right),
        "far1": xa_copy(1, at_x(2), 1, xa_mid.at[1], x_left),
        "near1": xa_copy(2, at_x(1), 1, xa_fin.at[0, 1], x_right),
        "near0": xa_copy(3, at_x(3), 0, xa_fin.at[1, 0], x_left),
        "sum0": xa_copy(4, at_x(1), 0, xa_fin.at[0, 0], x_right),
        "sum1": xa_copy(5, at_x(3), 1, xa_fin.at[1, 1], x_left),
    }
    for name in ("far0", "far1", "near1", "near0"):
        xa[name].start()

    for of in (-1, 1, -3, 3, 4):
        got(1, of)
    all_of(c_full.at[0:192], cx_recv.at[0])
    coupling = c_full[...]
    c_parts = split(coupling)
    ct_parts = split(coupling.T)

    def mul_c(t, carry):
        first = jnp.concatenate(
            [pa[:, :, t, h].reshape(256, 128) * col_mask(s1, 2 * t + h) for h in (0, 1)], axis=1
        )
        r = dot3(ct_parts, split(first))
        pb[:, :, t, 0] = r[:, :128].reshape(NX, NZ, 8, 128)
        pb[:, :, t, 1] = r[:, 128:].reshape(NX, NZ, 8, 128)
        return carry

    lax.fori_loop(0, 4, mul_c, 0)
    prepare(1, s2)

    def mul_b(t, carry):
        columns = pl.ds(pl.multiple_of(t * 256, 256), 256)
        r = dot3((p_hi[1], p_lo[1]), (g_hi[:, columns], g_lo[:, columns]))
        for h in (0, 1):
            block = r[:, h * 128:(h + 1) * 128].reshape(NX, NZ, 8, 128)
            pb[:, :, t, h] = block - pb[:, :, t, h]
        return carry

    lax.fori_loop(0, 4, mul_b, 0)

    def zb_copy(way, j, step):
        away = steps_of(way, j // 2) - step + 1
        d = at_z(away) if way == 0 else at_z(-away)
        to_z = at_z(1) if way == 0 else at_z(-1)
        return d, remote(
            pb.at[j, d], zb_in.at[way, j, step - 1],
            sent.at[1], zb_recv.at[way, j, step - 1],
            (x * NZ + to_z, q),
        )

    def zb_step(step):
        for i in range(4):
            for way in (0, 1):
                j = (i + 2 * way) % 4
                if step > steps_of(way, j // 2):
                    continue
                d, copy = zb_copy(way, j, step)
                if step > 1:
                    zb_copy(way, j, step - 1)[1].wait_recv()
                    pb[j, d] += zb_in[way, j, step - 2]
                copy.start()

    zb_step(1)
    xa["far0"].wait_recv()
    pa[at_x(1), 0:4] += xa_mid[0]
    xa["sum0"].start()
    xa["far1"].wait_recv()
    pa[at_x(3), 4:8] += xa_mid[1]
    xa["sum1"].start()
    zb_step(2)
    zb_step(3)
    all_of(xa_fin, xa_recv.at[2])
    for half in (0, 1):
        rows = slice(half * 4, half * 4 + 4)
        za[rows] = pa[x, rows] + xa_fin[0, half] + xa_fin[1, half]

    def xb_copy(k):
        return remote(
            sb.at[at_x(k)], xb_in.at[k], sent.at[1], xb_recv.at[0], (at_x(k) * NZ + z, q)
        )

    def za_copy(way, half, index):
        away, over = ((4, 2), (3, 2), (2, 2), (1, 1))[index]
        sign = 1 - 2 * way
        return remote(
            za.at[at_z(sign * away), half * 2:(half + 1) * 2], za_in.at[way, half, index],
            sent.at[1], za_recv.at[way, half, index], (x * NZ + at_z(sign * over), q),
        )

    sides = [(way, half) for half in (0, 1) for way in (0, 1)]

    def za_start():
        for way, half in sides:
            if steps_of(way, half) == 4:
                za_copy(way, half, 0).start()
            za_copy(way, half, 1).start()
        for way, half in sides:
            if steps_of(way, half) == 3:
                za_copy(way, half, 2).start()

    def za_middle():
        for way, half in sides:
            for index in (0, 1):
                if index == 0 and steps_of(way, half) == 3:
                    continue
                za_copy(way, half, index).wait_recv()
                d = at_z((2 - index) * (1 - 2 * way))
                za[d, half * 2:(half + 1) * 2] += za_in[way, half, index]
                za_copy(way, half, index + 2).start()

    to_col = 2 * z + 1 - lax.rem(x, 2)

    def hand_over(rows, into, parity, recv):
        return remote(
            rows.at[parity], into.at[x // 2], sent.at[1], recv.at[0],
            (q + 16 * parity, to_col),
        )

    za_start()
    zb_step(4)
    za_middle()
    for j in range(4):
        last = [steps_of(way, j // 2) for way in (0, 1)]
        for way in (0, 1):
            zb_copy(way, j, last[way])[1].wait_recv()
        sb[j] = pb[j, z] + zb_in[0, j, last[0] - 1] + zb_in[1, j, last[1] - 1]
    for k in (2, 1, 3):
        xb_copy(k).start()


    def deliver(value, c, struct, out, rows):
        block = value * (-col_mask(struct, c))
        out[c] = block
        rows[c % 2, c // 2] = block

    for half in (0, 1):
        value = za[z, half * 2:(half + 1) * 2]
        for way in (0, 1):
            for index in (2, 3):
                za_copy(way, half, index).wait_recv()
                value = value + za_in[way, half, index]
        for c in range(4 * half, 4 * half + 4):
            deliver(value[c // 2 - 2 * half, c % 2], c, s1, out_a, rows_1)
    for parity in (0, 1):
        hand_over(rows_1, ex_a, parity, exa_recv).start()
    all_of(xb_in.at[1:4], xb_recv.at[0])
    value = sb[x] + xb_in[1] + xb_in[2] + xb_in[3]
    for c in range(8):
        deliver(value[c // 2, c % 2], c, s2, out_b, rows_2)
    for parity in (0, 1):
        hand_over(rows_2, ex_b, parity, exb_recv).start()

    def at_sum(m, j):
        return j * NZ + lax.rem(y + 3 * m, NZ)

    def tile_copy(m, j):
        return remote(
            pt.at[m, j], rr.at[p], rr_send.at[0], rr_recv.at[0], (at_sum(m, j), q)
        )

    def panel_rows(ref):
        return split(jnp.concatenate([ref[:, r].reshape(16, 128) for r in range(4)], axis=1))

    def send_tiles(m, value):
        for s in range(2):
            for h in range(2):
                pt[m, s * 2 + h] = value[s * 8:(s + 1) * 8, h * 128:(h + 1) * 128]
        for j in range(4):
            @pl.when(at_sum(m, j) != p)
            def _():
                tile_copy(m, j).start()

            @pl.when(at_sum(m, j) == p)
            def _():
                pltpu.make_async_copy(pt.at[m, j], rr.at[p], rr_recv.at[0]).start()

    pltpu.make_async_copy(ex_a, ex_a, exa_recv.at[0]).wait()
    rows_a = panel_rows(ex_a)
    send_tiles(0, dot3(rows_a, (p_hi[0], p_lo[0]), NT))
    send_tiles(1, dot3(rows_a, (p_hi[1], p_lo[1]), NT))
    pltpu.make_async_copy(ex_b, ex_b, exb_recv.at[0]).wait()
    rows_b = panel_rows(ex_b)
    send_tiles(2, dot3(rows_b, (p_hi[1], p_lo[1]), NT))

    turn = lax.rem(z - y + NZ, NZ)
    mine = turn // 3

    def make_sums(which):
        @pl.when(which)
        def _():
            pltpu.make_async_copy(rr, rr, rr_recv.at[0]).wait()
            tile[...] = jnp.sum(rr[...], axis=0)
            place = fin.at[core, x, mine, y]
            spot = yz_recv.at[mine]
            pltpu.make_async_copy(tile, place, spot).start()

            def far_first(k):
                return 4 + (k + 1) // 2 * (1 - 2 * lax.rem(k, 2))

            def spread(k, carry):
                to_z, to_y = at_z(far_first(k // NY)), at_y(far_first(lax.rem(k, NY)))
                remote(
                    tile, place, yz_send.at[0], spot, (x * NZ + to_z, to_y * 2 + core)
                ).start()
                return carry

            lax.fori_loop(0, NY * NZ - 1, spread, 0)

    make_sums(jnp.logical_or(turn == 0, turn == 3))
    make_sums(turn == 6)

    def part(origin, which):
        return fin.at[core, origin, which]

    def fx_copy(which, k):
        return remote(
            part(x, which), part(x, which), sent.at[2], fx_recv.at[which, k],
            (at_x(k) * NZ + z, q),
        )

    def fs_copy(which, k):
        ref = part(at_x(-k), which)
        return remote(ref, ref, sent.at[2], fs_recv.at[which], sibling)

    for which in range(3):
        block = part(x, which)
        pltpu.make_async_copy(block, block, yz_recv.at[which]).wait()
        for k in (2, 1, 3):
            fx_copy(which, k).start()
        fs_copy(which, 0).start()
    for which in range(3):
        for k in (1, 3, 2):
            fx_copy(which, k).wait_recv()
            fs_copy(which, k).start()

    loads[1].wait()
    loads[2].wait()
    for which in (0, 1):
        all_of(fin.at[1 - core, :, which], fs_recv.at[which])

    def places():
        for co in range(2):
            for xo in range(4):
                xs, h = (1 - co) + 2 * (xo // 2), xo % 2
                yield (
                    slice(xs * 64, xs * 64 + 64), slice(h * 128, h * 128 + 128),
                    fin.at[co, xo],
                )

    for rows, columns, ref in places():
        own_1[rows, columns] = d1[rows, columns] - ref[0].reshape(64, 128)
        cross_out[rows, columns] = ref[1].reshape(64, 128)
    cross = -(cross_out[...].T + dot3(ct_parts, split(own_1[...])))
    cross_out[...] = cross
    last = d2[...] - dot3(split(cross), c_parts)
    all_of(fin.at[1 - core, :, 2], fs_recv.at[2])
    for rows, columns, ref in places():
        own_2[rows, columns] = last[rows, columns] - ref[2].reshape(64, 128)

    all_of(all_sent.at[0:302], sent.at[0])
    all_of(all_sent, sent.at[1])
    all_of(all_sent.at[0:168], sent.at[2])

    @pl.when(lax.rem(turn, 3) == 0)
    def _():
        all_of(all_sent.at[0:11], rr_send.at[0])
        all_of(all_sent.at[0:63], yz_send.at[0])

    @pl.when(lax.rem(turn, 3) != 0)
    def _():
        all_of(all_sent.at[0:12], rr_send.at[0])


def body(
    inverse_block,
    panel_first,
    panel_second,
    coupling,
    dinv_first,
    dinv_second,
    struct_first,
    struct_second,
):
    dma = pltpu.SemaphoreType.DMA
    any_space = pl.BlockSpec(memory_space=pl.ANY)
    vmem = pl.BlockSpec(memory_space=pltpu.VMEM)
    square = jax.ShapeDtypeStruct((256, 256), F32)
    rows = jax.ShapeDtypeStruct((8, 8, 128), F32)
    row_a, own_a, row_b, cross, own_b = pl.pallas_call(
        kernel,
        out_shape=(rows, square, rows, square, square),
        in_specs=[any_space] * 8,
        out_specs=(vmem,) * 5,
        scratch_shapes=[
            pltpu.SMEM((128,), jnp.int32),
            pltpu.SMEM((128,), jnp.int32),
            pltpu.VMEM((4096, 128), F32),
            pltpu.VMEM((512, 1024), BF16),
            pltpu.VMEM((512, 1024), BF16),
            pltpu.VMEM((2, 4, 256, 128), F32),
            pltpu.VMEM((2, 256, 512), BF16),
            pltpu.VMEM((2, 256, 512), BF16),
            pltpu.VMEM((256, 256), F32),
            pltpu.VMEM((256, 256), F32),
            pltpu.VMEM((256, 256), F32),
            pltpu.VMEM((4, 8, 4, 2, 8, 128), F32),
            pltpu.VMEM((4, 8, 4, 2, 8, 128), F32),
            pltpu.VMEM((8, 4, 2, 8, 128), F32),
            pltpu.VMEM((4, 4, 2, 8, 128), F32),
            pltpu.VMEM((2, 4, 4, 2, 8, 128), F32),
            pltpu.VMEM((2, 2, 4, 4, 2, 8, 128), F32),
            pltpu.VMEM((4, 4, 2, 8, 128), F32),
            pltpu.VMEM((2, 2, 4, 2, 2, 8, 128), F32),
            pltpu.VMEM((2, 4, 4, 4, 2, 8, 128), F32),
            pltpu.VMEM((2, 4, 8, 128), F32),
            pltpu.VMEM((2, 4, 8, 128), F32),
            pltpu.VMEM((2, 4, 8, 128), F32),
            pltpu.VMEM((2, 4, 8, 128), F32),
            pltpu.VMEM((3, 4, 8, 128), F32),
            pltpu.VMEM((32, 8, 128), F32),
            pltpu.VMEM((8, 128), F32),
            pltpu.VMEM((2, 4, 3, 8, 8, 128), F32),
            pltpu.VMEM((512, 8, 128), F32),
            dma((5,)), dma((3,)),
            dma((3,)), dma((2, 9)), dma((2,)), dma((1,)), dma((1,)),
            dma((3,)), dma((1,)), dma((2, 2, 4)), dma((2, 4, 4)),
            dma((1,)), dma((1,)), dma((1,)), dma((1,)), dma((1,)), dma((3,)),
            dma((3, 4)), dma((3,)),
        ],
        compiler_params=pltpu.CompilerParams(
            collective_id=0, has_side_effects=True, vmem_limit_bytes=60 * 1024 * 1024
        ),
        name="selected_inversion",
    )(
        inverse_block.reshape(4096, 128),
        panel_first.reshape(4, 16, 128),
        panel_second.reshape(4, 16, 128),
        coupling, dinv_first, dinv_second, struct_first, struct_second,
    )
    return (
        row_a.reshape(8, 1, 8, 128), own_a, row_b.reshape(8, 1, 8, 128), cross, own_b,
    )


def solution(mesh):
    return jax.shard_map(
        body,
        mesh=mesh,
        in_specs=(
            P(None, "prow", None, None, "pcol", None),
            P(None, "prow", "pcol", None),
            P(None, "prow", "pcol", None),
            P("prow", None),
            P(),
            P(),
            P(),
            P(),
        ),
        out_specs=(P(None, "pcol", "prow", None), P(), P(None, "pcol", "prow", None), P(), P()),
        check_vma=False,
    )
```

```python
import jax
import jax.numpy as jnp
from jax import lax
from jax.experimental import pallas as pl
from jax.experimental.pallas import tpu as pltpu
from jax.sharding import PartitionSpec as P

NX, NZ, NY = 4, 8, 8
F32, BF16 = jnp.float32, jnp.bfloat16
MESH = pl.DeviceIdType.MESH

NN = (((1,), (0,)), ((), ()))
NT = (((1,), (1,)), ((), ()))


def split(v):
    hi = v.astype(BF16)
    return hi, (v - hi.astype(F32)).astype(BF16)


def dot3(a, b, dims=NN):
    def one(u, v):
        return lax.dot_general(u, v, dims, preferred_element_type=F32)

    return one(a[0], b[0]) + (one(a[0], b[1]) + one(a[1], b[0]))


def steps_of(way, half):
    return 4 if (way == 0) == (half == 0) else 3


def kernel(
    g_hbm, a_hbm, b_hbm, c_hbm, d1_hbm, d2_hbm, s1_hbm, s2_hbm,
    out_a, own_1, out_b, cross_out, own_2,
    s1, s2, g_raw, g_hi, g_lo, full, p_hi, p_lo, c_full, d1, d2,
    pa, pb, za, sb,
    xa_mid, xa_fin, xb_in, za_in, zb_in,
    rows_1, rows_2, ex_a, ex_b, pt, rr, tile, fin, all_sent,
    load_sem, own_sem,
    sent, ag_recv, sib_recv, cz_recv, cx_recv,
    xa_recv, xb_recv, za_recv, zb_recv,
    exa_recv, exb_recv, rr_send, rr_recv, yz_send, yz_recv,
    fx_recv, fs_recv,
):
    p = lax.axis_index("prow")
    q = lax.axis_index("pcol")
    x, z = p // NZ, lax.rem(p, NZ)
    y, core = q // 2, lax.rem(q, 2)

    def at_x(k):
        return lax.rem(x + k + NX, NX)

    def at_z(k):
        return lax.rem(z + k + NZ, NZ)

    def at_y(k):
        return lax.rem(y + k + NY, NY)

    sibling = (p, y * 2 + 1 - core)

    def remote(src, dst, send, recv, where):
        return pltpu.make_async_remote_copy(
            src_ref=src, dst_ref=dst, send_sem=send, recv_sem=recv,
            device_id=where, device_id_type=MESH,
        )

    barrier = pltpu.get_barrier_semaphore()
    near = [(p, at_y(k) * 2 + core) for k in (1, -1, 2, -2)] + [sibling]
    near += [(x * NZ + at_z(k), q) for k in range(1, NZ)]
    near += [(at_x(k) * NZ + z, q) for k in range(1, NX)]
    for where in near:
        pl.semaphore_signal(barrier, inc=1, device_id=where, device_id_type=MESH)

    def all_of(ref, semaphore):
        pltpu.make_async_copy(ref, ref, semaphore).wait()

    rows16 = pl.ds(pl.multiple_of(q * 16, 16), 16)
    rows8 = pl.ds(pl.multiple_of(p * 8, 8), 8)
    own = [
        pltpu.make_async_copy(a_hbm, full.at[0, :, rows16], own_sem.at[0]),
        pltpu.make_async_copy(b_hbm, full.at[1, :, rows16], own_sem.at[1]),
        pltpu.make_async_copy(c_hbm, c_full.at[rows8], own_sem.at[2]),
    ]
    loads = [
        pltpu.make_async_copy(g_hbm, g_raw, load_sem.at[0]),
        pltpu.make_async_copy(d1_hbm, d1, load_sem.at[1]),
        pltpu.make_async_copy(d2_hbm, d2, load_sem.at[2]),
        pltpu.make_async_copy(s1_hbm, s1, load_sem.at[3]),
        pltpu.make_async_copy(s2_hbm, s2, load_sem.at[4]),
    ]
    for copy in own + loads:
        copy.start()

    pl.semaphore_wait(barrier, len(near))

    def shard(k, row_y):
        rows = row_y * 2 + core
        return full.at[k, :, pl.ds(pl.multiple_of(rows * 16, 16), 16)]

    def ring(k, of, to):
        ref = shard(k, at_y(of))
        return remote(
            ref, ref, sent.at[0], ag_recv.at[k, of - to + 4],
            (p, at_y(to) * 2 + core),
        )

    def push(k, of, to):
        copy = ring(k, of, to)
        copy.start()

    def across(k, of):
        ref = shard(k, at_y(of))
        copy = remote(ref, ref, sent.at[0], sib_recv.at[k], sibling)
        copy.start()

    def got(k, of):
        ring(k, of, 0).wait_recv()
        across(k, of)

    own[0].wait()
    for to in (2, -2, 1, -1):
        push(0, 0, to)
    across(0, 0)
    own[1].wait()
    for to in (2, -2):
        push(1, 0, to)
    own[2].wait()

    def cz_copy(k):
        return remote(
            c_full.at[rows8], c_full.at[rows8], sent.at[0], cz_recv.at[0],
            (x * NZ + at_z(k), q),
        )

    for k in range(1, NZ):
        cz_copy(k).start()

    for index in (0, 3, 4):
        loads[index].wait()

    def split_g(c, carry):
        hi, lo = split(g_raw[pl.ds(c, 512, stride=8), :])
        columns = pl.ds(pl.multiple_of(c * 128, 128), 128)
        g_hi[:, columns] = hi
        g_lo[:, columns] = lo
        return carry

    lax.fori_loop(0, 8, split_g, 0)

    def forward(k, of):
        ring(k, of, 0).wait_recv()
        way = 1 if of < 0 else -1
        push(k, of, way)
        if (of < 0) == (k == 0):
            push(k, of, 2 * way)
        across(k, of)

    forward(0, -2)
    forward(0, 2)
    for to in (1, -1):
        push(1, 0, to)
    across(1, 0)
    got(0, -1)
    got(0, 1)
    forward(1, -2)
    forward(1, 2)
    all_of(c_full.at[0:56], cz_recv.at[0])
    rows64 = pl.ds(pl.multiple_of(x * 64, 64), 64)

    def cx_copy(k):
        return remote(
            c_full.at[rows64], c_full.at[rows64], sent.at[0], cx_recv.at[0],
            (at_x(k) * NZ + z, q),
        )

    for k in range(1, NX):
        cx_copy(k).start()
    got(0, -3)
    got(0, 3)
    got(0, -4)

    def prepare(k, struct):
        all_of(full.at[k, :, 0:128], sib_recv.at[k])
        for r in range(4):
            mask = struct[r * (NX * NZ) + p].astype(F32)
            hi, lo = split(full[k, r] * mask)
            p_hi[k, :, r * 128:(r + 1) * 128] = hi
            p_lo[k, :, r * 128:(r + 1) * 128] = lo

    def col_mask(struct, c):
        return struct[c * (NY * 2) + q].astype(F32)

    prepare(0, s1)

    def mul_a(t, carry):
        columns = pl.ds(pl.multiple_of(t * 256, 256), 256)
        r = dot3((p_hi[0], p_lo[0]), (g_hi[:, columns], g_lo[:, columns]))
        pa[:, :, t, 0] = r[:, :128].reshape(NX, NZ, 8, 128)
        pa[:, :, t, 1] = r[:, 128:].reshape(NX, NZ, 8, 128)
        return carry

    lax.fori_loop(0, 4, mul_a, 0)

    x_right, x_left = (at_x(1) * NZ + z, q), (at_x(-1) * NZ + z, q)

    def xa_piece(d, half):
        return pa.at[d, half * 4:(half + 1) * 4]

    def xa_copy(index, d, half, into, where):
        return remote(xa_piece(d, half), into, sent.at[1], xa_recv.at[min(index, 2)], where)

    xa = {
        "far0": xa_copy(0, at_x(2), 0, xa_mid.at[0], x_right),
        "far1": xa_copy(1, at_x(2), 1, xa_mid.at[1], x_left),
        "near1": xa_copy(2, at_x(1), 1, xa_fin.at[0, 1], x_right),
        "near0": xa_copy(3, at_x(3), 0, xa_fin.at[1, 0], x_left),
        "sum0": xa_copy(4, at_x(1), 0, xa_fin.at[0, 0], x_right),
        "sum1": xa_copy(5, at_x(3), 1, xa_fin.at[1, 1], x_left),
    }
    for name in ("far0", "far1", "near1", "near0"):
        xa[name].start()

    for of in (-1, 1, -3, 3, 4):
        got(1, of)
    all_of(c_full.at[0:192], cx_recv.at[0])
    coupling = c_full[...]
    c_parts = split(coupling)
    ct_parts = split(coupling.T)

    def mul_c(t, carry):
        first = jnp.concatenate(
            [pa[:, :, t, h].reshape(256, 128) * col_mask(s1, 2 * t + h) for h in (0, 1)], axis=1
        )
        r = dot3(ct_parts, split(first))
        pb[:, :, t, 0] = r[:, :128].reshape(NX, NZ, 8, 128)
        pb[:, :, t, 1] = r[:, 128:].reshape(NX, NZ, 8, 128)
        return carry

    lax.fori_loop(0, 4, mul_c, 0)
    prepare(1, s2)

    def mul_b(t, carry):
        columns = pl.ds(pl.multiple_of(t * 256, 256), 256)
        r = dot3((p_hi[1], p_lo[1]), (g_hi[:, columns], g_lo[:, columns]))
        for h in (0, 1):
            block = r[:, h * 128:(h + 1) * 128].reshape(NX, NZ, 8, 128)
            pb[:, :, t, h] = block - pb[:, :, t, h]
        return carry

    lax.fori_loop(0, 4, mul_b, 0)

    def zb_copy(way, j, step):
        away = steps_of(way, j // 2) - step + 1
        d = at_z(away) if way == 0 else at_z(-away)
        to_z = at_z(1) if way == 0 else at_z(-1)
        return d, remote(
            pb.at[j, d], zb_in.at[way, j, step - 1],
            sent.at[1], zb_recv.at[way, j, step - 1],
            (x * NZ + to_z, q),
        )

    def zb_step(step):
        for j in range(4):
            for way in (0, 1):
                if step > steps_of(way, j // 2):
                    continue
                d, copy = zb_copy(way, j, step)
                if step > 1:
                    zb_copy(way, j, step - 1)[1].wait_recv()
                    pb[j, d] += zb_in[way, j, step - 2]
                copy.start()

    zb_step(1)
    xa["far0"].wait_recv()
    pa[at_x(1), 0:4] += xa_mid[0]
    xa["sum0"].start()
    xa["far1"].wait_recv()
    pa[at_x(3), 4:8] += xa_mid[1]
    xa["sum1"].start()
    zb_step(2)
    zb_step(3)
    all_of(xa_fin, xa_recv.at[2])
    for half in (0, 1):
        rows = slice(half * 4, half * 4 + 4)
        za[rows] = pa[x, rows] + xa_fin[0, half] + xa_fin[1, half]

    def xb_copy(k):
        return remote(
            sb.at[at_x(k)], xb_in.at[k], sent.at[1], xb_recv.at[0], (at_x(k) * NZ + z, q)
        )

    def za_copy(way, half, index):
        away, over = ((4, 2), (3, 2), (2, 2), (1, 1))[index]
        sign = 1 - 2 * way
        return remote(
            za.at[at_z(sign * away), half * 2:(half + 1) * 2], za_in.at[way, half, index],
            sent.at[1], za_recv.at[way, half, index], (x * NZ + at_z(sign * over), q),
        )

    sides = [(way, half) for half in (0, 1) for way in (0, 1)]

    def za_start():
        for way, half in sides:
            if steps_of(way, half) == 4:
                za_copy(way, half, 0).start()
            za_copy(way, half, 1).start()
        for way, half in sides:
            if steps_of(way, half) == 3:
                za_copy(way, half, 2).start()

    def za_middle():
        for way, half in sides:
            for index in (0, 1):
                if index == 0 and steps_of(way, half) == 3:
                    continue
                za_copy(way, half, index).wait_recv()
                d = at_z((2 - index) * (1 - 2 * way))
                za[d, half * 2:(half + 1) * 2] += za_in[way, half, index]
                za_copy(way, half, index + 2).start()

    to_col = 2 * z + 1 - lax.rem(x, 2)

    def hand_over(rows, into, parity, recv):
        return remote(
            rows.at[parity], into.at[x // 2], sent.at[1], recv.at[0],
            (q + 16 * parity, to_col),
        )

    za_start()
    zb_step(4)
    za_middle()
    for j in range(4):
        last = [steps_of(way, j // 2) for way in (0, 1)]
        for way in (0, 1):
            zb_copy(way, j, last[way])[1].wait_recv()
        sb[j] = pb[j, z] + zb_in[0, j, last[0] - 1] + zb_in[1, j, last[1] - 1]
    for k in (2, 1, 3):
        xb_copy(k).start()


    def deliver(value, c, struct, out, rows):
        block = value * (-col_mask(struct, c))
        out[c] = block
        rows[c % 2, c // 2] = block

    for half in (0, 1):
        value = za[z, half * 2:(half + 1) * 2]
        for way in (0, 1):
            for index in (2, 3):
                za_copy(way, half, index).wait_recv()
                value = value + za_in[way, half, index]
        for c in range(4 * half, 4 * half + 4):
            deliver(value[c // 2 - 2 * half, c % 2], c, s1, out_a, rows_1)
    for parity in (0, 1):
        hand_over(rows_1, ex_a, parity, exa_recv).start()
    all_of(xb_in.at[1:4], xb_recv.at[0])
    value = sb[x] + xb_in[1] + xb_in[2] + xb_in[3]
    for c in range(8):
        deliver(value[c // 2, c % 2], c, s2, out_b, rows_2)
    for parity in (0, 1):
        hand_over(rows_2, ex_b, parity, exb_recv).start()

    def at_sum(m, j):
        return j * NZ + lax.rem(y + 3 * m, NZ)

    def tile_copy(m, j):
        return remote(
            pt.at[m, j], rr.at[p], rr_send.at[0], rr_recv.at[0], (at_sum(m, j), q)
        )

    def panel_rows(ref):
        return split(jnp.concatenate([ref[:, r].reshape(16, 128) for r in range(4)], axis=1))

    def send_tiles(m, value):
        for s in range(2):
            for h in range(2):
                pt[m, s * 2 + h] = value[s * 8:(s + 1) * 8, h * 128:(h + 1) * 128]
        for j in range(4):
            @pl.when(at_sum(m, j) != p)
            def _():
                tile_copy(m, j).start()

            @pl.when(at_sum(m, j) == p)
            def _():
                pltpu.make_async_copy(pt.at[m, j], rr.at[p], rr_recv.at[0]).start()

    pltpu.make_async_copy(ex_a, ex_a, exa_recv.at[0]).wait()
    rows_a = panel_rows(ex_a)
    send_tiles(0, dot3(rows_a, (p_hi[0], p_lo[0]), NT))
    send_tiles(1, dot3(rows_a, (p_hi[1], p_lo[1]), NT))
    pltpu.make_async_copy(ex_b, ex_b, exb_recv.at[0]).wait()
    rows_b = panel_rows(ex_b)
    send_tiles(2, dot3(rows_b, (p_hi[1], p_lo[1]), NT))

    turn = lax.rem(z - y + NZ, NZ)
    mine = turn // 3

    def make_sums(which):
        @pl.when(which)
        def _():
            pltpu.make_async_copy(rr, rr, rr_recv.at[0]).wait()
            tile[...] = jnp.sum(rr[...], axis=0)
            place = fin.at[core, x, mine, y]
            spot = yz_recv.at[mine]
            pltpu.make_async_copy(tile, place, spot).start()

            far_first = (4, 3, 5, 2, 6, 1, 7, 0)
            columns = [at_y(k) * 2 + core for k in far_first]

            def spread(to_z, targets):
                for column in targets:
                    remote(
                        tile, place, yz_send.at[0], spot, (x * NZ + to_z, column)
                    ).start()

            def plane(k, carry):
                spread(at_z(4 + (k + 1) // 2 * (1 - 2 * lax.rem(k, 2))), columns)
                return carry

            lax.fori_loop(0, NZ - 1, plane, 0)
            spread(z, columns[:-1])

    make_sums(jnp.logical_or(turn == 0, turn == 3))
    make_sums(turn == 6)

    def part(origin, which):
        return fin.at[core, origin, which]

    def fx_copy(which, k):
        return remote(
            part(x, which), part(x, which), sent.at[2], fx_recv.at[which, k],
            (at_x(k) * NZ + z, q),
        )

    def fs_copy(which, k):
        ref = part(at_x(-k), which)
        return remote(ref, ref, sent.at[2], fs_recv.at[which], sibling)

    for which in range(3):
        block = part(x, which)
        pltpu.make_async_copy(block, block, yz_recv.at[which]).wait()
        for k in (2, 1, 3):
            fx_copy(which, k).start()
        fs_copy(which, 0).start()
    for which in range(3):
        for k in (1, 3, 2):
            fx_copy(which, k).wait_recv()
            fs_copy(which, k).start()

    loads[1].wait()
    loads[2].wait()
    for which in (0, 1):
        all_of(fin.at[1 - core, :, which], fs_recv.at[which])

    def places():
        for co in range(2):
            for xo in range(4):
                xs, h = (1 - co) + 2 * (xo // 2), xo % 2
                yield (
                    slice(xs * 64, xs * 64 + 64), slice(h * 128, h * 128 + 128),
                    fin.at[co, xo],
                )

    for rows, columns, ref in places():
        own_1[rows, columns] = d1[rows, columns] - ref[0].reshape(64, 128)
        cross_out[rows, columns] = ref[1].reshape(64, 128)
    cross = -(cross_out[...].T + dot3(ct_parts, split(own_1[...])))
    cross_out[...] = cross
    last = d2[...] - dot3(split(cross), c_parts)
    all_of(fin.at[1 - core, :, 2], fs_recv.at[2])
    for rows, columns, ref in places():
        own_2[rows, columns] = last[rows, columns] - ref[2].reshape(64, 128)

    all_of(all_sent.at[0:302], sent.at[0])
    all_of(all_sent, sent.at[1])
    all_of(all_sent.at[0:168], sent.at[2])

    @pl.when(lax.rem(turn, 3) == 0)
    def _():
        all_of(all_sent.at[0:11], rr_send.at[0])
        all_of(all_sent.at[0:63], yz_send.at[0])

    @pl.when(lax.rem(turn, 3) != 0)
    def _():
        all_of(all_sent.at[0:12], rr_send.at[0])


def body(
    inverse_block,
    panel_first,
    panel_second,
    coupling,
    dinv_first,
    dinv_second,
    struct_first,
    struct_second,
):
    dma = pltpu.SemaphoreType.DMA
    any_space = pl.BlockSpec(memory_space=pl.ANY)
    vmem = pl.BlockSpec(memory_space=pltpu.VMEM)
    square = jax.ShapeDtypeStruct((256, 256), F32)
    rows = jax.ShapeDtypeStruct((8, 8, 128), F32)
    row_a, own_a, row_b, cross, own_b = pl.pallas_call(
        kernel,
        out_shape=(rows, square, rows, square, square),
        in_specs=[any_space] * 8,
        out_specs=(vmem,) * 5,
        scratch_shapes=[
            pltpu.SMEM((128,), jnp.int32),
            pltpu.SMEM((128,), jnp.int32),
            pltpu.VMEM((4096, 128), F32),
            pltpu.VMEM((512, 1024), BF16),
            pltpu.VMEM((512, 1024), BF16),
            pltpu.VMEM((2, 4, 256, 128), F32),
            pltpu.VMEM((2, 256, 512), BF16),
            pltpu.VMEM((2, 256, 512), BF16),
            pltpu.VMEM((256, 256), F32),
            pltpu.VMEM((256, 256), F32),
            pltpu.VMEM((256, 256), F32),
            pltpu.VMEM((4, 8, 4, 2, 8, 128), F32),
            pltpu.VMEM((4, 8, 4, 2, 8, 128), F32),
            pltpu.VMEM((8, 4, 2, 8, 128), F32),
            pltpu.VMEM((4, 4, 2, 8, 128), F32),
            pltpu.VMEM((2, 4, 4, 2, 8, 128), F32),
            pltpu.VMEM((2, 2, 4, 4, 2, 8, 128), F32),
            pltpu.VMEM((4, 4, 2, 8, 128), F32),
            pltpu.VMEM((2, 2, 4, 2, 2, 8, 128), F32),
            pltpu.VMEM((2, 4, 4, 4, 2, 8, 128), F32),
            pltpu.VMEM((2, 4, 8, 128), F32),
            pltpu.VMEM((2, 4, 8, 128), F32),
            pltpu.VMEM((2, 4, 8, 128), F32),
            pltpu.VMEM((2, 4, 8, 128), F32),
            pltpu.VMEM((3, 4, 8, 128), F32),
            pltpu.VMEM((32, 8, 128), F32),
            pltpu.VMEM((8, 128), F32),
            pltpu.VMEM((2, 4, 3, 8, 8, 128), F32),
            pltpu.VMEM((512, 8, 128), F32),
            dma((5,)), dma((3,)),
            dma((3,)), dma((2, 9)), dma((2,)), dma((1,)), dma((1,)),
            dma((3,)), dma((1,)), dma((2, 2, 4)), dma((2, 4, 4)),
            dma((1,)), dma((1,)), dma((1,)), dma((1,)), dma((1,)), dma((3,)),
            dma((3, 4)), dma((3,)),
        ],
        compiler_params=pltpu.CompilerParams(
            collective_id=0, has_side_effects=True, vmem_limit_bytes=60 * 1024 * 1024
        ),
        name="selected_inversion",
    )(
        inverse_block.reshape(4096, 128),
        panel_first.reshape(4, 16, 128),
        panel_second.reshape(4, 16, 128),
        coupling, dinv_first, dinv_second, struct_first, struct_second,
    )
    return (
        row_a.reshape(8, 1, 8, 128), own_a, row_b.reshape(8, 1, 8, 128), cross, own_b,
    )


def solution(mesh):
    return jax.shard_map(
        body,
        mesh=mesh,
        in_specs=(
            P(None, "prow", None, None, "pcol", None),
            P(None, "prow", "pcol", None),
            P(None, "prow", "pcol", None),
            P("prow", None),
            P(),
            P(),
            P(),
            P(),
        ),
        out_specs=(P(None, "pcol", "prow", None), P(), P(None, "pcol", "prow", None), P(), P()),
        check_vma=False,
    )
```

```python
import jax
import jax.numpy as jnp
from jax import lax
from jax.experimental import pallas as pl
from jax.experimental.pallas import tpu as pltpu
from jax.sharding import PartitionSpec as P

NX, NZ, NY = 4, 8, 8
F32, BF16 = jnp.float32, jnp.bfloat16
MESH = pl.DeviceIdType.MESH

NN = (((1,), (0,)), ((), ()))
NT = (((1,), (1,)), ((), ()))


def split(v):
    hi = v.astype(BF16)
    return hi, (v - hi.astype(F32)).astype(BF16)


def dot3(a, b, dims=NN):
    def one(u, v):
        return lax.dot_general(u, v, dims, preferred_element_type=F32)

    return one(a[0], b[0]) + (one(a[0], b[1]) + one(a[1], b[0]))


def steps_of(way, half):
    return 4 if (way == 0) == (half == 0) else 3


def kernel(
    g_hbm, a_hbm, b_hbm, c_hbm, d1_hbm, d2_hbm, s1_hbm, s2_hbm,
    out_a, own_1, out_b, cross_out, own_2,
    s1, s2, g_raw, g_hi, g_lo, full, p_hi, p_lo, c_full, d1, d2,
    pa, pb, za, sb,
    xa_mid, xa_fin, xb_in, za_in, zb_in,
    rows_1, rows_2, ex_a, ex_b, pt, rr, tile, fin, all_sent,
    load_sem, own_sem,
    sent, ag_recv, sib_recv, cz_recv, cx_recv,
    xa_recv, xb_recv, za_recv, zb_recv,
    exa_recv, exb_recv, rr_send, rr_recv, yz_send, yz_recv,
    fx_recv, fs_recv,
):
    p = lax.axis_index("prow")
    q = lax.axis_index("pcol")
    x, z = p // NZ, lax.rem(p, NZ)
    y, core = q // 2, lax.rem(q, 2)

    def at_x(k):
        return lax.rem(x + k + NX, NX)

    def at_z(k):
        return lax.rem(z + k + NZ, NZ)

    def at_y(k):
        return lax.rem(y + k + NY, NY)

    sibling = (p, y * 2 + 1 - core)

    def remote(src, dst, send, recv, where):
        return pltpu.make_async_remote_copy(
            src_ref=src, dst_ref=dst, send_sem=send, recv_sem=recv,
            device_id=where, device_id_type=MESH,
        )

    barrier = pltpu.get_barrier_semaphore()
    near = [(p, at_y(k) * 2 + core) for k in (1, -1, 2, -2)] + [sibling]
    near += [(x * NZ + at_z(k), q) for k in range(1, NZ)]
    near += [(at_x(k) * NZ + z, q) for k in range(1, NX)]
    for where in near:
        pl.semaphore_signal(barrier, inc=1, device_id=where, device_id_type=MESH)

    def all_of(ref, semaphore):
        pltpu.make_async_copy(ref, ref, semaphore).wait()

    rows16 = pl.ds(pl.multiple_of(q * 16, 16), 16)
    rows8 = pl.ds(pl.multiple_of(p * 8, 8), 8)
    own = [
        pltpu.make_async_copy(a_hbm, full.at[0, :, rows16], own_sem.at[0]),
        pltpu.make_async_copy(b_hbm, full.at[1, :, rows16], own_sem.at[1]),
        pltpu.make_async_copy(c_hbm, c_full.at[rows8], own_sem.at[2]),
    ]
    loads = [
        pltpu.make_async_copy(g_hbm, g_raw, load_sem.at[0]),
        pltpu.make_async_copy(d1_hbm, d1, load_sem.at[1]),
        pltpu.make_async_copy(d2_hbm, d2, load_sem.at[2]),
        pltpu.make_async_copy(s1_hbm, s1, load_sem.at[3]),
        pltpu.make_async_copy(s2_hbm, s2, load_sem.at[4]),
    ]
    for copy in own + loads:
        copy.start()

    pl.semaphore_wait(barrier, len(near))

    def shard(k, row_y):
        rows = row_y * 2 + core
        return full.at[k, :, pl.ds(pl.multiple_of(rows * 16, 16), 16)]

    def ring(k, of, to):
        ref = shard(k, at_y(of))
        return remote(
            ref, ref, sent.at[0], ag_recv.at[k, of - to + 4],
            (p, at_y(to) * 2 + core),
        )

    def push(k, of, to):
        copy = ring(k, of, to)
        copy.start()

    def across(k, of):
        ref = shard(k, at_y(of))
        copy = remote(ref, ref, sent.at[0], sib_recv.at[k], sibling)
        copy.start()

    def got(k, of):
        ring(k, of, 0).wait_recv()
        across(k, of)

    own[0].wait()
    for to in (2, -2, 1, -1):
        push(0, 0, to)
    across(0, 0)
    own[1].wait()
    for to in (2, -2):
        push(1, 0, to)
    own[2].wait()

    def cz_copy(k):
        return remote(
            c_full.at[rows8], c_full.at[rows8], sent.at[0], cz_recv.at[0],
            (x * NZ + at_z(k), q),
        )

    for k in range(1, NZ):
        cz_copy(k).start()

    for index in (0, 3, 4):
        loads[index].wait()

    def split_g(c, carry):
        hi, lo = split(g_raw[pl.ds(c, 512, stride=8), :])
        columns = pl.ds(pl.multiple_of(c * 128, 128), 128)
        g_hi[:, columns] = hi
        g_lo[:, columns] = lo
        return carry

    lax.fori_loop(0, 8, split_g, 0)

    def forward(k, of):
        ring(k, of, 0).wait_recv()
        way = 1 if of < 0 else -1
        push(k, of, way)
        if (of < 0) == (k == 0):
            push(k, of, 2 * way)
        across(k, of)

    forward(0, -2)
    forward(0, 2)
    for to in (1, -1):
        push(1, 0, to)
    across(1, 0)
    got(0, -1)
    got(0, 1)
    all_of(c_full.at[0:56], cz_recv.at[0])
    rows64 = pl.ds(pl.multiple_of(x * 64, 64), 64)

    def cx_copy(k):
        return remote(
            c_full.at[rows64], c_full.at[rows64], sent.at[0], cx_recv.at[0],
            (at_x(k) * NZ + z, q),
        )

    for k in range(1, NX):
        cx_copy(k).start()
    forward(1, -2)
    forward(1, 2)
    got(0, -3)
    got(0, 3)
    got(0, -4)

    def prepare(k, struct):
        all_of(full.at[k, :, 0:128], sib_recv.at[k])
        for r in range(4):
            mask = struct[r * (NX * NZ) + p].astype(F32)
            hi, lo = split(full[k, r] * mask)
            p_hi[k, :, r * 128:(r + 1) * 128] = hi
            p_lo[k, :, r * 128:(r + 1) * 128] = lo

    def col_mask(struct, c):
        return struct[c * (NY * 2) + q].astype(F32)

    prepare(0, s1)

    def mul_a(t, carry):
        columns = pl.ds(pl.multiple_of(t * 256, 256), 256)
        r = dot3((p_hi[0], p_lo[0]), (g_hi[:, columns], g_lo[:, columns]))
        pa[:, :, t, 0] = r[:, :128].reshape(NX, NZ, 8, 128)
        pa[:, :, t, 1] = r[:, 128:].reshape(NX, NZ, 8, 128)
        return carry

    lax.fori_loop(0, 4, mul_a, 0)

    x_right, x_left = (at_x(1) * NZ + z, q), (at_x(-1) * NZ + z, q)

    def xa_piece(d, half):
        return pa.at[d, half * 4:(half + 1) * 4]

    def xa_copy(index, d, half, into, where):
        return remote(xa_piece(d, half), into, sent.at[1], xa_recv.at[min(index, 2)], where)

    xa = {
        "far0": xa_copy(0, at_x(2), 0, xa_mid.at[0], x_right),
        "far1": xa_copy(1, at_x(2), 1, xa_mid.at[1], x_left),
        "near1": xa_copy(2, at_x(1), 1, xa_fin.at[0, 1], x_right),
        "near0": xa_copy(3, at_x(3), 0, xa_fin.at[1, 0], x_left),
        "sum0": xa_copy(4, at_x(1), 0, xa_fin.at[0, 0], x_right),
        "sum1": xa_copy(5, at_x(3), 1, xa_fin.at[1, 1], x_left),
    }
    for name in ("far0", "far1", "near1", "near0"):
        xa[name].start()

    for of in (-1, 1, -3, 3, 4):
        got(1, of)
    all_of(c_full.at[0:192], cx_recv.at[0])
    coupling = c_full[...]
    c_parts = split(coupling)
    ct_parts = split(coupling.T)

    def mul_c(t, carry):
        first = jnp.concatenate(
            [pa[:, :, t, h].reshape(256, 128) * col_mask(s1, 2 * t + h) for h in (0, 1)], axis=1
        )
        r = dot3(ct_parts, split(first))
        pb[:, :, t, 0] = r[:, :128].reshape(NX, NZ, 8, 128)
        pb[:, :, t, 1] = r[:, 128:].reshape(NX, NZ, 8, 128)
        return carry

    lax.fori_loop(0, 4, mul_c, 0)
    prepare(1, s2)

    def mul_b(t, carry):
        columns = pl.ds(pl.multiple_of(t * 256, 256), 256)
        r = dot3((p_hi[1], p_lo[1]), (g_hi[:, columns], g_lo[:, columns]))
        for h in (0, 1):
            block = r[:, h * 128:(h + 1) * 128].reshape(NX, NZ, 8, 128)
            pb[:, :, t, h] = block - pb[:, :, t, h]
        return carry

    lax.fori_loop(0, 4, mul_b, 0)

    def zb_copy(way, j, step):
        away = steps_of(way, j // 2) - step + 1
        d = at_z(away) if way == 0 else at_z(-away)
        to_z = at_z(1) if way == 0 else at_z(-1)
        return d, remote(
            pb.at[j, d], zb_in.at[way, j, step - 1],
            sent.at[1], zb_recv.at[way, j, step - 1],
            (x * NZ + to_z, q),
        )

    def zb_step(step):
        for j in range(4):
            for way in (0, 1):
                if step > steps_of(way, j // 2):
                    continue
                d, copy = zb_copy(way, j, step)
                if step > 1:
                    zb_copy(way, j, step - 1)[1].wait_recv()
                    pb[j, d] += zb_in[way, j, step - 2]
                copy.start()

    zb_step(1)
    xa["far0"].wait_recv()
    pa[at_x(1), 0:4] += xa_mid[0]
    xa["sum0"].start()
    xa["far1"].wait_recv()
    pa[at_x(3), 4:8] += xa_mid[1]
    xa["sum1"].start()
    zb_step(2)
    zb_step(3)
    all_of(xa_fin, xa_recv.at[2])
    for half in (0, 1):
        rows = slice(half * 4, half * 4 + 4)
        za[rows] = pa[x, rows] + xa_fin[0, half] + xa_fin[1, half]

    def xb_copy(k):
        return remote(
            sb.at[at_x(k)], xb_in.at[k], sent.at[1], xb_recv.at[0], (at_x(k) * NZ + z, q)
        )

    def za_copy(way, half, index):
        away, over = ((4, 2), (3, 2), (2, 2), (1, 1))[index]
        sign = 1 - 2 * way
        return remote(
            za.at[at_z(sign * away), half * 2:(half + 1) * 2], za_in.at[way, half, index],
            sent.at[1], za_recv.at[way, half, index], (x * NZ + at_z(sign * over), q),
        )

    sides = [(way, half) for half in (0, 1) for way in (0, 1)]

    def za_start():
        for way, half in sides:
            if steps_of(way, half) == 4:
                za_copy(way, half, 0).start()
            za_copy(way, half, 1).start()
        for way, half in sides:
            if steps_of(way, half) == 3:
                za_copy(way, half, 2).start()

    def za_middle():
        for way, half in sides:
            for index in (0, 1):
                if index == 0 and steps_of(way, half) == 3:
                    continue
                za_copy(way, half, index).wait_recv()
                d = at_z((2 - index) * (1 - 2 * way))
                za[d, half * 2:(half + 1) * 2] += za_in[way, half, index]
                za_copy(way, half, index + 2).start()

    to_col = 2 * z + 1 - lax.rem(x, 2)

    def hand_over(rows, into, parity, recv):
        return remote(
            rows.at[parity], into.at[x // 2], sent.at[1], recv.at[0],
            (q + 16 * parity, to_col),
        )

    za_start()
    zb_step(4)
    za_middle()
    for j in range(4):
        last = [steps_of(way, j // 2) for way in (0, 1)]
        for way in (0, 1):
            zb_copy(way, j, last[way])[1].wait_recv()
        sb[j] = pb[j, z] + zb_in[0, j, last[0] - 1] + zb_in[1, j, last[1] - 1]
    for k in (2, 1, 3):
        xb_copy(k).start()


    def deliver(value, c, struct, out, rows):
        block = value * (-col_mask(struct, c))
        out[c] = block
        rows[c % 2, c // 2] = block

    for half in (0, 1):
        value = za[z, half * 2:(half + 1) * 2]
        for way in (0, 1):
            for index in (2, 3):
                za_copy(way, half, index).wait_recv()
                value = value + za_in[way, half, index]
        for c in range(4 * half, 4 * half + 4):
            deliver(value[c // 2 - 2 * half, c % 2], c, s1, out_a, rows_1)
    for parity in (0, 1):
        hand_over(rows_1, ex_a, parity, exa_recv).start()
    all_of(xb_in.at[1:4], xb_recv.at[0])
    value = sb[x] + xb_in[1] + xb_in[2] + xb_in[3]
    for c in range(8):
        deliver(value[c // 2, c % 2], c, s2, out_b, rows_2)
    for parity in (0, 1):
        hand_over(rows_2, ex_b, parity, exb_recv).start()

    def at_sum(m, j):
        return j * NZ + lax.rem(y + 3 * m, NZ)

    def tile_copy(m, j):
        return remote(
            pt.at[m, j], rr.at[p], rr_send.at[0], rr_recv.at[0], (at_sum(m, j), q)
        )

    def panel_rows(ref):
        return split(jnp.concatenate([ref[:, r].reshape(16, 128) for r in range(4)], axis=1))

    def send_tiles(m, value):
        for s in range(2):
            for h in range(2):
                pt[m, s * 2 + h] = value[s * 8:(s + 1) * 8, h * 128:(h + 1) * 128]
        for j in range(4):
            @pl.when(at_sum(m, j) != p)
            def _():
                tile_copy(m, j).start()

            @pl.when(at_sum(m, j) == p)
            def _():
                pltpu.make_async_copy(pt.at[m, j], rr.at[p], rr_recv.at[0]).start()

    pltpu.make_async_copy(ex_a, ex_a, exa_recv.at[0]).wait()
    rows_a = panel_rows(ex_a)
    send_tiles(0, dot3(rows_a, (p_hi[0], p_lo[0]), NT))
    send_tiles(1, dot3(rows_a, (p_hi[1], p_lo[1]), NT))
    pltpu.make_async_copy(ex_b, ex_b, exb_recv.at[0]).wait()
    rows_b = panel_rows(ex_b)
    send_tiles(2, dot3(rows_b, (p_hi[1], p_lo[1]), NT))

    turn = lax.rem(z - y + NZ, NZ)
    mine = turn // 3

    def make_sums(which):
        @pl.when(which)
        def _():
            pltpu.make_async_copy(rr, rr, rr_recv.at[0]).wait()
            tile[...] = jnp.sum(rr[...], axis=0)
            place = fin.at[core, x, mine, y]
            spot = yz_recv.at[mine]
            pltpu.make_async_copy(tile, place, spot).start()

            far_first = (4, 3, 5, 2, 6, 1, 7, 0)
            columns = [at_y(k) * 2 + core for k in far_first]

            def spread(to_z, targets):
                for column in targets:
                    remote(
                        tile, place, yz_send.at[0], spot, (x * NZ + to_z, column)
                    ).start()

            def plane(k, carry):
                spread(at_z(4 + (k + 1) // 2 * (1 - 2 * lax.rem(k, 2))), columns)
                return carry

            lax.fori_loop(0, NZ - 1, plane, 0)
            spread(z, columns[:-1])

    make_sums(jnp.logical_or(turn == 0, turn == 3))
    make_sums(turn == 6)

    def part(origin, which):
        return fin.at[core, origin, which]

    def fx_copy(which, k):
        return remote(
            part(x, which), part(x, which), sent.at[2], fx_recv.at[which, k],
            (at_x(k) * NZ + z, q),
        )

    def fs_copy(which, k):
        ref = part(at_x(-k), which)
        return remote(ref, ref, sent.at[2], fs_recv.at[which], sibling)

    for which in range(3):
        block = part(x, which)
        pltpu.make_async_copy(block, block, yz_recv.at[which]).wait()
        for k in (2, 1, 3):
            fx_copy(which, k).start()
        fs_copy(which, 0).start()
    for which in range(3):
        for k in (1, 3, 2):
            fx_copy(which, k).wait_recv()
            fs_copy(which, k).start()

    loads[1].wait()
    loads[2].wait()
    for which in (0, 1):
        all_of(fin.at[1 - core, :, which], fs_recv.at[which])

    def places():
        for co in range(2):
            for xo in range(4):
                xs, h = (1 - co) + 2 * (xo // 2), xo % 2
                yield (
                    slice(xs * 64, xs * 64 + 64), slice(h * 128, h * 128 + 128),
                    fin.at[co, xo],
                )

    for rows, columns, ref in places():
        own_1[rows, columns] = d1[rows, columns] - ref[0].reshape(64, 128)
        cross_out[rows, columns] = ref[1].reshape(64, 128)
    cross = -(cross_out[...].T + dot3(ct_parts, split(own_1[...])))
    cross_out[...] = cross
    last = d2[...] - dot3(split(cross), c_parts)
    all_of(fin.at[1 - core, :, 2], fs_recv.at[2])
    for rows, columns, ref in places():
        own_2[rows, columns] = last[rows, columns] - ref[2].reshape(64, 128)

    all_of(all_sent.at[0:302], sent.at[0])
    all_of(all_sent, sent.at[1])
    all_of(all_sent.at[0:168], sent.at[2])

    @pl.when(lax.rem(turn, 3) == 0)
    def _():
        all_of(all_sent.at[0:11], rr_send.at[0])
        all_of(all_sent.at[0:63], yz_send.at[0])

    @pl.when(lax.rem(turn, 3) != 0)
    def _():
        all_of(all_sent.at[0:12], rr_send.at[0])


def body(
    inverse_block,
    panel_first,
    panel_second,
    coupling,
    dinv_first,
    dinv_second,
    struct_first,
    struct_second,
):
    dma = pltpu.SemaphoreType.DMA
    any_space = pl.BlockSpec(memory_space=pl.ANY)
    vmem = pl.BlockSpec(memory_space=pltpu.VMEM)
    square = jax.ShapeDtypeStruct((256, 256), F32)
    rows = jax.ShapeDtypeStruct((8, 8, 128), F32)
    row_a, own_a, row_b, cross, own_b = pl.pallas_call(
        kernel,
        out_shape=(rows, square, rows, square, square),
        in_specs=[any_space] * 8,
        out_specs=(vmem,) * 5,
        scratch_shapes=[
            pltpu.SMEM((128,), jnp.int32),
            pltpu.SMEM((128,), jnp.int32),
            pltpu.VMEM((4096, 128), F32),
            pltpu.VMEM((512, 1024), BF16),
            pltpu.VMEM((512, 1024), BF16),
            pltpu.VMEM((2, 4, 256, 128), F32),
            pltpu.VMEM((2, 256, 512), BF16),
            pltpu.VMEM((2, 256, 512), BF16),
            pltpu.VMEM((256, 256), F32),
            pltpu.VMEM((256, 256), F32),
            pltpu.VMEM((256, 256), F32),
            pltpu.VMEM((4, 8, 4, 2, 8, 128), F32),
            pltpu.VMEM((4, 8, 4, 2, 8, 128), F32),
            pltpu.VMEM((8, 4, 2, 8, 128), F32),
            pltpu.VMEM((4, 4, 2, 8, 128), F32),
            pltpu.VMEM((2, 4, 4, 2, 8, 128), F32),
            pltpu.VMEM((2, 2, 4, 4, 2, 8, 128), F32),
            pltpu.VMEM((4, 4, 2, 8, 128), F32),
            pltpu.VMEM((2, 2, 4, 2, 2, 8, 128), F32),
            pltpu.VMEM((2, 4, 4, 4, 2, 8, 128), F32),
            pltpu.VMEM((2, 4, 8, 128), F32),
            pltpu.VMEM((2, 4, 8, 128), F32),
            pltpu.VMEM((2, 4, 8, 128), F32),
            pltpu.VMEM((2, 4, 8, 128), F32),
            pltpu.VMEM((3, 4, 8, 128), F32),
            pltpu.VMEM((32, 8, 128), F32),
            pltpu.VMEM((8, 128), F32),
            pltpu.VMEM((2, 4, 3, 8, 8, 128), F32),
            pltpu.VMEM((512, 8, 128), F32),
            dma((5,)), dma((3,)),
            dma((3,)), dma((2, 9)), dma((2,)), dma((1,)), dma((1,)),
            dma((3,)), dma((1,)), dma((2, 2, 4)), dma((2, 4, 4)),
            dma((1,)), dma((1,)), dma((1,)), dma((1,)), dma((1,)), dma((3,)),
            dma((3, 4)), dma((3,)),
        ],
        compiler_params=pltpu.CompilerParams(
            collective_id=0, has_side_effects=True, vmem_limit_bytes=60 * 1024 * 1024
        ),
        name="selected_inversion",
    )(
        inverse_block.reshape(4096, 128),
        panel_first.reshape(4, 16, 128),
        panel_second.reshape(4, 16, 128),
        coupling, dinv_first, dinv_second, struct_first, struct_second,
    )
    return (
        row_a.reshape(8, 1, 8, 128), own_a, row_b.reshape(8, 1, 8, 128), cross, own_b,
    )


def solution(mesh):
    return jax.shard_map(
        body,
        mesh=mesh,
        in_specs=(
            P(None, "prow", None, None, "pcol", None),
            P(None, "prow", "pcol", None),
            P(None, "prow", "pcol", None),
            P("prow", None),
            P(),
            P(),
            P(),
            P(),
        ),
        out_specs=(P(None, "pcol", "prow", None), P(), P(None, "pcol", "prow", None), P(), P()),
        check_vma=False,
    )
```
